128 devices in a mesh: pipe: 8 (over z_lo, x), tensor: 4 (over z_hi, core), dp: 4 (over y).
Axes of the slice: x: 4, y: 4, z: 4 (z_hi: 2, z_lo: 2; z = z_hi * 2 + z_lo), core: 2. Of those that a mesh axis runs over, the one named last changes fastest.
Arguments:
- encoded: bfloat16 [4, 1024, 4096], P('dp', 'pipe'), may hold values from -6 to 6
- kv_weight: bfloat16 [8, 2, 4096, 2048], P('pipe', None, None, 'tensor'), may hold values from -0.09375 to 0.09375
- queries: bfloat16 [4, 8, 512, 2048], P('dp', 'pipe', None, 'tensor'), may hold values from -70 to 70
- cotangent: bfloat16 [4, 8, 512, 2048], P('dp', 'pipe', None, 'tensor'), may hold values from -6 to 6
Outputs:
- attended: bfloat16 [4, 8, 512, 2048], P('dp', 'pipe', None, 'tensor')
- query_grad: bfloat16 [4, 8, 512, 2048], P('dp', 'pipe', None, 'tensor')
- encoded_grad: bfloat16 [4, 1024, 4096], P('dp', 'pipe')
- weight_grad: bfloat16 [8, 2, 4096, 2048], P('pipe', None, 'dp', 'tensor')
The draws below stay inside these ranges and needn't reach their ends.
All inputs are finite; a program needn't handle non-finite values.
Results may differ from the reference program's by a relative error of at most 0.03.
The reference program's roundings to bfloat16 on the way count: a program that leaves them out, or rounds other values in their place, can miss the bound.
Values may be sent and summed in bfloat16 or wider, within the bound.
No kernel may reach another device: no remote copies, remote signals or barrier semaphores. Data moves between devices by JAX's collectives and lax.ppermute only.
A program may use at most 128 MiB of HBM per device.

```python
import jax
import jax.numpy as jnp
from jax import lax

D = 4096
HEADS = 8
HEAD_DIM = 256
TGT = 512
INNER = 2048
ENC_LEN = 1024
LAYERS = 8
BATCH = 4


def draw_queries(key, part):
    key = jax.random.fold_in(key, 11)
    shape = (BATCH, LAYERS, TGT, HEADS * HEAD_DIM)
    return jnp.clip(jax.random.normal(key, shape, jnp.float32), -6.0, 6.0).astype(jnp.bfloat16)


def block_levels(rng, shape, shards, low, high):
    def one(position, blocks):
        steps = jax.random.uniform(jax.random.fold_in(jax.random.fold_in(rng, 6), position), (blocks,), jnp.float32, low / len(shards), high / len(shards))
        return jnp.repeat(jnp.exp(steps), shape[position] // blocks).reshape((-1,) + (1,) * (len(shape) - position - 1))

    factor_of = one(*shards[0])
    for cut in shards[1:]:
        factor_of = factor_of * one(*cut)
    return factor_of


def gaussian(key, shape, scale, limit, shards=(), dtype=jnp.bfloat16):
    drawn = jax.random.normal(key, shape, jnp.float32) * scale
    if len(shards) > 0:
        drawn = block_levels(key, shape, shards, -0.22, 0.18) * drawn
    return jnp.clip(drawn, min=-limit, max=limit).astype(dtype)


def setup_inputs(seed: int = 0) -> dict:
    seeds = jax.random.split(jax.random.key(seed), 5)
    return {
        "encoded": gaussian(seeds[0], (BATCH, ENC_LEN, D), 1.0, 6.0, ((0, 4), (1, 8))),
        "kv_weight": gaussian(seeds[1], (LAYERS, 2, D, INNER), D ** -0.5, 0.09375, ((0, 8), (3, 4))),
        "queries": draw_queries(jax.random.fold_in(seeds[4], 71), 0),
        "cotangent": gaussian(seeds[3], (BATCH, LAYERS, TGT, INNER), 1.0, 6.0, ((0, 4), (1, 8), (3, 4))),
    }


def attend(q, keys, values, dout):
    heads = q.shape[1] // HEAD_DIM
    scale = HEAD_DIM ** -0.5
    q_heads = q.astype(jnp.float32).reshape(q.shape[0], heads, HEAD_DIM)
    k_heads = keys.astype(jnp.float32).reshape(keys.shape[0], heads, HEAD_DIM)
    v_heads = values.astype(jnp.float32).reshape(values.shape[0], heads, HEAD_DIM)
    g_heads = dout.astype(jnp.float32).reshape(dout.shape[0], heads, HEAD_DIM)
    scores = jnp.einsum("qhd,khd->hqk", q_heads, k_heads) * scale
    top = jnp.max(scores, axis=-1, keepdims=True)
    expd = jnp.exp(scores - top)
    probs = expd / jnp.sum(expd, axis=-1, keepdims=True)
    probs_low = lax.optimization_barrier(probs.astype(jnp.bfloat16)).astype(jnp.float32)
    attended = jnp.einsum("hqk,khd->qhd", probs_low, v_heads).reshape(q.shape).astype(jnp.bfloat16)
    dprobs = jnp.einsum("qhd,khd->hqk", g_heads, v_heads)
    att_heads = attended.astype(jnp.float32).reshape(q.shape[0], heads, HEAD_DIM)
    delta = jnp.einsum("qhd,qhd->hq", g_heads, att_heads)
    dscores = probs * (dprobs - delta[:, :, None])
    ds_low = lax.optimization_barrier(dscores.astype(jnp.bfloat16)).astype(jnp.float32)
    query_grad = (scale * jnp.einsum("hqk,khd->qhd", ds_low, k_heads)).reshape(q.shape).astype(jnp.bfloat16)
    key_grad = (scale * jnp.einsum("hqk,qhd->khd", ds_low, q_heads)).reshape(keys.shape).astype(jnp.bfloat16)
    value_grad = jnp.einsum("hqk,qhd->khd", probs_low, g_heads).reshape(values.shape).astype(jnp.bfloat16)
    return attended, query_grad, key_grad, value_grad


def back_project(key_grad, value_grad, w_key, w_value):
    dims = (((1,), (1,)), ((), ()))
    first = lax.dot_general(key_grad, w_key, dims, preferred_element_type=jnp.float32)
    return first + lax.dot_general(value_grad, w_value, dims, preferred_element_type=jnp.float32)


def reference(encoded, kv_weight, queries, cotangent):
    dims = (((0,), (0,)), ((), ()))

    def per_layer(total, inputs):
        weights, q_layer, g_layer = inputs
        w_key = weights[0]
        w_value = weights[1]
        grad_w = jnp.zeros(weights.shape, jnp.float32)
        att_list = []
        dq_list = []
        for seq in range(BATCH):
            enc = encoded[seq]
            keys = jnp.dot(enc, w_key, preferred_element_type=jnp.float32).astype(jnp.bfloat16)
            values = jnp.dot(enc, w_value, preferred_element_type=jnp.float32).astype(jnp.bfloat16)
            attended, query_grad, key_grad, value_grad = attend(q_layer[seq], keys, values, g_layer[seq])
            att_list.append(attended)
            dq_list.append(query_grad)
            grad_k = lax.dot_general(enc, key_grad, dims, preferred_element_type=jnp.float32)
            grad_v = lax.dot_general(enc, value_grad, dims, preferred_element_type=jnp.float32)
            grad_w = grad_w + jnp.stack([grad_k, grad_v], 0)
            total = total.at[seq].add(back_project(key_grad, value_grad, w_key, w_value))
        return total, (jnp.stack(att_list, 0), jnp.stack(dq_list, 0), grad_w.astype(jnp.bfloat16))

    start_total = jnp.zeros((BATCH, ENC_LEN, D), jnp.float32)
    inputs = (kv_weight, jnp.transpose(queries, (1, 0, 2, 3)), jnp.transpose(cotangent, (1, 0, 2, 3)))
    total, (att_all, dq_all, grad_all) = lax.scan(per_layer, start_total, inputs)
    return (jnp.transpose(att_all, (1, 0, 2, 3)), jnp.transpose(dq_all, (1, 0, 2, 3)),
            total.astype(jnp.bfloat16), grad_all)
```

```python
import jax
import jax.numpy as jnp
from jax import lax
from jax.sharding import PartitionSpec as P

HEAD_DIM = 256
ALL = ("pipe", "tensor", "dp")


def attend(q, keys, values, dout):
    heads = q.shape[1] // HEAD_DIM
    scale = HEAD_DIM ** (-0.5)
    q_heads = q.astype(jnp.float32).reshape(q.shape[0], heads, HEAD_DIM)
    k_heads = keys.astype(jnp.float32).reshape(keys.shape[0], heads, HEAD_DIM)
    v_heads = values.astype(jnp.float32).reshape(values.shape[0], heads, HEAD_DIM)
    g_heads = dout.astype(jnp.float32).reshape(dout.shape[0], heads, HEAD_DIM)
    scores = jnp.einsum("qhd,khd->hqk", q_heads, k_heads) * scale
    top = jnp.max(scores, axis=-1, keepdims=True)
    expd = jnp.exp(scores - top)
    probs = expd / jnp.sum(expd, axis=-1, keepdims=True)
    probs_low = lax.optimization_barrier(probs.astype(jnp.bfloat16)).astype(jnp.float32)
    attended = jnp.einsum("hqk,khd->qhd", probs_low, v_heads).reshape(q.shape).astype(jnp.bfloat16)
    dprobs = jnp.einsum("qhd,khd->hqk", g_heads, v_heads)
    att_heads = attended.astype(jnp.float32).reshape(q.shape[0], heads, HEAD_DIM)
    delta = jnp.einsum("qhd,qhd->hq", g_heads, att_heads)
    dscores = probs * (dprobs - delta[:, :, None])
    ds_low = lax.optimization_barrier(dscores.astype(jnp.bfloat16)).astype(jnp.float32)
    query_grad = (
        (scale * jnp.einsum("hqk,khd->qhd", ds_low, k_heads)).reshape(q.shape).astype(jnp.bfloat16)
    )
    key_grad = (
        (scale * jnp.einsum("hqk,qhd->khd", ds_low, q_heads))
        .reshape(keys.shape)
        .astype(jnp.bfloat16)
    )
    value_grad = (
        jnp.einsum("hqk,qhd->khd", probs_low, g_heads).reshape(values.shape).astype(jnp.bfloat16)
    )
    return (attended, query_grad, key_grad, value_grad)


def pairs(move):
    def index(x, y, z, core):
        pipe = (z % 2) * 4 + x
        tensor = (z // 2) * 2 + core
        return (pipe * 4 + tensor) * 4 + y

    found = []
    for x in range(4):
        for y in range(4):
            for z in range(4):
                for core in range(2):
                    sign = 1 - 2 * core
                    to_x, to_y, to_z, to_core = move(x, y, z, core, sign)
                    found.append((index(x, y, z, core), index(to_x % 4, to_y % 4, to_z % 4, to_core)))
    return found


ALONG_X = pairs(lambda x, y, z, core, sign: (x + sign, y, z, core))
ALONG_Y = pairs(lambda x, y, z, core, sign: (x, y + sign, z, core))
ALONG_Z = pairs(lambda x, y, z, core, sign: (x, y, z + sign, core))
BACK_Z = pairs(lambda x, y, z, core, sign: (x, y, z - sign, core))
ACROSS_Z = pairs(lambda x, y, z, core, sign: (x, y, z + 2, core))
SWAP = pairs(lambda x, y, z, core, sign: (x, y, z, 1 - core))


def send(array, route):
    return lax.ppermute(array, ALL, route)


def on_device(encoded, kv_weight, queries, cotangent):
    f32, bf16 = jnp.float32, jnp.bfloat16
    w_key = kv_weight[0, 0]
    w_value = kv_weight[0, 1]
    q_rows = queries[0, 0]
    g_rows = cotangent[0, 0]
    core = lax.axis_index("tensor") % 2
    sign = 1 - 2 * core
    y = lax.axis_index("dp")
    block = encoded[0]
    half = block.shape[0] // 2

    mine = [lax.dynamic_slice_in_dim(block, core * half, half, 0)]
    theirs = [lax.dynamic_slice_in_dim(block, (1 - core) * half, half, 0)]
    for _ in range(3):
        mine.append(send(mine[-1], ALONG_X))
    beside = [send(piece, ALONG_Z) for piece in mine]
    theirs += [send(piece, SWAP) for piece in mine[1:]]
    theirs += [send(piece, SWAP) for piece in beside]
    mine += beside
    whole = jnp.concatenate(mine + theirs, 0)
    rows = whole.shape[0] // 2

    keys = jnp.dot(whole, w_key, preferred_element_type=f32).astype(bf16)
    values = jnp.dot(whole, w_value, preferred_element_type=f32).astype(bf16)
    attended, query_grad, key_grad, value_grad = attend(q_rows, keys, values, g_rows)

    tdims = (((0,), (0,)), ((), ()))
    width = whole.shape[1] // 4

    def weight_part(step, grad):
        start = (y - sign * step) % 4 * width
        part = lax.dynamic_slice_in_dim(whole, start, width, 1)
        return lax.dot_general(part, grad, tdims, preferred_element_type=f32)

    sums = {"value": weight_part(1, value_grad), "key": weight_part(1, key_grad)}
    for step in (2, 3, 0):
        for name, grad in (("value", value_grad), ("key", key_grad)):
            moved = send(sums[name].astype(bf16), ALONG_Y)
            sums[name] = weight_part(step, grad) + moved.astype(f32)
    grad_share = jnp.stack([sums["key"], sums["value"]], 0).astype(bf16)

    cdims = (((1,), (1,)), ((), ()))

    def encoder_part(low, high):
        first = lax.dot_general(key_grad[low:high], w_key, cdims, preferred_element_type=f32)
        return first + lax.dot_general(
            value_grad[low:high], w_value, cdims, preferred_element_type=f32
        )

    moved = send(encoder_part(rows, 2 * rows).astype(bf16), SWAP)
    total = (encoder_part(0, rows) + moved.astype(f32)).reshape(2, 4, half, -1)
    acc = total[:, 1]
    for step in (2, 3, 0):
        acc = total[:, step] + send(acc.astype(bf16), ALONG_X).astype(f32)
    here = acc[0] + send(acc[1].astype(bf16), BACK_Z).astype(f32)
    here = here.astype(bf16)
    final = (here.astype(f32) + send(here, ACROSS_Z).astype(f32)).astype(bf16)
    other = send(final, SWAP)
    enc_grad = jnp.where(
        core == 0, jnp.concatenate([final, other], 0), jnp.concatenate([other, final], 0)
    )
    return (attended[None, None], query_grad[None, None], enc_grad[None], grad_share[None])


def solution(mesh):
    return jax.shard_map(
        on_device,
        mesh=mesh,
        in_specs=(
            P("dp", "pipe", None),
            P("pipe", None, None, "tensor"),
            P("dp", "pipe", None, "tensor"),
            P("dp", "pipe", None, "tensor"),
        ),
        out_specs=(
            P("dp", "pipe", None, "tensor"),
            P("dp", "pipe", None, "tensor"),
            P("dp", "pipe", None),
            P("pipe", None, "dp", "tensor"),
        ),
        check_vma=False,
    )
```

```python
import functools

import jax
import jax.numpy as jnp
from jax import lax
from jax.experimental import pallas as pl
from jax.experimental.pallas import tpu as pltpu
from jax.sharding import PartitionSpec as P

HEAD_DIM = 256
ALL = ("pipe", "tensor", "dp")
F32, BF16 = jnp.float32, jnp.bfloat16
NT = (((1,), (1,)), ((), ()))
TN = (((0,), (0,)), ((), ()))
VMEM_BYTES = 48 * 1024 * 1024


def params():
    return pltpu.CompilerParams(vmem_limit_bytes=VMEM_BYTES)


def cost(flops, nbytes):
    return pl.CostEstimate(flops=flops, bytes_accessed=nbytes, transcendentals=0)


def pairs(move):
    def index(x, y, z, core):
        pipe = (z % 2) * 4 + x
        tensor = (z // 2) * 2 + core
        return (pipe * 4 + tensor) * 4 + y

    found = []
    for x in range(4):
        for y in range(4):
            for z in range(4):
                for core in range(2):
                    to_x, to_y, to_z, to_core = move(x, y, z, core)
                    found.append((index(x, y, z, core), index(to_x, to_y, to_z % 4, to_core)))
    return found


def partner(place, core, which):
    return place ^ 1 if core == which else 3 - place


X_FIRST = pairs(lambda x, y, z, core: (partner(x, core, 0), y, z, core))
X_SECOND = pairs(lambda x, y, z, core: (partner(x, core, 1), y, z, core))
Y_FIRST = pairs(lambda x, y, z, core: (x, partner(y, core, 0), z, core))
Y_SECOND = pairs(lambda x, y, z, core: (x, partner(y, core, 1), z, core))
ALONG_Z = pairs(lambda x, y, z, core: (x, y, z + 1 - 2 * core, core))
BACK_Z = pairs(lambda x, y, z, core: (x, y, z - 1 + 2 * core, core))
ACROSS_Z = pairs(lambda x, y, z, core: (x, y, z + 2, core))
SWAP = pairs(lambda x, y, z, core: (x, y, z, 1 - core))


def send(array, route):
    return lax.ppermute(array, ALL, route)


def project_body(a, b, c, d, w, keys, values, acc):
    x = jnp.concatenate([a[...], b[...], c[...], d[...]], 0)
    step = pl.program_id(0)
    width = keys.shape[1]
    for part in range(2):
        cols = slice(part * width, (part + 1) * width)
        dot = jnp.dot(x, w[0, part], preferred_element_type=F32)

        @pl.when(step == 0)
        def _():
            acc[:, cols] = dot

        @pl.when(step > 0)
        def _():
            acc[:, cols] += dot

    @pl.when(step == pl.num_programs(0) - 1)
    def _():
        keys[...] = acc[:, :width].astype(BF16)
        values[...] = acc[:, width:].astype(BF16)


def project(pieces, kv_weight):
    _, _, depth, width = kv_weight.shape
    rows = 4 * pieces[0].shape[0]
    tile = depth // 4
    shape = jax.ShapeDtypeStruct((rows, width), BF16)
    return pl.pallas_call(
        project_body,
        grid=(4,),
        in_specs=[pl.BlockSpec((rows // 4, tile), lambda i: (0, i))] * 4
        + [pl.BlockSpec((1, 2, tile, width), lambda i: (0, 0, i, 0))],
        out_specs=[pl.BlockSpec((rows, width), lambda i: (0, 0))] * 2,
        out_shape=[shape, shape],
        scratch_shapes=[pltpu.VMEM((rows, 2 * width), F32)],
        compiler_params=params(),
        cost_estimate=cost(4 * rows * depth * width, 4 * depth * width + 2 * rows * depth),
    )(*pieces, kv_weight)


def arrange(groups):
    quarter = groups[0].shape[0] // 4

    def at(group, place):
        return groups[group][place * quarter : (place + 1) * quarter, :]

    order = [(0, 0), (1, 0), (1, 2), (3, 0), (0, 2), (2, 0), (2, 2), (3, 2)]
    return jnp.concatenate(
        [at(g, p) for g, p in order] + [at(g, p + 1) for g, p in order], 0
    )


def attend_body(q, g, k0, k1, k2, k3, v0, v1, v2, v3, att, dq, kg, vg, kgt, vgt, low, dlow):
    scale = HEAD_DIM ** (-0.5)
    k = arrange([k0, k1, k2, k3])
    v = arrange([v0, v1, v2, v3])
    total = q.shape[2]
    chunk = total // 2
    for part in range(2):
        rows = slice(part * chunk, (part + 1) * chunk)
        g_rows = g[0, 0, rows, :]
        scores = lax.dot_general(q[0, 0, rows, :], k, NT, preferred_element_type=F32) * scale
        expd = jnp.exp(scores - jnp.max(scores, axis=-1, keepdims=True))
        probs = expd * (1.0 / jnp.sum(expd, axis=-1, keepdims=True))
        probs_low = probs.astype(BF16)
        low[rows, :] = probs_low
        out = jnp.dot(probs_low, v, preferred_element_type=F32).astype(BF16)
        att[0, 0, rows, :] = out
        dprobs = lax.dot_general(g_rows, v, NT, preferred_element_type=F32)
        delta = jnp.sum(g_rows.astype(F32) * out.astype(F32), axis=-1, keepdims=True)
        ds_low = (probs * (dprobs - delta)).astype(BF16)
        dlow[rows, :] = ds_low
        dq[0, 0, rows, :] = (
            scale * jnp.dot(ds_low, k, preferred_element_type=F32)
        ).astype(BF16)
    value_t = lax.dot_general(g[0, 0], low[...], TN, preferred_element_type=F32)
    vgt[...] = value_t.astype(BF16)
    vg[...] = value_t.T.astype(BF16)
    key_t = scale * lax.dot_general(q[0, 0], dlow[...], TN, preferred_element_type=F32)
    kgt[...] = key_t.astype(BF16)
    kg[...] = key_t.T.astype(BF16)


def attend(queries, cotangent, keys, values):
    _, _, total, width = queries.shape
    rows = keys[0].shape[0]
    span = 4 * rows
    head = pl.BlockSpec((1, 1, total, HEAD_DIM), lambda h: (0, 0, 0, h))
    group = pl.BlockSpec((rows, HEAD_DIM), lambda h: (0, h))
    tall = pl.BlockSpec((span, HEAD_DIM), lambda h: (0, h))
    flat = pl.BlockSpec((HEAD_DIM, span), lambda h: (h, 0))
    same = jax.ShapeDtypeStruct(queries.shape, BF16)
    tall_shape = jax.ShapeDtypeStruct((span, width), BF16)
    flat_shape = jax.ShapeDtypeStruct((width, span), BF16)
    return pl.pallas_call(
        attend_body,
        grid=(width // HEAD_DIM,),
        in_specs=[head, head] + [group] * 8,
        out_specs=[head, head, tall, tall, flat, flat],
        out_shape=[same, same, tall_shape, tall_shape, flat_shape, flat_shape],
        scratch_shapes=[pltpu.VMEM((total, span), BF16)] * 2,
        compiler_params=params(),
        cost_estimate=cost(12 * total * span * width, 16 * span * width),
    )(queries, cotangent, *keys, *values)


def weight_body(count, final, index, grad_t, *refs):
    pieces, refs = refs[:count], refs[count:]
    moved, out = refs[:-1], refs[-1]
    if final:
        moved = [ref for ref in moved if ref.ndim == 2]
    rows = jnp.concatenate([piece[...] for piece in pieces], 0)
    total = jnp.dot(grad_t[...], rows, preferred_element_type=F32)
    for ref in moved:
        total = total + ref[...].astype(F32)
    if final:
        out[0, 0] = total.T.astype(BF16)
    else:
        out[...] = total.astype(BF16)


TILE = 512


def weight_part(index, grad_t, pieces, moved=(), offsets=(), final=None, into=None):
    width, span = grad_t.shape
    steps = index.shape[0]
    depth = pieces[0].shape[1]
    specs = [pl.BlockSpec((width, span), lambda i, index: (0, 0))]
    specs += [pl.BlockSpec((p.shape[0], TILE), lambda i, index: (0, index[i])) for p in pieces]
    for offset in offsets:
        specs.append(
            pl.BlockSpec((width, TILE), functools.partial(lambda o, i, index: (0, o + i), offset))
        )
    operands = [index, grad_t, *pieces, *moved]
    aliases = {}
    if final is None:
        out_spec = pl.BlockSpec((width, TILE), lambda i, index: (0, i))
        out_shape = jax.ShapeDtypeStruct((width, steps * TILE), BF16)
    else:
        out_spec = pl.BlockSpec((1, 1, TILE, width), lambda i, index: (0, final, i, 0))
        out_shape = jax.ShapeDtypeStruct((1, 2, depth // 4, width), BF16)
        if into is not None:
            specs.append(pl.BlockSpec(memory_space=pl.ANY))
            aliases = {len(operands): 0}
            operands.append(into)
    return pl.pallas_call(
        functools.partial(weight_body, len(pieces), final is not None),
        grid_spec=pltpu.PrefetchScalarGridSpec(
            num_scalar_prefetch=1, grid=(steps,), in_specs=specs, out_specs=out_spec
        ),
        out_shape=out_shape,
        input_output_aliases=aliases,
        compiler_params=params(),
        cost_estimate=cost(2 * width * span * TILE * steps, 4 * span * TILE * steps),
    )(*operands)


def encoder_body(kg, vg, w, *refs):
    total = lax.dot_general(kg[...], w[0, 0], NT, preferred_element_type=F32)
    total = total + lax.dot_general(vg[...], w[0, 1], NT, preferred_element_type=F32)
    if len(refs) > 1:
        total = total + refs[0][...].astype(F32)
    refs[-1][...] = total.astype(BF16)


def encoder_part(key_grad, value_grad, kv_weight, block, moved=None):
    span, width = key_grad.shape
    depth = kv_weight.shape[2]
    rows = span // 4
    grad = pl.BlockSpec((rows, width), lambda i: (block, 0))
    tile = pl.BlockSpec((rows, TILE), lambda i: (0, i))
    extra = [] if moved is None else [moved]
    return pl.pallas_call(
        encoder_body,
        grid=(depth // TILE,),
        in_specs=[grad, grad, pl.BlockSpec((1, 2, TILE, width), lambda i: (0, 0, i, 0))]
        + [tile] * len(extra),
        out_specs=tile,
        out_shape=jax.ShapeDtypeStruct((rows, depth), BF16),
        compiler_params=params(),
        cost_estimate=cost(4 * rows * depth * width, 4 * depth * width + 4 * rows * depth),
    )(key_grad, value_grad, kv_weight, *extra)


def tie(array, *others):
    return lax.optimization_barrier((array, *others))[0]


def on_device(encoded, kv_weight, queries, cotangent):
    core = lax.axis_index("tensor") % 2
    y = lax.axis_index("dp")
    block = encoded[0]
    half = block.shape[0] // 2

    h = {"o": lax.dynamic_slice_in_dim(block, core * half, half, 0)}
    h_too = {"o": lax.dynamic_slice_in_dim(block, (1 - core) * half, half, 0)}
    g, g_too = {}, {}
    h["a"] = send(h["o"], X_FIRST)
    g["o"] = send(h["o"], ALONG_Z)
    h["b"] = send(tie(h["o"], h["a"]), X_SECOND)
    g["a"] = send(h["a"], ALONG_Z)
    h["d"] = send(h["a"], X_SECOND)
    g["b"] = send(h["b"], ALONG_Z)
    g["d"] = send(h["d"], ALONG_Z)
    for name in "abd":
        h_too[name] = send(h[name], SWAP)
    for name in "oabd":
        g_too[name] = send(g[name], SWAP)
    groups = [
        (h["o"], h_too["o"], h["a"], h_too["a"]),
        (g["o"], g_too["o"], h["b"], h_too["b"]),
        (g["a"], g_too["a"], h["d"], h_too["d"]),
        (g["b"], g_too["b"], g["d"], g_too["d"]),
    ]
    keys, values = zip(*[project(group, kv_weight) for group in groups])
    order = ["ho", "go", "hb", "gb", "ha", "ga", "hd", "gd"]
    pieces = [{"h": h, "g": g}[name[0]][name[1]] for name in order]
    pieces += [{"h": h_too, "g": g_too}[name[0]][name[1]] for name in order]

    attended, query_grad, key_grad, value_grad, key_grad_t, value_grad_t = attend(
        queries, cotangent, keys, values
    )

    one, other = y ^ 1, 3 - y
    first = jnp.where(core == 0, one, other)
    second = jnp.where(core == 0, other, one)
    across = (y + 2) % 4

    def tiles(*slices):
        return jnp.stack([2 * s + i for s in slices for i in range(2)]).astype(jnp.int32)

    value_out = weight_part(tiles(first, across), value_grad_t, pieces)
    value_in = send(value_out, Y_FIRST)

    key_grad, value_grad = lax.optimization_barrier((key_grad, value_grad, value_out))[:2]
    grads = (key_grad, value_grad, kv_weight)
    moved_send = send(encoder_part(*grads, 3), SWAP)
    moved_keep = send(encoder_part(*grads, 2), SWAP)
    x_out = encoder_part(*grads, 1, moved_send)
    x_in = send(x_out, X_FIRST)
    keep = encoder_part(*grads, 0, moved_keep)

    key_out = weight_part(tiles(first, across), tie(key_grad_t, x_out), pieces)
    key_in = send(key_out, Y_FIRST)

    total = keep.astype(F32) + x_in.astype(F32)
    x_in = send(total[2 * half :].astype(BF16), X_SECOND)
    total = total[: 2 * half] + x_in.astype(F32)
    here = total[:half] + send(total[half:].astype(BF16), BACK_Z).astype(F32)
    here = here.astype(BF16)
    last = (here.astype(F32) + send(here, ACROSS_Z).astype(F32)).astype(BF16)
    last_too = send(last, SWAP)
    enc_grad = jnp.where(
        core == 0, jnp.concatenate([last, last_too], 0), jnp.concatenate([last_too, last], 0)
    )

    value_two = send(
        weight_part(tiles(second), value_grad_t, pieces, [value_in], [2]), Y_SECOND
    )
    key_two = send(weight_part(tiles(second), key_grad_t, pieces, [key_in], [2]), Y_SECOND)
    share = weight_part(tiles(y), value_grad_t, pieces, [value_in, value_two], [0, 0], 1)
    share = weight_part(tiles(y), key_grad_t, pieces, [key_in, key_two], [0, 0], 0, share)
    return (attended, query_grad, enc_grad[None], share)


def solution(mesh):
    return jax.shard_map(
        on_device,
        mesh=mesh,
        in_specs=(
            P("dp", "pipe", None),
            P("pipe", None, None, "tensor"),
            P("dp", "pipe", None, "tensor"),
            P("dp", "pipe", None, "tensor"),
        ),
        out_specs=(
            P("dp", "pipe", None, "tensor"),
            P("dp", "pipe", None, "tensor"),
            P("dp", "pipe", None),
            P("pipe", None, "dp", "tensor"),
        ),
        check_vma=False,
    )
```

```python
import functools

import jax
import jax.numpy as jnp
from jax import lax
from jax.experimental import pallas as pl
from jax.experimental.pallas import tpu as pltpu
from jax.sharding import PartitionSpec as P

HEAD_DIM = 256
ALL = ("pipe", "tensor", "dp")
F32, BF16 = jnp.float32, jnp.bfloat16
NT = (((1,), (1,)), ((), ()))
TN = (((0,), (0,)), ((), ()))
TILE = 512
WHOLE = pl.BlockSpec(memory_space=pltpu.VMEM)
SCALARS = pl.BlockSpec(memory_space=pltpu.SMEM)


def call(body, operands, shapes, scratch=(), index=0):
    many = isinstance(shapes, (list, tuple))
    return pl.pallas_call(
        body,
        in_specs=[SCALARS] * index + [WHOLE] * (len(operands) - index),
        out_specs=[WHOLE] * len(shapes) if many else WHOLE,
        out_shape=shapes,
        scratch_shapes=scratch,
        compiler_params=pltpu.CompilerParams(vmem_limit_bytes=20 * 1024 * 1024),
        cost_estimate=pl.CostEstimate(flops=1000, bytes_accessed=1000, transcendentals=0),
    )(*operands)


def bf16(*shape):
    return jax.ShapeDtypeStruct(shape, BF16)


def pairs(move):
    def index(x, y, z, core):
        pipe = (z % 2) * 4 + x
        tensor = (z // 2) * 2 + core
        return (pipe * 4 + tensor) * 4 + y

    found = []
    for x in range(4):
        for y in range(4):
            for z in range(4):
                for core in range(2):
                    to_x, to_y, to_z, to_core = move(x, y, z, core)
                    found.append((index(x, y, z, core), index(to_x, to_y, to_z % 4, to_core)))
    return found


def partner(place, core, which):
    return place ^ 1 if core == which else 3 - place


X_FIRST = pairs(lambda x, y, z, core: (partner(x, core, 0), y, z, core))
X_SECOND = pairs(lambda x, y, z, core: (partner(x, core, 1), y, z, core))
Y_FIRST = pairs(lambda x, y, z, core: (x, partner(y, core, 0), z, core))
Y_SECOND = pairs(lambda x, y, z, core: (x, partner(y, core, 1), z, core))
ALONG_Z = pairs(lambda x, y, z, core: (x, y, z + 1 - 2 * core, core))
BACK_Z = pairs(lambda x, y, z, core: (x, y, z - 1 + 2 * core, core))
ACROSS_Z = pairs(lambda x, y, z, core: (x, y, z + 2, core))
SWAP = pairs(lambda x, y, z, core: (x, y, z, 1 - core))


def send(array, route):
    return lax.ppermute(array, ALL, route)


def project_body(a, b, c, d, w, keys, values):
    x = jnp.concatenate([a[...], b[...], c[...], d[...]], 0)
    keys[...] = jnp.dot(x, w[0, 0], preferred_element_type=F32).astype(BF16)
    values[...] = jnp.dot(x, w[0, 1], preferred_element_type=F32).astype(BF16)


def project(pieces, kv_weight):
    shape = bf16(4 * pieces[0].shape[0], kv_weight.shape[3])
    return call(project_body, [*pieces, kv_weight], [shape, shape])


def arrange(groups):
    quarter = groups[0].shape[0] // 4

    def at(group, place):
        return groups[group][place * quarter : (place + 1) * quarter, :]

    order = [(0, 0), (1, 0), (1, 2), (3, 0), (0, 2), (2, 0), (2, 2), (3, 2)]
    return jnp.concatenate(
        [at(g, p) for g, p in order] + [at(g, p + 1) for g, p in order], 0
    )


def attend_body(q, g, k0, k1, k2, k3, v0, v1, v2, v3, att, dq, kg, vg, kgt, vgt, low, dlow):
    scale = HEAD_DIM ** (-0.5)
    total = q.shape[2]
    chunk = total // 2
    for head in range(q.shape[3] // HEAD_DIM):
        cols = slice(head * HEAD_DIM, (head + 1) * HEAD_DIM)
        k = arrange([ref[:, cols] for ref in (k0, k1, k2, k3)])
        v = arrange([ref[:, cols] for ref in (v0, v1, v2, v3)])
        for part in range(2):
            rows = slice(part * chunk, (part + 1) * chunk)
            g_rows = g[0, 0, rows, cols]
            scores = scale * lax.dot_general(
                q[0, 0, rows, cols], k, NT, preferred_element_type=F32
            )
            expd = jnp.exp(scores - jnp.max(scores, axis=-1, keepdims=True))
            probs = expd * (1.0 / jnp.sum(expd, axis=-1, keepdims=True))
            probs_low = probs.astype(BF16)
            low[head, rows, :] = probs_low
            out = jnp.dot(probs_low, v, preferred_element_type=F32).astype(BF16)
            att[0, 0, rows, cols] = out
            dprobs = lax.dot_general(g_rows, v, NT, preferred_element_type=F32)
            delta = jnp.sum(g_rows.astype(F32) * out.astype(F32), axis=-1, keepdims=True)
            ds_low = (probs * (dprobs - delta)).astype(BF16)
            dlow[head, rows, :] = ds_low
            dq[0, 0, rows, cols] = (
                scale * jnp.dot(ds_low, k, preferred_element_type=F32)
            ).astype(BF16)
        value_t = lax.dot_general(g[0, 0, :, cols], low[head], TN, preferred_element_type=F32)
        vgt[cols, :] = value_t.astype(BF16)
        vg[:, cols] = value_t.T.astype(BF16)
        key_t = scale * lax.dot_general(
            q[0, 0, :, cols], dlow[head], TN, preferred_element_type=F32
        )
        kgt[cols, :] = key_t.astype(BF16)
        kg[:, cols] = key_t.T.astype(BF16)


def attend(queries, cotangent, keys, values):
    _, _, total, width = queries.shape
    span = 4 * keys[0].shape[0]
    same = bf16(*queries.shape)
    return call(
        attend_body,
        [queries, cotangent, *keys, *values],
        [same, same, bf16(span, width), bf16(span, width), bf16(width, span), bf16(width, span)],
        [pltpu.VMEM((width // HEAD_DIM, total, span), BF16)] * 2,
    )


def weight_body(count, offsets, final, index, grad_t, *refs):
    pieces, refs = refs[:count], refs[count:]
    moved, outs = refs[: len(offsets)], refs[len(offsets) :]
    for i in range(index.shape[0]):
        start = pl.multiple_of(index[i] * TILE, TILE)
        rows = jnp.concatenate([piece[:, pl.ds(start, TILE)] for piece in pieces], 0)
        total = jnp.dot(grad_t[...], rows, preferred_element_type=F32)
        for ref, offset in zip(moved, offsets):
            low = (offset + i) * TILE
            total = total + ref[:, low : low + TILE].astype(F32)
        cols = slice(i * TILE, (i + 1) * TILE)
        if final:
            outs[0][cols, :] = total.T.astype(BF16)
        else:
            outs[0][:, cols] = total.astype(BF16)


def weight_part(index, grad_t, pieces, moved=(), offsets=(), final=False):
    span = index.shape[0] * TILE
    width = grad_t.shape[0]
    return call(
        functools.partial(weight_body, len(pieces), offsets, final),
        [index, grad_t, *pieces, *moved],
        bf16(span, width) if final else bf16(width, span),
        index=1,
    )


def encoder_body(low, kg, vg, w, *refs):
    out = refs[-1]
    rows = slice(low, low + out.shape[0])
    for i in range(out.shape[1] // TILE):
        cols = slice(i * TILE, (i + 1) * TILE)
        total = lax.dot_general(kg[rows, :], w[0, 0, cols, :], NT, preferred_element_type=F32)
        total = total + lax.dot_general(
            vg[rows, :], w[0, 1, cols, :], NT, preferred_element_type=F32
        )
        if len(refs) > 1:
            total = total + refs[0][:, cols].astype(F32)
        out[:, cols] = total.astype(BF16)


def encoder_part(key_grad, value_grad, kv_weight, block, *moved):
    rows = key_grad.shape[0] // 4
    return call(
        functools.partial(encoder_body, block * rows),
        [key_grad, value_grad, kv_weight, *moved],
        bf16(rows, kv_weight.shape[2]),
    )


def tie(array, *others):
    return lax.optimization_barrier((array, *others))[0]


def on_device(encoded, kv_weight, queries, cotangent):
    core = lax.axis_index("tensor") % 2
    y = lax.axis_index("dp")
    block = encoded[0]
    half = block.shape[0] // 2

    h = {"o": lax.dynamic_slice_in_dim(block, core * half, half, 0)}
    h_too = {"o": lax.dynamic_slice_in_dim(block, (1 - core) * half, half, 0)}
    g, g_too = {}, {}
    h["a"] = send(h["o"], X_FIRST)
    g["o"] = send(h["o"], ALONG_Z)
    h["b"] = send(tie(h["o"], h["a"]), X_SECOND)
    g["a"] = send(tie(h["a"], g["o"]), ALONG_Z)
    h["d"] = send(tie(h["a"], h["b"]), X_SECOND)
    g["b"] = send(tie(h["b"], g["a"]), ALONG_Z)
    g["d"] = send(tie(h["d"], g["b"]), ALONG_Z)
    for name in "abd":
        h_too[name] = send(h[name], SWAP)
    for name in "oa":
        g_too[name] = send(g[name], SWAP)
    done = [
        project((h["o"], h_too["o"], h["a"], h_too["a"]), kv_weight),
        project((g["o"], g_too["o"], h["b"], h_too["b"]), kv_weight),
        project((g["a"], g_too["a"], h["d"], h_too["d"]), kv_weight),
    ]
    g_too["b"] = send(tie(g["b"], done[0][0], done[1][0]), SWAP)
    g_too["d"] = send(tie(g["d"], done[2][0]), SWAP)
    done.append(project((g["b"], g_too["b"], g["d"], g_too["d"]), kv_weight))
    keys, values = zip(*done)
    order = ["ho", "go", "hb", "gb", "ha", "ga", "hd", "gd"]
    pieces = [{"h": h, "g": g}[name[0]][name[1]] for name in order]
    pieces += [{"h": h_too, "g": g_too}[name[0]][name[1]] for name in order]

    attended, query_grad, key_grad, value_grad, key_grad_t, value_grad_t = attend(
        queries, cotangent, keys, values
    )

    one, other = y ^ 1, 3 - y
    first = jnp.where(core == 0, one, other)
    second = jnp.where(core == 0, other, one)
    across = (y + 2) % 4

    def tiles(*slices):
        return jnp.stack([2 * s + i for s in slices for i in range(2)]).astype(jnp.int32)

    value_out = weight_part(tiles(first, across), value_grad_t, pieces)
    value_in = send(value_out, Y_FIRST)

    key_grad, value_grad = lax.optimization_barrier((key_grad, value_grad, value_out))[:2]
    grads = (key_grad, value_grad, kv_weight)
    moved_send = send(encoder_part(*grads, 3), SWAP)
    moved_keep = send(encoder_part(*grads, 2), SWAP)
    x_out = encoder_part(*grads, 1, moved_send)
    x_in = send(x_out, X_FIRST)

    key_out = weight_part(tiles(first, across), tie(key_grad_t, x_out), pieces)
    key_in = send(tie(key_out, value_in), Y_FIRST)
    keep = encoder_part(tie(key_grad, key_out), value_grad, kv_weight, 0, moved_keep)

    total = keep.astype(F32) + x_in.astype(F32)
    x_in = send(total[2 * half :].astype(BF16), X_SECOND)
    total = total[: 2 * half] + x_in.astype(F32)
    here = total[:half] + send(total[half:].astype(BF16), BACK_Z).astype(F32)
    here = here.astype(BF16)
    last = (here.astype(F32) + send(here, ACROSS_Z).astype(F32)).astype(BF16)
    last_too = send(last, SWAP)
    enc_grad = jnp.where(
        core == 0, jnp.concatenate([last, last_too], 0), jnp.concatenate([last_too, last], 0)
    )

    value_two = weight_part(tiles(second), value_grad_t, pieces, [value_in], [2])
    value_two = send(tie(value_two, key_in), Y_SECOND)
    key_two = weight_part(tiles(second), key_grad_t, pieces, [key_in], [2])
    key_two = send(tie(key_two, value_two), Y_SECOND)
    value_share = weight_part(tiles(y), value_grad_t, pieces, [value_in, value_two], [0, 0], True)
    key_share = weight_part(tiles(y), key_grad_t, pieces, [key_in, key_two], [0, 0], True)
    share = jnp.stack([key_share, value_share], 0)
    return (attended, query_grad, enc_grad[None], share[None])


def solution(mesh):
    return jax.shard_map(
        on_device,
        mesh=mesh,
        in_specs=(
            P("dp", "pipe", None),
            P("pipe", None, None, "tensor"),
            P("dp", "pipe", None, "tensor"),
            P("dp", "pipe", None, "tensor"),
        ),
        out_specs=(
            P("dp", "pipe", None, "tensor"),
            P("dp", "pipe", None, "tensor"),
            P("dp", "pipe", None),
            P("pipe", None, "dp", "tensor"),
        ),
        check_vma=False,
    )
```

```python
import functools

import jax
import jax.numpy as jnp
from jax import lax
from jax.experimental import pallas as pl
from jax.experimental.pallas import tpu as pltpu
from jax.sharding import PartitionSpec as P

HEAD_DIM = 256
ALL = ("pipe", "tensor", "dp")
F32, BF16 = jnp.float32, jnp.bfloat16
NT = (((1,), (1,)), ((), ()))
TN = (((0,), (0,)), ((), ()))
TILE = 512
WHOLE = pl.BlockSpec(memory_space=pltpu.VMEM)
SCALARS = pl.BlockSpec(memory_space=pltpu.SMEM)


LITTLE = pl.CostEstimate(flops=1000, bytes_accessed=1000, transcendentals=0)


def call(body, operands, shapes, scratch=(), index=0, after=(), room=8):
    many = isinstance(shapes, (list, tuple))
    count = len(operands)
    operands = [*operands, *after]

    def reads(*refs):
        body(*refs[:count], *refs[count + len(after) :])

    return pl.pallas_call(
        reads,
        in_specs=[SCALARS] * index
        + [WHOLE] * (count - index)
        + [pl.BlockSpec(memory_space=pl.ANY)] * len(after),
        out_specs=[WHOLE] * len(shapes) if many else WHOLE,
        out_shape=shapes,
        scratch_shapes=scratch,
        compiler_params=pltpu.CompilerParams(vmem_limit_bytes=room * 1024 * 1024),
        cost_estimate=LITTLE,
    )(*operands)


def bf16(*shape):
    return jax.ShapeDtypeStruct(shape, BF16)


def pairs(move):
    def index(x, y, z, core):
        pipe = (z % 2) * 4 + x
        tensor = (z // 2) * 2 + core
        return (pipe * 4 + tensor) * 4 + y

    found = []
    for x in range(4):
        for y in range(4):
            for z in range(4):
                for core in range(2):
                    to_x, to_y, to_z, to_core = move(x, y, z, core)
                    found.append((index(x, y, z, core), index(to_x, to_y, to_z % 4, to_core)))
    return found


def partner(place, core, which):
    return place ^ 1 if core == which else 3 - place


X_FIRST = pairs(lambda x, y, z, core: (partner(x, core, 0), y, z, core))
X_SECOND = pairs(lambda x, y, z, core: (partner(x, core, 1), y, z, core))
Y_FIRST = pairs(lambda x, y, z, core: (x, partner(y, core, 0), z, core))
Y_SECOND = pairs(lambda x, y, z, core: (x, partner(y, core, 1), z, core))
ALONG_Z = pairs(lambda x, y, z, core: (x, y, z + 1 - 2 * core, core))
BACK_Z = pairs(lambda x, y, z, core: (x, y, z - 1 + 2 * core, core))
ACROSS_Z = pairs(lambda x, y, z, core: (x, y, z + 2, core))
SWAP = pairs(lambda x, y, z, core: (x, y, z, 1 - core))


def send(array, route):
    return lax.ppermute(array, ALL, route)


def project_body(a, b, c, d, w, keys, values):
    x = jnp.concatenate([a[...], b[...], c[...], d[...]], 0)
    keys[...] = jnp.dot(x, w[0, 0], preferred_element_type=F32).astype(BF16)
    values[...] = jnp.dot(x, w[0, 1], preferred_element_type=F32).astype(BF16)


def project(pieces, kv_weight):
    shape = bf16(4 * pieces[0].shape[0], kv_weight.shape[3])
    return call(project_body, [*pieces, kv_weight], [shape, shape])


def arrange(groups):
    quarter = groups[0].shape[0] // 4

    def at(group, place):
        return groups[group][place * quarter : (place + 1) * quarter, :]

    order = [(0, 0), (1, 0), (1, 2), (3, 0), (0, 2), (2, 0), (2, 2), (3, 2)]
    return jnp.concatenate(
        [at(g, p) for g, p in order] + [at(g, p + 1) for g, p in order], 0
    )


def attend_body(q, g, k0, k1, k2, k3, v0, v1, v2, v3, att, dq, kg, vg, kgt, vgt, low, dlow):
    scale = HEAD_DIM ** (-0.5)
    total = q.shape[2]
    chunk = total // 2
    for head in range(q.shape[3] // HEAD_DIM):
        cols = slice(head * HEAD_DIM, (head + 1) * HEAD_DIM)
        k = arrange([ref[:, cols] for ref in (k0, k1, k2, k3)])
        v = arrange([ref[:, cols] for ref in (v0, v1, v2, v3)])
        for part in range(2):
            rows = slice(part * chunk, (part + 1) * chunk)
            g_rows = g[0, 0, rows, cols]
            scores = scale * lax.dot_general(
                q[0, 0, rows, cols], k, NT, preferred_element_type=F32
            )
            expd = jnp.exp(scores - jnp.max(scores, axis=-1, keepdims=True))
            probs = expd * (1.0 / jnp.sum(expd, axis=-1, keepdims=True))
            probs_low = probs.astype(BF16)
            low[head, rows, :] = probs_low
            out = jnp.dot(probs_low, v, preferred_element_type=F32).astype(BF16)
            att[0, 0, rows, cols] = out
            dprobs = lax.dot_general(g_rows, v, NT, preferred_element_type=F32)
            delta = jnp.sum(g_rows.astype(F32) * out.astype(F32), axis=-1, keepdims=True)
            ds_low = (probs * (dprobs - delta)).astype(BF16)
            dlow[head, rows, :] = ds_low
            dq[0, 0, rows, cols] = (
                scale * jnp.dot(ds_low, k, preferred_element_type=F32)
            ).astype(BF16)
        value_t = lax.dot_general(g[0, 0, :, cols], low[head], TN, preferred_element_type=F32)
        vgt[cols, :] = value_t.astype(BF16)
        vg[:, cols] = value_t.T.astype(BF16)
        key_t = scale * lax.dot_general(
            q[0, 0, :, cols], dlow[head], TN, preferred_element_type=F32
        )
        kgt[cols, :] = key_t.astype(BF16)
        kg[:, cols] = key_t.T.astype(BF16)


def attend(queries, cotangent, keys, values):
    _, _, total, width = queries.shape
    span = 4 * keys[0].shape[0]
    same = bf16(*queries.shape)
    return call(
        attend_body,
        [queries, cotangent, *keys, *values],
        [same, same, bf16(span, width), bf16(span, width), bf16(width, span), bf16(width, span)],
        [pltpu.VMEM((width // HEAD_DIM, total, span), BF16)] * 2,
        room=16,
    )


def weight_body(count, index, grad_t, *refs):
    pieces, outs = refs[:count], refs[count:]
    for i, out in enumerate(outs):
        start = pl.multiple_of(index[i], out.shape[1])
        rows = jnp.concatenate([piece[:, pl.ds(start, out.shape[1])] for piece in pieces], 0)
        out[...] = jnp.dot(grad_t[...], rows, preferred_element_type=F32).astype(BF16)


def weight_part(index, widths, grad_t, pieces, after=()):
    return call(
        functools.partial(weight_body, len(pieces)),
        [index, grad_t, *pieces],
        [bf16(grad_t.shape[0], width) for width in widths],
        index=1,
        after=after,
    )


def share_body(part, count, *refs):
    out, turned, sems = refs[-3:]
    step = TILE // 2
    copies = []
    for i in range(count):
        for j in range(2):
            cols = slice(j * step, (j + 1) * step)
            rows = slice((2 * i + j) * step, (2 * i + j + 1) * step)
            total = sum(ref[:, cols].astype(F32) for ref in refs[3 * i : 3 * i + 3])
            turned[rows, :] = total.T.astype(BF16)
            copies.append(
                pltpu.make_async_copy(
                    turned.at[rows, :], out.at[0, part, rows, :], sems.at[2 * i + j]
                )
            )
            copies[-1].start()
    for copy in copies:
        copy.wait()


def share(part, terms, into=None):
    width = terms[0][0].shape[0]
    count = len(terms)
    given = [] if into is None else [into]
    return pl.pallas_call(
        functools.partial(share_body, part, count),
        in_specs=[WHOLE] * (3 * count) + [pl.BlockSpec(memory_space=pl.ANY)] * len(given),
        out_specs=pl.BlockSpec(memory_space=pl.ANY),
        out_shape=bf16(1, 2, count * TILE, width),
        scratch_shapes=[
            pltpu.VMEM((count * TILE, width), BF16),
            pltpu.SemaphoreType.DMA((2 * count,)),
        ],
        input_output_aliases={3 * count: 0} if given else {},
        compiler_params=pltpu.CompilerParams(vmem_limit_bytes=6 * 1024 * 1024),
        cost_estimate=LITTLE,
    )(*[term for tile in terms for term in tile], *given)


def place_body(core, mine, theirs, out, sems):
    half = mine.shape[0]
    low = pl.multiple_of(core[0] * half, half)
    high = pl.multiple_of((1 - core[0]) * half, half)
    copies = [
        pltpu.make_async_copy(mine, out.at[0, pl.ds(low, half), :], sems.at[0]),
        pltpu.make_async_copy(theirs, out.at[0, pl.ds(high, half), :], sems.at[1]),
    ]
    for copy in copies:
        copy.start()
    for copy in copies:
        copy.wait()


def place(core, mine, theirs):
    half, depth = mine.shape
    return pl.pallas_call(
        place_body,
        in_specs=[SCALARS, WHOLE, WHOLE],
        out_specs=pl.BlockSpec(memory_space=pl.ANY),
        out_shape=bf16(1, 2 * half, depth),
        scratch_shapes=[pltpu.SemaphoreType.DMA((2,))],
        compiler_params=pltpu.CompilerParams(vmem_limit_bytes=4 * 1024 * 1024),
        cost_estimate=LITTLE,
    )(core[None], mine, theirs)


def load_body(*refs):
    count = len(refs) // 2
    sems = refs[-1]
    copies = [
        pltpu.make_async_copy(refs[i], refs[count + i], sems.at[i]) for i in range(count)
    ]
    for copy in copies:
        copy.start()
    for copy in copies:
        copy.wait()


def load(*arrays):
    return pl.pallas_call(
        load_body,
        in_specs=[pl.BlockSpec(memory_space=pl.ANY)] * len(arrays),
        out_specs=[WHOLE] * len(arrays),
        out_shape=[bf16(*array.shape) for array in arrays],
        scratch_shapes=[pltpu.SemaphoreType.DMA((len(arrays),))],
        compiler_params=pltpu.CompilerParams(vmem_limit_bytes=4 * 1024 * 1024),
        cost_estimate=LITTLE,
    )(*arrays)


def encoder_body(low, left, kg, vg, w, *refs):
    out = refs[-1]
    rows = slice(low, low + out.shape[0])
    for i in range(out.shape[1] // TILE):
        cols = slice(i * TILE, (i + 1) * TILE)
        from_w = slice(left + i * TILE, left + (i + 1) * TILE)
        total = lax.dot_general(kg[rows, :], w[0, 0, from_w, :], NT, preferred_element_type=F32)
        total = total + lax.dot_general(
            vg[rows, :], w[0, 1, from_w, :], NT, preferred_element_type=F32
        )
        if len(refs) > 1:
            total = total + refs[0][:, cols].astype(F32)
        out[:, cols] = total.astype(BF16)


def encoder_part(key_grad, value_grad, kv_weight, block, moved=None, columns=(0, 1), after=()):
    rows = key_grad.shape[0] // 4
    depth = kv_weight.shape[2] // columns[1]
    return call(
        functools.partial(encoder_body, block * rows, columns[0] * depth),
        [key_grad, value_grad, kv_weight] + ([] if moved is None else [moved]),
        bf16(rows, depth),
        after=after,
    )


def tie(array, *others):
    return lax.optimization_barrier((array, *others))[0]


def on_device(encoded, kv_weight, queries, cotangent):
    core = lax.axis_index("tensor") % 2
    y = lax.axis_index("dp")
    block = encoded[0]
    half = block.shape[0] // 2

    h = {"o": lax.dynamic_slice_in_dim(block, core * half, half, 0)}
    h_too = {"o": lax.dynamic_slice_in_dim(block, (1 - core) * half, half, 0)}
    g, g_too = {}, {}
    h["a"] = send(h["o"], X_FIRST)
    h["b"] = send(h["o"], X_SECOND)
    g["o"] = send(h["o"], ALONG_Z)
    kv_weight, queries, cotangent = load(kv_weight, queries, cotangent)
    g["a"] = send(tie(h["a"], kv_weight, queries), ALONG_Z)
    h["d"] = send(h["a"], X_SECOND)
    g["b"] = send(h["b"], ALONG_Z)
    h_too["a"] = send(h["a"], SWAP)
    h_too["b"] = send(h["b"], SWAP)
    g_too["o"] = send(g["o"], SWAP)
    done = [
        project((h["o"], h_too["o"], h["a"], h_too["a"]), kv_weight),
        project((g["o"], g_too["o"], h["b"], h_too["b"]), kv_weight),
    ]
    g["d"] = send(tie(g["a"], done[0][0], done[1][0]), X_SECOND)
    h_too["d"] = send(h["d"], SWAP)
    g_too["a"] = send(g["a"], SWAP)
    g_too["b"] = send(g["b"], SWAP)
    done.append(project((g["a"], g_too["a"], h["d"], h_too["d"]), kv_weight))
    g_too["d"] = send(tie(g["d"], done[2][0]), SWAP)
    done.append(project((g["b"], g_too["b"], g["d"], g_too["d"]), kv_weight))
    keys, values = zip(*done)
    order = ["ho", "go", "hb", "gb", "ha", "ga", "hd", "gd"]
    pieces = [{"h": h, "g": g}[name[0]][name[1]] for name in order]
    pieces += [{"h": h_too, "g": g_too}[name[0]][name[1]] for name in order]

    attended, query_grad, key_grad, value_grad, key_grad_t, value_grad_t = attend(
        queries, cotangent, keys, values
    )

    one, other = y ^ 1, 3 - y
    first = jnp.where(core == 0, one, other)
    second = jnp.where(core == 0, other, one)
    across = (y + 2) % 4

    def starts(*places):
        return jnp.stack([2 * TILE * place + low for place, low in places]).astype(jnp.int32)

    half_tile = TILE // 2
    go = starts((across, 0), (across, TILE), (first, 0), (first, TILE))
    go_five = starts(
        (across, 0), (across, half_tile), (across, TILE), (first, 0), (first, TILE)
    )
    stay = starts((second, 0), (second, TILE), (y, 0), (y, TILE))
    value_out = weight_part(
        go_five, [half_tile, half_tile, TILE, TILE, TILE], value_grad_t, pieces
    )

    def chain(out, route, moved=()):
        moved = list(moved)
        for part in out:
            moved.append(send(tie(part, *moved[-1:]), route))
        return moved

    def onward(keep, moved):
        return [
            (keep[i].astype(F32) + moved[i].astype(F32)).astype(BF16) for i in range(2)
        ]

    value_in = chain(value_out, Y_FIRST)
    key_out = weight_part(go, [TILE] * 4, key_grad_t, pieces, value_out[:1])
    key_in = chain(key_out, Y_FIRST)

    grads = (key_grad, value_grad, kv_weight)
    early = (value_in[0], key_out[0])
    moved = [send(encoder_part(*grads, 3, None, (i, 2), early), SWAP) for i in range(2)]
    moved_keep = send(encoder_part(*grads, 2, None, (0, 1), early), SWAP)
    early = (value_in[1],)
    x_out = [encoder_part(*grads, 1, moved[i], (i, 2), early) for i in range(2)]
    x_in = [send(part, X_FIRST) for part in x_out]
    keep = encoder_part(*grads, 0, moved_keep, (0, 1), x_out)
    value_keep = weight_part(stay, [TILE] * 4, value_grad_t, pieces, [keep])
    key_keep = weight_part(stay, [TILE] * 4, key_grad_t, pieces, value_keep[:1])

    value_in = [jnp.concatenate(value_in[:2], 1), *value_in[2:]]
    value_two = chain(onward(value_keep, value_in), Y_SECOND, value_in[-1:])[1:]
    key_two = chain(onward(key_keep, key_in), Y_SECOND, key_in[-1:])[1:]

    keep = tie(keep, key_keep[0], value_in[2])
    total = keep.astype(F32) + jnp.concatenate(x_in, 1).astype(F32)
    x_in = send(total[2 * half :].astype(BF16), X_SECOND)
    total = tie(total, value_in[3])[: 2 * half] + x_in.astype(F32)
    here = total[:half] + send(total[half:].astype(BF16), BACK_Z).astype(F32)
    here = tie(here.astype(BF16), value_two[0])
    last = (here.astype(F32) + send(here, ACROSS_Z).astype(F32)).astype(BF16)
    last = tie(last, value_two[1])
    enc_grad = place(core, last, send(last, SWAP))

    def terms(keep, one, two):
        return [(keep[2 + i], one[2 + i], two[i]) for i in range(2)]

    weight_grad = share(1, terms(value_keep, value_in, value_two))
    weight_grad = share(0, terms(key_keep, key_in, key_two), weight_grad)
    return (attended, query_grad, enc_grad, weight_grad)


def solution(mesh):
    return jax.shard_map(
        on_device,
        mesh=mesh,
        in_specs=(
            P("dp", "pipe", None),
            P("pipe", None, None, "tensor"),
            P("dp", "pipe", None, "tensor"),
            P("dp", "pipe", None, "tensor"),
        ),
        out_specs=(
            P("dp", "pipe", None, "tensor"),
            P("dp", "pipe", None, "tensor"),
            P("dp", "pipe", None),
            P("pipe", None, "dp", "tensor"),
        ),
        check_vma=False,
    )
```

```python
import functools

import jax
import jax.numpy as jnp
from jax import lax
from jax.experimental import pallas as pl
from jax.experimental.pallas import tpu as pltpu
from jax.sharding import PartitionSpec as P

HEAD_DIM = 256
ALL = ("pipe", "tensor", "dp")
F32, BF16 = jnp.float32, jnp.bfloat16
NT = (((1,), (1,)), ((), ()))
TN = (((0,), (0,)), ((), ()))
TILE = 512
ANY = pl.BlockSpec(memory_space=pl.ANY)
SCALARS = pl.BlockSpec(memory_space=pltpu.SMEM)
LITTLE = pl.CostEstimate(flops=1000, bytes_accessed=1000, transcendentals=0)


def bf16(*shape):
    return jax.ShapeDtypeStruct(shape, BF16)


def vmem(*shape):
    return pltpu.VMEM(shape, BF16)


def call(body, operands, shapes, scratch, copies, after=(), aliases=None):
    count = len(operands)
    operands = [*operands, *after]

    def reads(*refs):
        body(*refs[:count], *refs[count + len(after) :])

    return pl.pallas_call(
        reads,
        in_specs=[ANY] * len(operands),
        out_specs=[ANY] * len(shapes),
        out_shape=shapes,
        scratch_shapes=[*scratch, pltpu.SemaphoreType.DMA((copies,))],
        input_output_aliases=aliases or {},
        compiler_params=pltpu.CompilerParams(vmem_limit_bytes=40 * 1024 * 1024),
        cost_estimate=LITTLE,
    )(*operands)


class Copies:
    def __init__(self, sems):
        self.sems, self.used = sems, 0

    def start(self, source, target):
        copy = pltpu.make_async_copy(source, target, self.sems.at[self.used])
        self.used += 1
        copy.start()
        return copy


def wait(copies):
    for copy in copies:
        copy.wait()


def pairs(move):
    def index(x, y, z, core):
        pipe = (z % 2) * 4 + x
        tensor = (z // 2) * 2 + core
        return (pipe * 4 + tensor) * 4 + y

    found = []
    for x in range(4):
        for y in range(4):
            for z in range(4):
                for core in range(2):
                    to_x, to_y, to_z, to_core = move(x, y, z, core)
                    found.append((index(x, y, z, core), index(to_x, to_y, to_z % 4, to_core)))
    return found


def partner(place, core, which):
    return place ^ 1 if core == which else 3 - place


X_FIRST = pairs(lambda x, y, z, core: (partner(x, core, 0), y, z, core))
X_SECOND = pairs(lambda x, y, z, core: (partner(x, core, 1), y, z, core))
Y_FIRST = pairs(lambda x, y, z, core: (x, partner(y, core, 0), z, core))
Y_SECOND = pairs(lambda x, y, z, core: (x, partner(y, core, 1), z, core))
ALONG_Z = pairs(lambda x, y, z, core: (x, y, z + 1 - 2 * core, core))
BACK_Z = pairs(lambda x, y, z, core: (x, y, z - 1 + 2 * core, core))
ACROSS_Z = pairs(lambda x, y, z, core: (x, y, z + 2, core))
SWAP = pairs(lambda x, y, z, core: (x, y, z, 1 - core))


def send(array, route):
    return lax.ppermute(array, ALL, route)


def project_body(a, b, c, d, w, keys, values, x, w_in, acc, out, sems):
    copies = Copies(sems)
    rows = a.shape[0]
    depth = x.shape[1] // 4
    x_copies, w_copies = [], []
    for i, piece in enumerate((a, b, c, d)):
        x_copies.append(copies.start(piece, x.at[i * rows : (i + 1) * rows, :]))
    for i in range(4):
        span = slice(i * depth, (i + 1) * depth)
        w_copies.append(copies.start(w.at[0, :, span, :], w_in.at[:, span, :]))
    wait(x_copies)
    for i in range(4):
        span = slice(i * depth, (i + 1) * depth)
        w_copies[i].wait()
        for part in range(2):
            dot = jnp.dot(x[:, span], w_in[part, span, :], preferred_element_type=F32)
            if i > 0:
                dot = dot + acc[part]
            if i < 3:
                acc[part] = dot
            else:
                out[part] = dot.astype(BF16)
    wait([copies.start(out.at[0], keys), copies.start(out.at[1], values)])


def project(pieces, kv_weight):
    _, _, depth, width = kv_weight.shape
    rows = 4 * pieces[0].shape[0]
    return call(
        project_body,
        [*pieces, kv_weight],
        [bf16(rows, width)] * 2,
        [
            vmem(rows, depth),
            vmem(2, depth, width),
            pltpu.VMEM((2, rows, width), F32),
            vmem(2, rows, width),
        ],
        10,
    )


KEEP, SEND = [(0, 0), (1, 0), (1, 2), (3, 0)], [(0, 2), (2, 0), (2, 2), (3, 2)]
ORDER = KEEP + SEND + [(g, p + 1) for g, p in KEEP + SEND]


def attend_body(q_any, g_any, *refs):
    groups, refs = refs[:8], refs[8:]
    att_any, dq_any, kg_any, vg_any = refs[:4]
    q, g, k_all, v_all, att, dq, kg, vg, low, dlow, sems = refs[4:]
    copies = Copies(sems)
    piece = groups[0].shape[0] // 4
    coming = [copies.start(q_any.at[0, 0], q)]
    for target, own in ((k_all, groups[:4]), (v_all, groups[4:])):
        for i, (group, place) in enumerate(ORDER):
            coming.append(
                copies.start(
                    own[group].at[place * piece : (place + 1) * piece, :],
                    target.at[i * piece : (i + 1) * piece, :],
                )
            )
    coming.append(copies.start(g_any.at[0, 0], g))
    wait(coming)
    going = []
    scale = HEAD_DIM ** (-0.5)
    total = q.shape[0]
    chunk = total // 2
    for head in range(q.shape[1] // HEAD_DIM):
        cols = slice(head * HEAD_DIM, (head + 1) * HEAD_DIM)
        k, v = k_all[:, cols], v_all[:, cols]
        for part in range(2):
            rows = slice(part * chunk, (part + 1) * chunk)
            g_rows = g[rows, cols]
            scores = scale * lax.dot_general(q[rows, cols], k, NT, preferred_element_type=F32)
            expd = jnp.exp(scores - jnp.max(scores, axis=-1, keepdims=True))
            probs = expd * (1.0 / jnp.sum(expd, axis=-1, keepdims=True))
            probs_low = probs.astype(BF16)
            low[head, rows, :] = probs_low
            out = jnp.dot(probs_low, v, preferred_element_type=F32).astype(BF16)
            att[rows, cols] = out
            dprobs = lax.dot_general(g_rows, v, NT, preferred_element_type=F32)
            delta = jnp.sum(g_rows.astype(F32) * out.astype(F32), axis=-1, keepdims=True)
            ds_low = (probs * (dprobs - delta)).astype(BF16)
            dlow[head, rows, :] = ds_low
            dq[rows, cols] = (scale * jnp.dot(ds_low, k, preferred_element_type=F32)).astype(BF16)
        value_t = lax.dot_general(g[:, cols], low[head], TN, preferred_element_type=F32)
        vg[:, cols] = value_t.T.astype(BF16)
        key_t = scale * lax.dot_general(q[:, cols], dlow[head], TN, preferred_element_type=F32)
        kg[:, cols] = key_t.T.astype(BF16)
        for source, target in ((vg, vg_any), (kg, kg_any)):
            going.append(copies.start(source.at[:, cols], target.at[:, cols]))
        for source, target in ((att, att_any), (dq, dq_any)):
            going.append(copies.start(source.at[:, cols], target.at[0, 0, :, cols]))
    wait(going)


def attend(queries, cotangent, keys, values):
    _, _, total, width = queries.shape
    span = 4 * keys[0].shape[0]
    same, tall = bf16(*queries.shape), bf16(span, width)
    low = vmem(width // HEAD_DIM, total, span)
    return call(
        attend_body,
        [queries, cotangent, *keys, *values],
        [same, same, tall, tall],
        [vmem(total, width)] * 2
        + [vmem(span, width)] * 2
        + [vmem(total, width)] * 2
        + [vmem(span, width)] * 2
        + [low, low],
        2 + 2 * len(ORDER) + 4 * (width // HEAD_DIM),
    )


def weight_body(grad_any, *refs):
    pieces, (out_any, grad, tiles, outs, sems) = refs[:-5], refs[-5:]
    copies = Copies(sems)
    rows = pieces[0].shape[0]
    steps = out_any.shape[0] // TILE

    def fetch(i):
        return [
            copies.start(
                piece.at[:, i * TILE : (i + 1) * TILE],
                tiles.at[i % 2, j * rows : (j + 1) * rows, :],
            )
            for j, piece in enumerate(pieces)
        ]

    coming = fetch(0)
    grad_copy = copies.start(grad_any, grad)
    going = []
    for i in range(steps):
        after = fetch(i + 1) if i + 1 < steps else []
        wait(coming)
        if i == 0:
            grad_copy.wait()
        if i > 1:
            going[i - 2].wait()
        outs[i % 2] = lax.dot_general(
            tiles[i % 2], grad[...], TN, preferred_element_type=F32
        ).astype(BF16)
        going.append(copies.start(outs.at[i % 2], out_any.at[i * TILE : (i + 1) * TILE, :]))
        coming = after
    wait(going[-2:])


def weight_part(grad, pieces, after=()):
    span, width = grad.shape
    depth = pieces[0].shape[1]
    steps = depth // TILE
    return call(
        weight_body,
        [grad, *pieces],
        [bf16(depth, width)],
        [vmem(span, width), vmem(2, span, TILE), vmem(2, TILE, width)],
        1 + steps * (len(pieces) + 1),
        after,
    )[0]


def encoder_body(low, left, kg_any, vg_any, w, *refs):
    outs_any, (grads, w_in, out, came, sems) = refs[-7:-5], refs[-5:]
    moved = refs[:-7]
    copies = Copies(sems)
    rows, span = out.shape
    steps = span // TILE
    coming = [
        copies.start(ref.at[low : low + rows, :], grads.at[i])
        for i, ref in enumerate((kg_any, vg_any))
    ]
    w_copies, moved_copies, going = [], [], []
    for i in range(steps):
        cols = slice(i * TILE, (i + 1) * TILE)
        from_w = slice(left + i * TILE, left + (i + 1) * TILE)
        w_copies.append(copies.start(w.at[0, :, from_w, :], w_in.at[:, cols, :]))
        if moved:
            moved_copies.append(copies.start(moved[0].at[:, cols], came.at[:, cols]))
    wait(coming)
    for i in range(steps):
        cols = slice(i * TILE, (i + 1) * TILE)
        w_copies[i].wait()
        total = lax.dot_general(grads[0], w_in[0, cols, :], NT, preferred_element_type=F32)
        total = total + lax.dot_general(
            grads[1], w_in[1, cols, :], NT, preferred_element_type=F32
        )
        if moved:
            moved_copies[i].wait()
            total = total + came[:, cols].astype(F32)
        out[:, cols] = total.astype(BF16)
        if not moved:
            going.append(copies.start(out.at[:, cols], outs_any[0].at[:, cols]))
            continue
        for j, target in enumerate(outs_any):
            part = slice(j * rows // 2, (j + 1) * rows // 2)
            going.append(copies.start(out.at[part, cols], target.at[:, cols]))
    wait(going)


def encoder_part(key_grad, value_grad, kv_weight, side, columns, moved=None, after=()):
    span, width = key_grad.shape
    rows, depth = span // 2, kv_weight.shape[2] // 2
    shapes = [bf16(rows, depth), bf16(8, 128)] if moved is None else [bf16(rows // 2, depth)] * 2
    return call(
        functools.partial(encoder_body, side * rows, columns * depth),
        [key_grad, value_grad, kv_weight] + ([] if moved is None else [moved]),
        shapes,
        [vmem(2, rows, width), vmem(2, depth, width), vmem(rows, depth), vmem(rows, depth)],
        2 + 4 * depth // TILE,
        after,
    )


def put_body(part, array, *refs):
    out, sems = refs[-2:]
    wait([Copies(sems).start(array, out.at[0, part])])


def put(part, array, into=None):
    given = [] if into is None else [into]
    return call(
        functools.partial(put_body, part),
        [array, *given],
        [bf16(1, 2, *array.shape)],
        [],
        1,
        aliases={1: 0} if given else None,
    )[0]


def place_body(core, mine, theirs, out, sems):
    half = mine.shape[0]
    low = pl.multiple_of(core[0] * half, half)
    high = pl.multiple_of((1 - core[0]) * half, half)
    copies = Copies(sems)
    wait(
        [
            copies.start(mine, out.at[0, pl.ds(low, half), :]),
            copies.start(theirs, out.at[0, pl.ds(high, half), :]),
        ]
    )


def place(core, mine, theirs):
    half, depth = mine.shape
    return pl.pallas_call(
        place_body,
        in_specs=[SCALARS, ANY, ANY],
        out_specs=ANY,
        out_shape=bf16(1, 2 * half, depth),
        scratch_shapes=[pltpu.SemaphoreType.DMA((2,))],
        cost_estimate=LITTLE,
    )(core[None], mine, theirs)


def tie(array, *others):
    return lax.optimization_barrier((array, *others))[0]


def on_device(encoded, kv_weight, queries, cotangent):
    core = lax.axis_index("tensor") % 2
    block = encoded[0]
    half = block.shape[0] // 2

    h = {"o": lax.dynamic_slice_in_dim(block, core * half, half, 0)}
    h_too = {"o": lax.dynamic_slice_in_dim(block, (1 - core) * half, half, 0)}
    g, g_too = {}, {}
    h["a"] = send(h["o"], X_FIRST)
    h["b"] = send(h["o"], X_SECOND)
    g["o"] = send(h["o"], ALONG_Z)
    g["a"] = send(h["a"], ALONG_Z)
    h["d"] = send(h["a"], X_SECOND)
    g["b"] = send(h["b"], ALONG_Z)
    h_too["a"] = send(h["a"], SWAP)
    h_too["b"] = send(h["b"], SWAP)
    g_too["o"] = send(g["o"], SWAP)
    done = [
        project((h["o"], h_too["o"], h["a"], h_too["a"]), kv_weight),
        project((g["o"], g_too["o"], h["b"], h_too["b"]), kv_weight),
    ]
    g["d"] = send(tie(g["a"], done[0][0], done[1][0]), X_SECOND)
    h_too["d"] = send(h["d"], SWAP)
    g_too["a"] = send(g["a"], SWAP)
    g_too["b"] = send(g["b"], SWAP)
    done.append(project((g["a"], g_too["a"], h["d"], h_too["d"]), kv_weight))
    g_too["d"] = send(tie(g["d"], done[2][0]), SWAP)
    done.append(project((g["b"], g_too["b"], g["d"], g_too["d"]), kv_weight))
    keys, values = zip(*done)
    names = ["ho", "go", "hb", "gb", "ha", "ga", "hd", "gd"]
    pieces = [{"h": h, "g": g}[name[0]][name[1]] for name in names]
    pieces += [{"h": h_too, "g": g_too}[name[0]][name[1]] for name in names]

    attended, query_grad, key_grad, value_grad = attend(queries, cotangent, keys, values)

    def scatter(part):
        return lax.psum_scatter(part, "dp", scatter_dimension=0, tiled=True)

    value_part = weight_part(value_grad, pieces)
    value_share = scatter(value_part)

    grads = (key_grad, value_grad, kv_weight)
    early = (value_part,)
    moved = [send(encoder_part(*grads, 1, i, None, early)[0], SWAP) for i in range(2)]
    kept, x_out = zip(*[encoder_part(*grads, 0, i, moved[i]) for i in range(2)])
    key_part = weight_part(key_grad, pieces, x_out)
    key_share = scatter(key_part)
    totals = []
    for keep, out in zip(kept, x_out):
        came = send(out, X_FIRST)
        total = tie(keep, key_part).astype(F32) + came.astype(F32)
        came = send(total[2 * half :].astype(BF16), X_SECOND)
        totals.append(total[: 2 * half] + came.astype(F32))
    total = jnp.concatenate(totals, 1)

    here = total[:half] + send(total[half:].astype(BF16), BACK_Z).astype(F32)
    here = here.astype(BF16)
    last = (here.astype(F32) + send(here, ACROSS_Z).astype(F32)).astype(BF16)
    enc_grad = place(core, last, send(last, SWAP))

    weight_grad = put(0, key_share, put(1, value_share))
    return (attended, query_grad, enc_grad, weight_grad)


def solution(mesh):
    return jax.shard_map(
        on_device,
        mesh=mesh,
        in_specs=(
            P("dp", "pipe", None),
            P("pipe", None, None, "tensor"),
            P("dp", "pipe", None, "tensor"),
            P("dp", "pipe", None, "tensor"),
        ),
        out_specs=(
            P("dp", "pipe", None, "tensor"),
            P("dp", "pipe", None, "tensor"),
            P("dp", "pipe", None),
            P("pipe", None, "dp", "tensor"),
        ),
        check_vma=False,
    )
```

```python
import functools

import jax
import jax.numpy as jnp
from jax import lax
from jax.experimental import pallas as pl
from jax.experimental.pallas import tpu as pltpu
from jax.sharding import PartitionSpec as P

HEAD_DIM = 256
ALL = ("pipe", "tensor", "dp")
F32, BF16 = jnp.float32, jnp.bfloat16
NT = (((1,), (1,)), ((), ()))
TN = (((0,), (0,)), ((), ()))
TILE = 512
WHOLE = pl.BlockSpec(memory_space=pltpu.VMEM)
SCALARS = pl.BlockSpec(memory_space=pltpu.SMEM)


LITTLE = pl.CostEstimate(flops=1000, bytes_accessed=1000, transcendentals=0)


def call(body, operands, shapes, scratch=(), index=0, after=(), room=8):
    many = isinstance(shapes, (list, tuple))
    count = len(operands)
    operands = [*operands, *after]

    def reads(*refs):
        body(*refs[:count], *refs[count + len(after) :])

    return pl.pallas_call(
        reads,
        in_specs=[SCALARS] * index
        + [WHOLE] * (count - index)
        + [pl.BlockSpec(memory_space=pl.ANY)] * len(after),
        out_specs=[WHOLE] * len(shapes) if many else WHOLE,
        out_shape=shapes,
        scratch_shapes=scratch,
        compiler_params=pltpu.CompilerParams(vmem_limit_bytes=room * 1024 * 1024),
        cost_estimate=LITTLE,
    )(*operands)


def bf16(*shape):
    return jax.ShapeDtypeStruct(shape, BF16)


def pairs(move):
    def index(x, y, z, core):
        pipe = (z % 2) * 4 + x
        tensor = (z // 2) * 2 + core
        return (pipe * 4 + tensor) * 4 + y

    found = []
    for x in range(4):
        for y in range(4):
            for z in range(4):
                for core in range(2):
                    to_x, to_y, to_z, to_core = move(x, y, z, core)
                    found.append((index(x, y, z, core), index(to_x, to_y, to_z % 4, to_core)))
    return found


def partner(place, core, which):
    return place ^ 1 if core == which else 3 - place


X_FIRST = pairs(lambda x, y, z, core: (partner(x, core, 0), y, z, core))
X_SECOND = pairs(lambda x, y, z, core: (partner(x, core, 1), y, z, core))
Y_FIRST = pairs(lambda x, y, z, core: (x, partner(y, core, 0), z, core))
Y_SECOND = pairs(lambda x, y, z, core: (x, partner(y, core, 1), z, core))
ALONG_Z = pairs(lambda x, y, z, core: (x, y, z + 1 - 2 * core, core))
BACK_Z = pairs(lambda x, y, z, core: (x, y, z - 1 + 2 * core, core))
ACROSS_Z = pairs(lambda x, y, z, core: (x, y, z + 2, core))
SWAP = pairs(lambda x, y, z, core: (x, y, z, 1 - core))


def send(array, route):
    return lax.ppermute(array, ALL, route)


def project_body(a, b, c, d, w, keys, values):
    x = jnp.concatenate([a[...], b[...], c[...], d[...]], 0)
    keys[...] = jnp.dot(x, w[0, 0], preferred_element_type=F32).astype(BF16)
    values[...] = jnp.dot(x, w[0, 1], preferred_element_type=F32).astype(BF16)


def project(pieces, kv_weight):
    shape = bf16(4 * pieces[0].shape[0], kv_weight.shape[3])
    return call(project_body, [*pieces, kv_weight], [shape, shape])


def arrange(groups):
    quarter = groups[0].shape[0] // 4

    def at(group, place):
        return groups[group][place * quarter : (place + 1) * quarter, :]

    order = [(0, 0), (1, 0), (1, 2), (3, 0), (0, 2), (2, 0), (2, 2), (3, 2)]
    return jnp.concatenate(
        [at(g, p) for g, p in order] + [at(g, p + 1) for g, p in order], 0
    )


def attend_body(q, g, k0, k1, k2, k3, v0, v1, v2, v3, att, dq, kg, vg, kgt, vgt, low, dlow):
    scale = HEAD_DIM ** (-0.5)
    total = q.shape[2]
    chunk = total // 2
    for head in range(q.shape[3] // HEAD_DIM):
        cols = slice(head * HEAD_DIM, (head + 1) * HEAD_DIM)
        k = arrange([ref[:, cols] for ref in (k0, k1, k2, k3)])
        v = arrange([ref[:, cols] for ref in (v0, v1, v2, v3)])
        for part in range(2):
            rows = slice(part * chunk, (part + 1) * chunk)
            g_rows = g[0, 0, rows, cols]
            scores = scale * lax.dot_general(
                q[0, 0, rows, cols], k, NT, preferred_element_type=F32
            )
            expd = jnp.exp(scores - jnp.max(scores, axis=-1, keepdims=True))
            probs = expd * (1.0 / jnp.sum(expd, axis=-1, keepdims=True))
            probs_low = probs.astype(BF16)
            low[head, rows, :] = probs_low
            out = jnp.dot(probs_low, v, preferred_element_type=F32).astype(BF16)
            att[0, 0, rows, cols] = out
            dprobs = lax.dot_general(g_rows, v, NT, preferred_element_type=F32)
            delta = jnp.sum(g_rows.astype(F32) * out.astype(F32), axis=-1, keepdims=True)
            ds_low = (probs * (dprobs - delta)).astype(BF16)
            dlow[head, rows, :] = ds_low
            dq[0, 0, rows, cols] = (
                scale * jnp.dot(ds_low, k, preferred_element_type=F32)
            ).astype(BF16)
        value_t = lax.dot_general(g[0, 0, :, cols], low[head], TN, preferred_element_type=F32)
        vgt[cols, :] = value_t.astype(BF16)
        vg[:, cols] = value_t.T.astype(BF16)
        key_t = scale * lax.dot_general(
            q[0, 0, :, cols], dlow[head], TN, preferred_element_type=F32
        )
        kgt[cols, :] = key_t.astype(BF16)
        kg[:, cols] = key_t.T.astype(BF16)


def attend(queries, cotangent, keys, values):
    _, _, total, width = queries.shape
    span = 4 * keys[0].shape[0]
    same = bf16(*queries.shape)
    return call(
        attend_body,
        [queries, cotangent, *keys, *values],
        [same, same, bf16(span, width), bf16(span, width), bf16(width, span), bf16(width, span)],
        [pltpu.VMEM((width // HEAD_DIM, total, span), BF16)] * 2,
        room=16,
    )


def weight_body(count, index, grad_t, *refs):
    pieces, (out_any, tiles, outs, sems, out_sems) = refs[:count], refs[count:]
    rows = pieces[0].shape[0]
    steps = index.shape[0]

    def fetch(i):
        start = pl.multiple_of(index[i], TILE)
        copies = [
            pltpu.make_async_copy(
                piece.at[:, pl.ds(start, TILE)],
                tiles.at[i % 2, j * rows : (j + 1) * rows, :],
                sems.at[i * count + j],
            )
            for j, piece in enumerate(pieces)
        ]
        for copy in copies:
            copy.start()
        return copies

    coming = fetch(0)
    going = []
    for i in range(steps):
        after = fetch(i + 1) if i + 1 < steps else []
        for copy in coming:
            copy.wait()
        cols = slice(i * TILE, (i + 1) * TILE)
        outs[:, cols] = jnp.dot(
            grad_t[...], tiles[i % 2], preferred_element_type=F32
        ).astype(BF16)
        going.append(
            pltpu.make_async_copy(outs.at[:, cols], out_any.at[:, cols], out_sems.at[i])
        )
        going[-1].start()
        coming = after
    for copy in going:
        copy.wait()


def weight_part(index, grad_t, pieces, after=()):
    width, span = grad_t.shape
    steps, count = index.shape[0], len(pieces)

    def body(*refs):
        weight_body(count, *refs[: 2 + count], *refs[2 + count + len(after) :])

    return pl.pallas_call(
        body,
        in_specs=[SCALARS, WHOLE] + [pl.BlockSpec(memory_space=pl.ANY)] * (count + len(after)),
        out_specs=pl.BlockSpec(memory_space=pl.ANY),
        out_shape=bf16(width, steps * TILE),
        scratch_shapes=[
            pltpu.VMEM((2, span, TILE), BF16),
            pltpu.VMEM((width, steps * TILE), BF16),
            pltpu.SemaphoreType.DMA((steps * count,)),
            pltpu.SemaphoreType.DMA((steps,)),
        ],
        compiler_params=pltpu.CompilerParams(vmem_limit_bytes=34 * 1024 * 1024),
        cost_estimate=LITTLE,
    )(index, grad_t, *pieces, *after)


def share_body(part, keep, first, second, *refs):
    out, terms, turned, sems = refs[-4:]
    span = second.shape[1]
    step = TILE // 2
    sources = (keep.at[:, span:], first.at[:, :span], second)
    coming = [
        pltpu.make_async_copy(source, terms.at[i], sems.at[i])
        for i, source in enumerate(sources)
    ]
    for copy in coming:
        copy.start()
    for copy in coming:
        copy.wait()
    going = []
    for i in range(span // step):
        cols = slice(i * step, (i + 1) * step)
        total = terms[0, :, cols].astype(F32) + terms[1, :, cols].astype(F32)
        total = total + terms[2, :, cols].astype(F32)
        turned[cols, :] = total.T.astype(BF16)
        going.append(
            pltpu.make_async_copy(turned.at[cols, :], out.at[0, part, cols, :], sems.at[3 + i])
        )
        going[-1].start()
    for copy in going:
        copy.wait()


def share(part, keep, first, second, into=None):
    width, span = second.shape
    given = [] if into is None else [into]
    return pl.pallas_call(
        functools.partial(share_body, part),
        in_specs=[pl.BlockSpec(memory_space=pl.ANY)] * (3 + len(given)),
        out_specs=pl.BlockSpec(memory_space=pl.ANY),
        out_shape=bf16(1, 2, span, width),
        scratch_shapes=[
            pltpu.VMEM((3, width, span), BF16),
            pltpu.VMEM((span, width), BF16),
            pltpu.SemaphoreType.DMA((3 + 2 * span // TILE,)),
        ],
        input_output_aliases={3: 0} if given else {},
        compiler_params=pltpu.CompilerParams(vmem_limit_bytes=40 * 1024 * 1024),
        cost_estimate=LITTLE,
    )(keep, first, second, *given)


def place_body(core, mine, theirs, out, sems):
    half = mine.shape[0]
    low = pl.multiple_of(core[0] * half, half)
    high = pl.multiple_of((1 - core[0]) * half, half)
    copies = [
        pltpu.make_async_copy(mine, out.at[0, pl.ds(low, half), :], sems.at[0]),
        pltpu.make_async_copy(theirs, out.at[0, pl.ds(high, half), :], sems.at[1]),
    ]
    for copy in copies:
        copy.start()
    for copy in copies:
        copy.wait()


def place(core, mine, theirs):
    half, depth = mine.shape
    return pl.pallas_call(
        place_body,
        in_specs=[SCALARS, WHOLE, WHOLE],
        out_specs=pl.BlockSpec(memory_space=pl.ANY),
        out_shape=bf16(1, 2 * half, depth),
        scratch_shapes=[pltpu.SemaphoreType.DMA((2,))],
        compiler_params=pltpu.CompilerParams(vmem_limit_bytes=4 * 1024 * 1024),
        cost_estimate=LITTLE,
    )(core[None], mine, theirs)


def load_body(*refs):
    count = len(refs) // 2
    sems = refs[-1]
    copies = [
        pltpu.make_async_copy(refs[i], refs[count + i], sems.at[i]) for i in range(count)
    ]
    for copy in copies:
        copy.start()
    for copy in copies:
        copy.wait()


def load(*arrays):
    return pl.pallas_call(
        load_body,
        in_specs=[pl.BlockSpec(memory_space=pl.ANY)] * len(arrays),
        out_specs=[WHOLE] * len(arrays),
        out_shape=[bf16(*array.shape) for array in arrays],
        scratch_shapes=[pltpu.SemaphoreType.DMA((len(arrays),))],
        compiler_params=pltpu.CompilerParams(vmem_limit_bytes=4 * 1024 * 1024),
        cost_estimate=LITTLE,
    )(*arrays)


def encoder_body(low, left, kg, vg, w, *refs):
    outs = refs[-1:] if len(refs) == 1 else refs[-2:]
    rows = slice(low, low + kg.shape[0] // 2)
    half = outs[0].shape[0]
    for i in range(outs[0].shape[1] // TILE):
        cols = slice(i * TILE, (i + 1) * TILE)
        from_w = slice(left + i * TILE, left + (i + 1) * TILE)
        total = lax.dot_general(kg[rows, :], w[0, 0, from_w, :], NT, preferred_element_type=F32)
        total = total + lax.dot_general(
            vg[rows, :], w[0, 1, from_w, :], NT, preferred_element_type=F32
        )
        if len(refs) > 1:
            total = total + refs[0][:, cols].astype(F32)
        for j, out in enumerate(outs):
            out[:, cols] = total[j * half : (j + 1) * half].astype(BF16)


def encoder_part(key_grad, value_grad, kv_weight, side, columns, moved=None, after=()):
    rows, depth = key_grad.shape[0] // 2, kv_weight.shape[2] // 2
    return call(
        functools.partial(encoder_body, side * rows, columns * depth),
        [key_grad, value_grad, kv_weight] + ([] if moved is None else [moved]),
        bf16(rows, depth) if moved is None else [bf16(rows // 2, depth)] * 2,
        after=after,
        room=12,
    )


def tie(array, *others):
    return lax.optimization_barrier((array, *others))[0]


def on_device(encoded, kv_weight, queries, cotangent):
    core = lax.axis_index("tensor") % 2
    y = lax.axis_index("dp")
    block = encoded[0]
    half = block.shape[0] // 2

    h = {"o": lax.dynamic_slice_in_dim(block, core * half, half, 0)}
    h_too = {"o": lax.dynamic_slice_in_dim(block, (1 - core) * half, half, 0)}
    g, g_too = {}, {}
    h["a"] = send(h["o"], X_FIRST)
    h["b"] = send(h["o"], X_SECOND)
    g["o"] = send(h["o"], ALONG_Z)
    kv_weight, queries, cotangent = load(kv_weight, queries, cotangent)
    g["a"] = send(tie(h["a"], kv_weight, queries), ALONG_Z)
    h["d"] = send(h["a"], X_SECOND)
    g["b"] = send(h["b"], ALONG_Z)
    h_too["a"] = send(h["a"], SWAP)
    h_too["b"] = send(h["b"], SWAP)
    g_too["o"] = send(g["o"], SWAP)
    done = [
        project((h["o"], h_too["o"], h["a"], h_too["a"]), kv_weight),
        project((g["o"], g_too["o"], h["b"], h_too["b"]), kv_weight),
    ]
    g["d"] = send(tie(g["a"], done[0][0], done[1][0]), X_SECOND)
    h_too["d"] = send(h["d"], SWAP)
    g_too["a"] = send(g["a"], SWAP)
    g_too["b"] = send(g["b"], SWAP)
    done.append(project((g["a"], g_too["a"], h["d"], h_too["d"]), kv_weight))
    g_too["d"] = send(tie(g["d"], done[2][0]), SWAP)
    done.append(project((g["b"], g_too["b"], g["d"], g_too["d"]), kv_weight))
    keys, values = zip(*done)
    order = ["ho", "go", "hb", "gb", "ha", "ga", "hd", "gd"]
    pieces = [{"h": h, "g": g}[name[0]][name[1]] for name in order]
    pieces += [{"h": h_too, "g": g_too}[name[0]][name[1]] for name in order]

    attended, query_grad, key_grad, value_grad, key_grad_t, value_grad_t = attend(
        queries, cotangent, keys, values
    )

    one, other = y ^ 1, 3 - y
    first = jnp.where(core == 0, one, other)
    second = jnp.where(core == 0, other, one)
    across = (y + 2) % 4

    def starts(*places):
        return jnp.stack([2 * TILE * place + low for place in places for low in (0, TILE)])

    go = starts(first, across).astype(jnp.int32)
    stay = starts(second, y).astype(jnp.int32)

    grads = (key_grad, value_grad, kv_weight)
    moved = [encoder_part(*grads, 1, i) for i in range(2)]
    value_out = weight_part(go, value_grad_t, pieces, moved)
    moved = [send(part, SWAP) for part in moved]
    early = (value_out,)
    kept, x_out = zip(*[encoder_part(*grads, 0, i, moved[i], early) for i in range(2)])
    key_out = weight_part(go, key_grad_t, pieces, x_out)
    value_keep = weight_part(stay, value_grad_t, pieces, (key_out,))
    key_keep = weight_part(stay, key_grad_t, pieces, (value_keep,))

    def onward(keep, moved):
        span = keep.shape[1] // 2
        return (keep[:, :span].astype(F32) + moved[:, span:].astype(F32)).astype(BF16)

    value_in = send(value_out, Y_FIRST)
    key_in = send(tie(key_out, value_in), Y_FIRST)
    value_two = send(tie(onward(value_keep, value_in), key_in), Y_SECOND)
    key_two = send(tie(onward(key_keep, key_in), value_two), Y_SECOND)

    last = []
    for keep, out in zip(kept, x_out):
        came = send(out, X_FIRST)
        total = tie(keep, key_keep).astype(F32) + came.astype(F32)
        came = send(total[2 * half :].astype(BF16), X_SECOND)
        total = total[: 2 * half] + came.astype(F32)
        here = total[:half] + send(total[half:].astype(BF16), BACK_Z).astype(F32)
        here = here.astype(BF16)
        came = send(here, ACROSS_Z)
        last.append((tie(here, key_in).astype(F32) + came.astype(F32)).astype(BF16))
    last = jnp.concatenate(last, 1)
    enc_grad = place(core, last, send(last, SWAP))

    weight_grad = share(1, value_keep, value_in, value_two)
    weight_grad = share(0, key_keep, key_in, key_two, weight_grad)
    return (attended, query_grad, enc_grad, weight_grad)


def solution(mesh):
    return jax.shard_map(
        on_device,
        mesh=mesh,
        in_specs=(
            P("dp", "pipe", None),
            P("pipe", None, None, "tensor"),
            P("dp", "pipe", None, "tensor"),
            P("dp", "pipe", None, "tensor"),
        ),
        out_specs=(
            P("dp", "pipe", None, "tensor"),
            P("dp", "pipe", None, "tensor"),
            P("dp", "pipe", None),
            P("pipe", None, "dp", "tensor"),
        ),
        check_vma=False,
    )
```

```python
import functools

import jax
import jax.numpy as jnp
from jax import lax
from jax.experimental import pallas as pl
from jax.experimental.pallas import tpu as pltpu
from jax.sharding import PartitionSpec as P

HEAD_DIM = 256
ALL = ("pipe", "tensor", "dp")
F32, BF16 = jnp.float32, jnp.bfloat16
NT = (((1,), (1,)), ((), ()))
TN = (((0,), (0,)), ((), ()))
TILE = 512
WHOLE = pl.BlockSpec(memory_space=pltpu.VMEM)
ANY = pl.BlockSpec(memory_space=pl.ANY)
LARGE = pltpu.CompilerParams(vmem_limit_bytes=46 * 1024 * 1024)
SCALARS = pl.BlockSpec(memory_space=pltpu.SMEM)


LITTLE = pl.CostEstimate(flops=1000, bytes_accessed=1000, transcendentals=0)


def call(body, operands, shapes, scratch=(), index=0, after=(), room=8):
    many = isinstance(shapes, (list, tuple))
    count = len(operands)
    operands = [*operands, *after]

    def reads(*refs):
        body(*refs[:count], *refs[count + len(after) :])

    return pl.pallas_call(
        reads,
        in_specs=[SCALARS] * index
        + [WHOLE] * (count - index)
        + [pl.BlockSpec(memory_space=pl.ANY)] * len(after),
        out_specs=[WHOLE] * len(shapes) if many else WHOLE,
        out_shape=shapes,
        scratch_shapes=scratch,
        compiler_params=pltpu.CompilerParams(vmem_limit_bytes=room * 1024 * 1024),
        cost_estimate=LITTLE,
    )(*operands)


def bf16(*shape):
    return jax.ShapeDtypeStruct(shape, BF16)


def pairs(move):
    def index(x, y, z, core):
        pipe = (z % 2) * 4 + x
        tensor = (z // 2) * 2 + core
        return (pipe * 4 + tensor) * 4 + y

    found = []
    for x in range(4):
        for y in range(4):
            for z in range(4):
                for core in range(2):
                    to_x, to_y, to_z, to_core = move(x, y, z, core)
                    found.append((index(x, y, z, core), index(to_x, to_y, to_z % 4, to_core)))
    return found


def partner(place, core, which):
    return place ^ 1 if core == which else 3 - place


X_FIRST = pairs(lambda x, y, z, core: (partner(x, core, 0), y, z, core))
X_SECOND = pairs(lambda x, y, z, core: (partner(x, core, 1), y, z, core))
Y_FIRST = pairs(lambda x, y, z, core: (x, partner(y, core, 0), z, core))
Y_SECOND = pairs(lambda x, y, z, core: (x, partner(y, core, 1), z, core))
ALONG_Z = pairs(lambda x, y, z, core: (x, y, z + 1 - 2 * core, core))
BACK_Z = pairs(lambda x, y, z, core: (x, y, z - 1 + 2 * core, core))
ACROSS_Z = pairs(lambda x, y, z, core: (x, y, z + 2, core))
SWAP = pairs(lambda x, y, z, core: (x, y, z, 1 - core))


def send(array, route):
    return lax.ppermute(array, ALL, route)


def project_body(a, b, c, d, w, keys, values, x, w_in, acc, sems):
    depth = x.shape[1] // 4
    copies = []
    for i in range(4):
        span = slice(i * depth, (i + 1) * depth)
        copies.append(
            pltpu.make_async_copy(w.at[0, :, span, :], w_in.at[:, span, :], sems.at[i])
        )
        copies[-1].start()
    x[...] = jnp.concatenate([a[...], b[...], c[...], d[...]], 0)
    for i in range(4):
        span = slice(i * depth, (i + 1) * depth)
        copies[i].wait()
        for part, out in enumerate((keys, values)):
            dot = jnp.dot(x[:, span], w_in[part, span, :], preferred_element_type=F32)
            if i > 0:
                dot = dot + acc[part]
            if i < 3:
                acc[part] = dot
            else:
                out[...] = dot.astype(BF16)


def project(pieces, kv_weight):
    _, _, depth, width = kv_weight.shape
    rows = 4 * pieces[0].shape[0]
    return pl.pallas_call(
        project_body,
        in_specs=[WHOLE] * 4 + [ANY],
        out_specs=[WHOLE] * 2,
        out_shape=[bf16(rows, width)] * 2,
        scratch_shapes=[
            pltpu.VMEM((rows, depth), BF16),
            pltpu.VMEM((2, depth, width), BF16),
            pltpu.VMEM((2, rows, width), F32),
            pltpu.SemaphoreType.DMA((4,)),
        ],
        compiler_params=LARGE,
        cost_estimate=LITTLE,
    )(*pieces, kv_weight)


def arrange(groups):
    quarter = groups[0].shape[0] // 4

    def at(group, place):
        return groups[group][place * quarter : (place + 1) * quarter, :]

    order = [(0, 0), (1, 0), (1, 2), (3, 0), (0, 2), (2, 0), (2, 2), (3, 2)]
    return jnp.concatenate(
        [at(g, p) for g, p in order] + [at(g, p + 1) for g, p in order], 0
    )


def attend_body(q, g, k0, k1, k2, k3, v0, v1, v2, v3, att, dq, kg, vg, kgt, vgt, low, dlow):
    scale = HEAD_DIM ** (-0.5)
    total = q.shape[2]
    chunk = total // 2
    for head in range(q.shape[3] // HEAD_DIM):
        cols = slice(head * HEAD_DIM, (head + 1) * HEAD_DIM)
        k = arrange([ref[:, cols] for ref in (k0, k1, k2, k3)])
        v = arrange([ref[:, cols] for ref in (v0, v1, v2, v3)])
        for part in range(2):
            rows = slice(part * chunk, (part + 1) * chunk)
            g_rows = g[0, 0, rows, cols]
            scores = scale * lax.dot_general(
                q[0, 0, rows, cols], k, NT, preferred_element_type=F32
            )
            expd = jnp.exp(scores - jnp.max(scores, axis=-1, keepdims=True))
            probs = expd * (1.0 / jnp.sum(expd, axis=-1, keepdims=True))
            probs_low = probs.astype(BF16)
            low[head, rows, :] = probs_low
            out = jnp.dot(probs_low, v, preferred_element_type=F32).astype(BF16)
            att[0, 0, rows, cols] = out
            dprobs = lax.dot_general(g_rows, v, NT, preferred_element_type=F32)
            delta = jnp.sum(g_rows.astype(F32) * out.astype(F32), axis=-1, keepdims=True)
            ds_low = (probs * (dprobs - delta)).astype(BF16)
            dlow[head, rows, :] = ds_low
            dq[0, 0, rows, cols] = (
                scale * jnp.dot(ds_low, k, preferred_element_type=F32)
            ).astype(BF16)
        value_t = lax.dot_general(g[0, 0, :, cols], low[head], TN, preferred_element_type=F32)
        vgt[cols, :] = value_t.astype(BF16)
        vg[:, cols] = value_t.T.astype(BF16)
        key_t = scale * lax.dot_general(
            q[0, 0, :, cols], dlow[head], TN, preferred_element_type=F32
        )
        kgt[cols, :] = key_t.astype(BF16)
        kg[:, cols] = key_t.T.astype(BF16)


def attend(queries, cotangent, keys, values):
    _, _, total, width = queries.shape
    span = 4 * keys[0].shape[0]
    same = bf16(*queries.shape)
    return call(
        attend_body,
        [queries, cotangent, *keys, *values],
        [same, same, bf16(span, width), bf16(span, width), bf16(width, span), bf16(width, span)],
        [pltpu.VMEM((width // HEAD_DIM, total, span), BF16)] * 2,
        room=16,
    )


def weight_body(count, after, index, grad_t, *refs):
    pieces, (out_any, outs, sems) = refs[:count], refs[count + after :]
    going = []
    for i in range(index.shape[0]):
        start = pl.multiple_of(index[i], TILE)
        cols = slice(i * TILE, (i + 1) * TILE)
        rows = jnp.concatenate([piece[:, pl.ds(start, TILE)] for piece in pieces], 0)
        outs[:, cols] = jnp.dot(grad_t[...], rows, preferred_element_type=F32).astype(BF16)
        going.append(pltpu.make_async_copy(outs.at[:, cols], out_any.at[:, cols], sems.at[i]))
        going[-1].start()
    for copy in going:
        copy.wait()


def weight_part(index, grad_t, pieces, after=()):
    width, steps = grad_t.shape[0], index.shape[0]
    return pl.pallas_call(
        functools.partial(weight_body, len(pieces), len(after)),
        in_specs=[SCALARS] + [WHOLE] * (1 + len(pieces)) + [ANY] * len(after),
        out_specs=ANY,
        out_shape=bf16(width, steps * TILE),
        scratch_shapes=[
            pltpu.VMEM((width, steps * TILE), BF16),
            pltpu.SemaphoreType.DMA((steps,)),
        ],
        compiler_params=pltpu.CompilerParams(vmem_limit_bytes=10 * 1024 * 1024),
        cost_estimate=LITTLE,
    )(index, grad_t, *pieces, *after)


def share_body(part, keep, first, second, *refs):
    out, terms, turned, sems = refs[-4:]
    span = second.shape[1]
    step = TILE // 2
    sources = (keep.at[:, span:], first.at[:, :span], second)
    coming = [
        pltpu.make_async_copy(source, terms.at[i], sems.at[i])
        for i, source in enumerate(sources)
    ]
    for copy in coming:
        copy.start()
    for copy in coming:
        copy.wait()
    going = []
    for i in range(span // step):
        cols = slice(i * step, (i + 1) * step)
        total = terms[0, :, cols].astype(F32) + terms[1, :, cols].astype(F32)
        total = total + terms[2, :, cols].astype(F32)
        turned[cols, :] = total.T.astype(BF16)
        going.append(
            pltpu.make_async_copy(turned.at[cols, :], out.at[0, part, cols, :], sems.at[3 + i])
        )
        going[-1].start()
    for copy in going:
        copy.wait()


def share(part, keep, first, second, into=None):
    width, span = second.shape
    given = [] if into is None else [into]
    return pl.pallas_call(
        functools.partial(share_body, part),
        in_specs=[pl.BlockSpec(memory_space=pl.ANY)] * (3 + len(given)),
        out_specs=pl.BlockSpec(memory_space=pl.ANY),
        out_shape=bf16(1, 2, span, width),
        scratch_shapes=[
            pltpu.VMEM((3, width, span), BF16),
            pltpu.VMEM((span, width), BF16),
            pltpu.SemaphoreType.DMA((3 + 2 * span // TILE,)),
        ],
        input_output_aliases={3: 0} if given else {},
        compiler_params=pltpu.CompilerParams(vmem_limit_bytes=40 * 1024 * 1024),
        cost_estimate=LITTLE,
    )(keep, first, second, *given)


def place_body(core, mine, theirs, out, sems):
    half = mine.shape[0]
    low = pl.multiple_of(core[0] * half, half)
    high = pl.multiple_of((1 - core[0]) * half, half)
    copies = [
        pltpu.make_async_copy(mine, out.at[0, pl.ds(low, half), :], sems.at[0]),
        pltpu.make_async_copy(theirs, out.at[0, pl.ds(high, half), :], sems.at[1]),
    ]
    for copy in copies:
        copy.start()
    for copy in copies:
        copy.wait()


def place(core, mine, theirs):
    half, depth = mine.shape
    return pl.pallas_call(
        place_body,
        in_specs=[SCALARS, WHOLE, WHOLE],
        out_specs=pl.BlockSpec(memory_space=pl.ANY),
        out_shape=bf16(1, 2 * half, depth),
        scratch_shapes=[pltpu.SemaphoreType.DMA((2,))],
        compiler_params=pltpu.CompilerParams(vmem_limit_bytes=4 * 1024 * 1024),
        cost_estimate=LITTLE,
    )(core[None], mine, theirs)


def encoder_body(low, left, after, kg, vg, w, *refs):
    refs, (w_in, out, came, sems) = refs[:-4], refs[-4:]
    moved, outs = (refs[:1], refs[-2:]) if len(refs) > 1 + after else ((), refs[-1:])
    rows = slice(low, low + out.shape[0])
    half = outs[0].shape[0]
    steps = out.shape[1] // TILE
    used = iter(range(sems.shape[0]))

    def start(source, target):
        copy = pltpu.make_async_copy(source, target, sems.at[next(used)])
        copy.start()
        return copy

    coming, going = [], []
    for i in range(steps):
        cols = slice(i * TILE, (i + 1) * TILE)
        from_w = slice(left + i * TILE, left + (i + 1) * TILE)
        coming.append([start(w.at[0, :, from_w, :], w_in.at[:, cols, :])])
        if moved:
            coming[-1].append(start(moved[0].at[:, cols], came.at[:, cols]))
    for i in range(steps):
        cols = slice(i * TILE, (i + 1) * TILE)
        for copy in coming[i]:
            copy.wait()
        total = lax.dot_general(kg[rows, :], w_in[0, cols, :], NT, preferred_element_type=F32)
        total = total + lax.dot_general(
            vg[rows, :], w_in[1, cols, :], NT, preferred_element_type=F32
        )
        if moved:
            total = total + came[:, cols].astype(F32)
        out[:, cols] = total.astype(BF16)
        for j, target in enumerate(outs):
            going.append(start(out.at[j * half : (j + 1) * half, cols], target.at[:, cols]))
    for copy in going:
        copy.wait()


def encoder_part(key_grad, value_grad, kv_weight, side, columns, moved=None, after=()):
    span, width = key_grad.shape
    rows, depth = span // 2, kv_weight.shape[2] // 2
    steps = depth // TILE
    given = [] if moved is None else [moved]
    return pl.pallas_call(
        functools.partial(encoder_body, side * rows, columns * depth, len(after)),
        in_specs=[WHOLE, WHOLE] + [ANY] * (1 + len(given) + len(after)),
        out_specs=ANY if moved is None else [ANY, ANY],
        out_shape=bf16(rows, depth) if moved is None else [bf16(rows // 2, depth)] * 2,
        scratch_shapes=[
            pltpu.VMEM((2, depth, width), BF16),
            pltpu.VMEM((rows, depth), BF16),
            pltpu.VMEM((rows, depth), BF16),
            pltpu.SemaphoreType.DMA((4 * steps,)),
        ],
        compiler_params=LARGE,
        cost_estimate=LITTLE,
    )(key_grad, value_grad, kv_weight, *given, *after)


def tie(array, *others):
    return lax.optimization_barrier((array, *others))[0]


def on_device(encoded, kv_weight, queries, cotangent):
    core = lax.axis_index("tensor") % 2
    y = lax.axis_index("dp")
    block = encoded[0]
    half = block.shape[0] // 2

    h = {"o": lax.dynamic_slice_in_dim(block, core * half, half, 0)}
    h_too = {"o": lax.dynamic_slice_in_dim(block, (1 - core) * half, half, 0)}
    g, g_too = {}, {}
    h["a"] = send(h["o"], X_FIRST)
    h["b"] = send(h["o"], X_SECOND)
    g["o"] = send(h["o"], ALONG_Z)
    g["a"] = send(h["a"], ALONG_Z)
    h["d"] = send(h["a"], X_SECOND)
    g["b"] = send(h["b"], ALONG_Z)
    h_too["a"] = send(h["a"], SWAP)
    h_too["b"] = send(h["b"], SWAP)
    g_too["o"] = send(g["o"], SWAP)
    done = [
        project((h["o"], h_too["o"], h["a"], h_too["a"]), kv_weight),
        project((g["o"], g_too["o"], h["b"], h_too["b"]), kv_weight),
    ]
    g["d"] = send(tie(g["a"], done[0][0], done[1][0]), X_SECOND)
    h_too["d"] = send(h["d"], SWAP)
    g_too["a"] = send(g["a"], SWAP)
    g_too["b"] = send(g["b"], SWAP)
    done.append(project((g["a"], g_too["a"], h["d"], h_too["d"]), kv_weight))
    g_too["d"] = send(tie(g["d"], done[2][0]), SWAP)
    done.append(project((g["b"], g_too["b"], g["d"], g_too["d"]), kv_weight))
    keys, values = zip(*done)
    order = ["ho", "go", "hb", "gb", "ha", "ga", "hd", "gd"]
    pieces = [{"h": h, "g": g}[name[0]][name[1]] for name in order]
    pieces += [{"h": h_too, "g": g_too}[name[0]][name[1]] for name in order]

    attended, query_grad, key_grad, value_grad, key_grad_t, value_grad_t = attend(
        queries, cotangent, keys, values
    )

    one, other = y ^ 1, 3 - y
    first = jnp.where(core == 0, one, other)
    second = jnp.where(core == 0, other, one)
    across = (y + 2) % 4

    def starts(*places):
        return jnp.stack([2 * TILE * place + low for place in places for low in (0, TILE)])

    go = starts(first, across).astype(jnp.int32)
    stay = starts(second, y).astype(jnp.int32)

    grads = (key_grad, value_grad, kv_weight)
    moved = [encoder_part(*grads, 1, i) for i in range(2)]
    value_out = weight_part(go, value_grad_t, pieces, moved)
    moved = [send(part, SWAP) for part in moved]
    early = (value_out,)
    kept, x_out = zip(*[encoder_part(*grads, 0, i, moved[i], early) for i in range(2)])
    key_out = weight_part(go, key_grad_t, pieces, x_out)
    value_keep = weight_part(stay, value_grad_t, pieces, (key_out,))
    key_keep = weight_part(stay, key_grad_t, pieces, (value_keep,))

    def onward(keep, moved):
        span = keep.shape[1] // 2
        return (keep[:, :span].astype(F32) + moved[:, span:].astype(F32)).astype(BF16)

    value_in = send(value_out, Y_FIRST)
    key_in = send(tie(key_out, value_in), Y_FIRST)
    value_two = send(tie(onward(value_keep, value_in), key_in), Y_SECOND)
    key_two = send(tie(onward(key_keep, key_in), value_two), Y_SECOND)

    last = []
    for keep, out in zip(kept, x_out):
        came = send(out, X_FIRST)
        total = tie(keep, key_keep).astype(F32) + came.astype(F32)
        came = send(total[2 * half :].astype(BF16), X_SECOND)
        total = total[: 2 * half] + came.astype(F32)
        here = total[:half] + send(total[half:].astype(BF16), BACK_Z).astype(F32)
        here = here.astype(BF16)
        came = send(here, ACROSS_Z)
        last.append((tie(here, key_in).astype(F32) + came.astype(F32)).astype(BF16))
    last = jnp.concatenate(last, 1)
    enc_grad = place(core, last, send(last, SWAP))

    weight_grad = share(1, value_keep, value_in, value_two)
    weight_grad = share(0, key_keep, key_in, key_two, weight_grad)
    return (attended, query_grad, enc_grad, weight_grad)


def solution(mesh):
    return jax.shard_map(
        on_device,
        mesh=mesh,
        in_specs=(
            P("dp", "pipe", None),
            P("pipe", None, None, "tensor"),
            P("dp", "pipe", None, "tensor"),
            P("dp", "pipe", None, "tensor"),
        ),
        out_specs=(
            P("dp", "pipe", None, "tensor"),
            P("dp", "pipe", None, "tensor"),
            P("dp", "pipe", None),
            P("pipe", None, "dp", "tensor"),
        ),
        check_vma=False,
    )
```

```python
import functools

import jax
import jax.numpy as jnp
from jax import lax
from jax.experimental import pallas as pl
from jax.experimental.pallas import tpu as pltpu
from jax.sharding import PartitionSpec as P

HEAD_DIM = 256
ALL = ("pipe", "tensor", "dp")
F32, BF16 = jnp.float32, jnp.bfloat16
NT = (((1,), (1,)), ((), ()))
TN = (((0,), (0,)), ((), ()))
TILE = 512
WHOLE = pl.BlockSpec(memory_space=pltpu.VMEM)
ANY = pl.BlockSpec(memory_space=pl.ANY)
LARGE = pltpu.CompilerParams(vmem_limit_bytes=50 * 1024 * 1024)
SCALARS = pl.BlockSpec(memory_space=pltpu.SMEM)


LITTLE = pl.CostEstimate(flops=1000, bytes_accessed=1000, transcendentals=0)


def call(body, operands, shapes, scratch=(), index=0, after=(), room=8):
    many = isinstance(shapes, (list, tuple))
    count = len(operands)
    operands = [*operands, *after]

    def reads(*refs):
        body(*refs[:count], *refs[count + len(after) :])

    return pl.pallas_call(
        reads,
        in_specs=[SCALARS] * index
        + [WHOLE] * (count - index)
        + [pl.BlockSpec(memory_space=pl.ANY)] * len(after),
        out_specs=[WHOLE] * len(shapes) if many else WHOLE,
        out_shape=shapes,
        scratch_shapes=scratch,
        compiler_params=pltpu.CompilerParams(vmem_limit_bytes=room * 1024 * 1024),
        cost_estimate=LITTLE,
    )(*operands)


def bf16(*shape):
    return jax.ShapeDtypeStruct(shape, BF16)


def pairs(move):
    def index(x, y, z, core):
        pipe = (z % 2) * 4 + x
        tensor = (z // 2) * 2 + core
        return (pipe * 4 + tensor) * 4 + y

    found = []
    for x in range(4):
        for y in range(4):
            for z in range(4):
                for core in range(2):
                    to_x, to_y, to_z, to_core = move(x, y, z, core)
                    found.append((index(x, y, z, core), index(to_x, to_y, to_z % 4, to_core)))
    return found


def partner(place, core, which):
    return place ^ 1 if core == which else 3 - place


X_FIRST = pairs(lambda x, y, z, core: (partner(x, core, 0), y, z, core))
X_SECOND = pairs(lambda x, y, z, core: (partner(x, core, 1), y, z, core))
Y_FIRST = pairs(lambda x, y, z, core: (x, partner(y, core, 0), z, core))
Y_SECOND = pairs(lambda x, y, z, core: (x, partner(y, core, 1), z, core))
ALONG_Z = pairs(lambda x, y, z, core: (x, y, z + 1 - 2 * core, core))
BACK_Z = pairs(lambda x, y, z, core: (x, y, z - 1 + 2 * core, core))
ACROSS_Z = pairs(lambda x, y, z, core: (x, y, z + 2, core))
SWAP = pairs(lambda x, y, z, core: (x, y, z, 1 - core))


def send(array, route):
    return lax.ppermute(array, ALL, route)


def project_body(a, b, c, d, w, keys, values, x, w_in, acc, sems):
    depth = x.shape[1] // 4
    copies = []
    for i in range(4):
        span = slice(i * depth, (i + 1) * depth)
        copies.append(
            pltpu.make_async_copy(w.at[0, :, span, :], w_in.at[:, span, :], sems.at[i])
        )
        copies[-1].start()
    x[...] = jnp.concatenate([a[...], b[...], c[...], d[...]], 0)
    for i in range(4):
        span = slice(i * depth, (i + 1) * depth)
        copies[i].wait()
        for part, out in enumerate((keys, values)):
            dot = jnp.dot(x[:, span], w_in[part, span, :], preferred_element_type=F32)
            if i > 0:
                dot = dot + acc[part]
            if i < 3:
                acc[part] = dot
            else:
                out[...] = dot.astype(BF16)


def project(pieces, kv_weight):
    _, _, depth, width = kv_weight.shape
    rows = 4 * pieces[0].shape[0]
    return pl.pallas_call(
        project_body,
        in_specs=[WHOLE] * 4 + [ANY],
        out_specs=[WHOLE] * 2,
        out_shape=[bf16(rows, width)] * 2,
        scratch_shapes=[
            pltpu.VMEM((rows, depth), BF16),
            pltpu.VMEM((2, depth, width), BF16),
            pltpu.VMEM((2, rows, width), F32),
            pltpu.SemaphoreType.DMA((4,)),
        ],
        compiler_params=LARGE,
        cost_estimate=LITTLE,
    )(*pieces, kv_weight)


def arrange(groups):
    quarter = groups[0].shape[0] // 4

    def at(group, place):
        return groups[group][place * quarter : (place + 1) * quarter, :]

    order = [(0, 0), (1, 0), (1, 2), (3, 0), (0, 2), (2, 0), (2, 2), (3, 2)]
    return jnp.concatenate(
        [at(g, p) for g, p in order] + [at(g, p + 1) for g, p in order], 0
    )


def attend_body(q, g, k0, k1, k2, k3, v0, v1, v2, v3, *refs):
    att_any, dq_any, kg_any, vg_any, kgt_any, vgt_any = refs[:6]
    att, dq, kg, vg, kgt, vgt, low, dlow, sems = refs[6:]
    going = []

    def out(source, target):
        copy = pltpu.make_async_copy(source, target, sems.at[len(going)])
        copy.start()
        going.append(copy)

    scale = HEAD_DIM ** (-0.5)
    total = q.shape[2]
    chunk = total // 2
    for head in range(q.shape[3] // HEAD_DIM):
        cols = slice(head * HEAD_DIM, (head + 1) * HEAD_DIM)
        k = arrange([ref[:, cols] for ref in (k0, k1, k2, k3)])
        v = arrange([ref[:, cols] for ref in (v0, v1, v2, v3)])
        for part in range(2):
            rows = slice(part * chunk, (part + 1) * chunk)
            g_rows = g[0, 0, rows, cols]
            scores = scale * lax.dot_general(
                q[0, 0, rows, cols], k, NT, preferred_element_type=F32
            )
            expd = jnp.exp(scores - jnp.max(scores, axis=-1, keepdims=True))
            probs = expd * (1.0 / jnp.sum(expd, axis=-1, keepdims=True))
            probs_low = probs.astype(BF16)
            low[head, rows, :] = probs_low
            rows_out = jnp.dot(probs_low, v, preferred_element_type=F32).astype(BF16)
            att[0, 0, rows, cols] = rows_out
            dprobs = lax.dot_general(g_rows, v, NT, preferred_element_type=F32)
            delta = jnp.sum(g_rows.astype(F32) * rows_out.astype(F32), axis=-1, keepdims=True)
            ds_low = (probs * (dprobs - delta)).astype(BF16)
            dlow[head, rows, :] = ds_low
            dq[0, 0, rows, cols] = (
                scale * jnp.dot(ds_low, k, preferred_element_type=F32)
            ).astype(BF16)
        value_t = lax.dot_general(g[0, 0, :, cols], low[head], TN, preferred_element_type=F32)
        vgt[cols, :] = value_t.astype(BF16)
        out(vgt.at[cols, :], vgt_any.at[cols, :])
        vg[:, cols] = value_t.T.astype(BF16)
        out(vg.at[:, cols], vg_any.at[:, cols])
        out(att.at[:, :, :, cols], att_any.at[:, :, :, cols])
        key_t = scale * lax.dot_general(
            q[0, 0, :, cols], dlow[head], TN, preferred_element_type=F32
        )
        kgt[cols, :] = key_t.astype(BF16)
        out(kgt.at[cols, :], kgt_any.at[cols, :])
        kg[:, cols] = key_t.T.astype(BF16)
        out(kg.at[:, cols], kg_any.at[:, cols])
        out(dq.at[:, :, :, cols], dq_any.at[:, :, :, cols])
    for copy in going:
        copy.wait()


def attend(queries, cotangent, keys, values):
    _, _, total, width = queries.shape
    span, heads = 4 * keys[0].shape[0], width // HEAD_DIM
    shapes = [queries.shape] * 2 + [(span, width)] * 2 + [(width, span)] * 2
    return pl.pallas_call(
        attend_body,
        in_specs=[WHOLE] * 10,
        out_specs=[ANY] * 6,
        out_shape=[bf16(*shape) for shape in shapes],
        scratch_shapes=[pltpu.VMEM(shape, BF16) for shape in shapes]
        + [pltpu.VMEM((heads, total, span), BF16)] * 2
        + [pltpu.SemaphoreType.DMA((6 * heads,))],
        compiler_params=pltpu.CompilerParams(vmem_limit_bytes=24 * 1024 * 1024),
        cost_estimate=LITTLE,
    )(queries, cotangent, *keys, *values)


def weight_body(count, index, grad_any, *refs):
    pieces, (*outs_any, grad_t, tiles, outs, sems, out_sems) = refs[:count], refs[count:]
    rows = pieces[0].shape[0]
    steps = index.shape[0]

    def fetch(i):
        start = pl.multiple_of(index[i], TILE)
        copies = [
            pltpu.make_async_copy(
                piece.at[:, pl.ds(start, TILE)],
                tiles.at[i % 2, j * rows : (j + 1) * rows, :],
                sems.at[i * count + j],
            )
            for j, piece in enumerate(pieces)
        ]
        for copy in copies:
            copy.start()
        return copies

    grad_copy = pltpu.make_async_copy(grad_any, grad_t, out_sems.at[steps])
    grad_copy.start()
    coming = fetch(0)
    grad_copy.wait()
    going = []
    for i in range(steps):
        after = fetch(i + 1) if i + 1 < steps else []
        for copy in coming:
            copy.wait()
        cols = slice(i * TILE, (i + 1) * TILE)
        outs[:, cols] = jnp.dot(
            grad_t[...], tiles[i % 2], preferred_element_type=F32
        ).astype(BF16)
        going.append(
            pltpu.make_async_copy(
                outs.at[:, cols],
                outs_any[i // 2].at[:, (i % 2) * TILE : (i % 2 + 1) * TILE],
                out_sems.at[i],
            )
        )
        going[-1].start()
        coming = after
    for copy in going:
        copy.wait()


def weight_part(index, grad_t, pieces, after=()):
    width, span = grad_t.shape
    steps, count = index.shape[0], len(pieces)

    def body(*refs):
        weight_body(count, *refs[: 2 + count], *refs[2 + count + len(after) :])

    return pl.pallas_call(
        body,
        in_specs=[SCALARS] + [ANY] * (1 + count + len(after)),
        out_specs=[ANY, ANY],
        out_shape=[bf16(width, steps // 2 * TILE)] * 2,
        scratch_shapes=[
            pltpu.VMEM((width, span), BF16),
            pltpu.VMEM((2, span, TILE), BF16),
            pltpu.VMEM((width, steps * TILE), BF16),
            pltpu.SemaphoreType.DMA((steps * count,)),
            pltpu.SemaphoreType.DMA((steps + 1,)),
        ],
        compiler_params=pltpu.CompilerParams(vmem_limit_bytes=50 * 1024 * 1024),
        cost_estimate=LITTLE,
    )(index, grad_t, *pieces, *after)


def share_body(part, keep, first, second, *refs):
    out, terms, turned, sems = refs[-4:]
    span = second.shape[1]
    step = TILE // 2
    sources = (keep, first, second)
    coming = [
        pltpu.make_async_copy(source, terms.at[i], sems.at[i])
        for i, source in enumerate(sources)
    ]
    for copy in coming:
        copy.start()
    for copy in coming:
        copy.wait()
    going = []
    for i in range(span // step):
        cols = slice(i * step, (i + 1) * step)
        total = terms[0, :, cols].astype(F32) + terms[1, :, cols].astype(F32)
        total = total + terms[2, :, cols].astype(F32)
        turned[cols, :] = total.T.astype(BF16)
        going.append(
            pltpu.make_async_copy(turned.at[cols, :], out.at[0, part, cols, :], sems.at[3 + i])
        )
        going[-1].start()
    for copy in going:
        copy.wait()


def share(part, keep, first, second, into=None):
    width, span = second.shape
    given = [] if into is None else [into]
    return pl.pallas_call(
        functools.partial(share_body, part),
        in_specs=[pl.BlockSpec(memory_space=pl.ANY)] * (3 + len(given)),
        out_specs=pl.BlockSpec(memory_space=pl.ANY),
        out_shape=bf16(1, 2, span, width),
        scratch_shapes=[
            pltpu.VMEM((3, width, span), BF16),
            pltpu.VMEM((span, width), BF16),
            pltpu.SemaphoreType.DMA((3 + 2 * span // TILE,)),
        ],
        input_output_aliases={3: 0} if given else {},
        compiler_params=pltpu.CompilerParams(vmem_limit_bytes=50 * 1024 * 1024),
        cost_estimate=LITTLE,
    )(keep, first, second, *given)


def place_body(core, mine, theirs, out, sems):
    half = mine.shape[0]
    low = pl.multiple_of(core[0] * half, half)
    high = pl.multiple_of((1 - core[0]) * half, half)
    copies = [
        pltpu.make_async_copy(mine, out.at[0, pl.ds(low, half), :], sems.at[0]),
        pltpu.make_async_copy(theirs, out.at[0, pl.ds(high, half), :], sems.at[1]),
    ]
    for copy in copies:
        copy.start()
    for copy in copies:
        copy.wait()


def place(core, mine, theirs):
    half, depth = mine.shape
    return pl.pallas_call(
        place_body,
        in_specs=[SCALARS, WHOLE, WHOLE],
        out_specs=pl.BlockSpec(memory_space=pl.ANY),
        out_shape=bf16(1, 2 * half, depth),
        scratch_shapes=[pltpu.SemaphoreType.DMA((2,))],
        compiler_params=pltpu.CompilerParams(vmem_limit_bytes=4 * 1024 * 1024),
        cost_estimate=LITTLE,
    )(core[None], mine, theirs)


def encoder_body(low, left, after, kg, vg, w, *refs):
    refs, (grads, w_in, out, came, sems) = refs[:-5], refs[-5:]
    moved, outs = (refs[:1], refs[-2:]) if len(refs) > 1 + after else ((), refs[-1:])
    rows = slice(low, low + out.shape[0])
    half = outs[0].shape[0]
    steps = out.shape[1] // TILE
    used = iter(range(sems.shape[0]))

    def start(source, target):
        copy = pltpu.make_async_copy(source, target, sems.at[next(used)])
        copy.start()
        return copy

    coming, going = [], []
    first = [start(ref.at[rows, :], grads.at[i]) for i, ref in enumerate((kg, vg))]
    for i in range(steps):
        cols = slice(i * TILE, (i + 1) * TILE)
        from_w = slice(left + i * TILE, left + (i + 1) * TILE)
        coming.append([start(w.at[0, :, from_w, :], w_in.at[:, cols, :])])
        if moved:
            coming[-1].append(start(moved[0].at[:, cols], came.at[:, cols]))
    for i in range(steps):
        cols = slice(i * TILE, (i + 1) * TILE)
        for copy in first + coming[i]:
            copy.wait()
        first = []
        total = lax.dot_general(grads[0], w_in[0, cols, :], NT, preferred_element_type=F32)
        total = total + lax.dot_general(
            grads[1], w_in[1, cols, :], NT, preferred_element_type=F32
        )
        if moved:
            total = total + came[:, cols].astype(F32)
        out[:, cols] = total.astype(BF16)
        for j, target in enumerate(outs):
            going.append(start(out.at[j * half : (j + 1) * half, cols], target.at[:, cols]))
    for copy in going:
        copy.wait()


def encoder_part(key_grad, value_grad, kv_weight, side, columns, moved=None, after=()):
    span, width = key_grad.shape
    rows, depth = span // 2, kv_weight.shape[2] // 2
    steps = depth // TILE
    given = [] if moved is None else [moved]
    return pl.pallas_call(
        functools.partial(encoder_body, side * rows, columns * depth, len(after)),
        in_specs=[ANY] * (3 + len(given) + len(after)),
        out_specs=ANY if moved is None else [ANY, ANY],
        out_shape=bf16(rows, depth) if moved is None else [bf16(rows // 2, depth)] * 2,
        scratch_shapes=[
            pltpu.VMEM((2, rows, width), BF16),
            pltpu.VMEM((2, depth, width), BF16),
            pltpu.VMEM((rows, depth), BF16),
            pltpu.VMEM((rows, depth), BF16),
            pltpu.SemaphoreType.DMA((2 + 4 * steps,)),
        ],
        compiler_params=LARGE,
        cost_estimate=LITTLE,
    )(key_grad, value_grad, kv_weight, *given, *after)


def tie(array, *others):
    return lax.optimization_barrier((array, *others))[0]


def on_device(encoded, kv_weight, queries, cotangent):
    core = lax.axis_index("tensor") % 2
    y = lax.axis_index("dp")
    block = encoded[0]
    half = block.shape[0] // 2

    h = {"o": lax.dynamic_slice_in_dim(block, core * half, half, 0)}
    h_too = {"o": lax.dynamic_slice_in_dim(block, (1 - core) * half, half, 0)}
    g, g_too = {}, {}
    h["a"] = send(h["o"], X_FIRST)
    h["b"] = send(h["o"], X_SECOND)
    g["o"] = send(h["o"], ALONG_Z)
    g["a"] = send(h["a"], ALONG_Z)
    h["d"] = send(h["a"], X_SECOND)
    g["b"] = send(tie(h["b"], g["a"]), ALONG_Z)
    h_too["a"] = send(h["a"], SWAP)
    h_too["b"] = send(h["b"], SWAP)
    g_too["o"] = send(g["o"], SWAP)
    done = [
        project((h["o"], h_too["o"], h["a"], h_too["a"]), kv_weight),
        project((g["o"], g_too["o"], h["b"], h_too["b"]), kv_weight),
    ]
    g["d"] = send(g["a"], X_SECOND)
    h_too["d"] = send(tie(h["d"], done[0][0]), SWAP)
    g_too["a"] = send(g["a"], SWAP)
    g_too["b"] = send(tie(g["b"], done[1][0]), SWAP)
    done.append(project((g["a"], g_too["a"], h["d"], h_too["d"]), kv_weight))
    g_too["d"] = send(tie(g["d"], done[2][0]), SWAP)
    done.append(project((g["b"], g_too["b"], g["d"], g_too["d"]), kv_weight))
    keys, values = zip(*done)
    order = ["ho", "go", "hb", "gb", "ha", "ga", "hd", "gd"]
    pieces = [{"h": h, "g": g}[name[0]][name[1]] for name in order]
    pieces += [{"h": h_too, "g": g_too}[name[0]][name[1]] for name in order]

    attended, query_grad, key_grad, value_grad, key_grad_t, value_grad_t = attend(
        queries, cotangent, keys, values
    )

    one, other = y ^ 1, 3 - y
    first = jnp.where(core == 0, one, other)
    second = jnp.where(core == 0, other, one)
    across = (y + 2) % 4

    def starts(*places):
        return jnp.stack([2 * TILE * place + low for place in places for low in (0, TILE)])

    go = starts(across, first).astype(jnp.int32)
    stay = starts(second, y).astype(jnp.int32)
    grads = (key_grad, value_grad, kv_weight)

    theirs_first = encoder_part(*grads, 1, 0)
    value_out = weight_part(go, value_grad_t, pieces, (theirs_first,))
    moved_first = send(theirs_first, SWAP)
    value_in = [send(value_out[0], Y_FIRST)]
    kept_first, x_first = encoder_part(*grads, 0, 0, moved_first, value_out)
    key_out = weight_part(go, key_grad_t, pieces, (x_first,))
    early = (value_in[0], *key_out)
    moved_second = send(encoder_part(*grads, 1, 1, None, early), SWAP)
    kept_second, x_second = encoder_part(*grads, 0, 1, moved_second)
    value_keep = weight_part(stay, value_grad_t, pieces, (x_second,))
    key_keep = weight_part(stay, key_grad_t, pieces, value_keep)

    def onward(keep, moved):
        return (keep.astype(F32) + moved.astype(F32)).astype(BF16)

    value_in.append(send(tie(value_out[1], value_in[0]), Y_FIRST))
    key_in = [send(tie(key_out[0], value_in[1]), Y_FIRST)]
    key_in.append(send(tie(key_out[1], key_in[0]), Y_FIRST))
    value_two = send(tie(onward(value_keep[0], value_in[0]), key_in[1]), Y_SECOND)
    key_two = send(tie(onward(key_keep[0], key_in[0]), value_two), Y_SECOND)
    kept = (kept_first, kept_second)

    last = []
    x_came = [send(x_first, X_FIRST)]
    x_came.append(send(tie(x_second, x_came[0]), X_FIRST))
    for keep, came in zip(kept, x_came):
        total = tie(keep, key_keep[0]).astype(F32) + came.astype(F32)
        came = send(total[2 * half :].astype(BF16), X_SECOND)
        total = total[: 2 * half] + came.astype(F32)
        here = total[:half] + send(total[half:].astype(BF16), BACK_Z).astype(F32)
        here = here.astype(BF16)
        came = send(here, ACROSS_Z)
        last.append((tie(here, key_in[1]).astype(F32) + came.astype(F32)).astype(BF16))
    last = jnp.concatenate(last, 1)
    enc_grad = place(core, last, send(last, SWAP))

    weight_grad = share(1, value_keep[1], value_in[1], value_two)
    weight_grad = share(0, key_keep[1], key_in[1], key_two, weight_grad)
    return (attended, query_grad, enc_grad, weight_grad)


def solution(mesh):
    return jax.shard_map(
        on_device,
        mesh=mesh,
        in_specs=(
            P("dp", "pipe", None),
            P("pipe", None, None, "tensor"),
            P("dp", "pipe", None, "tensor"),
            P("dp", "pipe", None, "tensor"),
        ),
        out_specs=(
            P("dp", "pipe", None, "tensor"),
            P("dp", "pipe", None, "tensor"),
            P("dp", "pipe", None),
            P("pipe", None, "dp", "tensor"),
        ),
        check_vma=False,
    )
```

```python
import functools

import jax
import jax.numpy as jnp
from jax import lax
from jax.experimental import pallas as pl
from jax.experimental.pallas import tpu as pltpu
from jax.sharding import PartitionSpec as P

HEAD_DIM = 256
ALL = ("pipe", "tensor", "dp")
F32, BF16 = jnp.float32, jnp.bfloat16
NT = (((1,), (1,)), ((), ()))
TN = (((0,), (0,)), ((), ()))
TILE = 512
WHOLE = pl.BlockSpec(memory_space=pltpu.VMEM)
SCALARS = pl.BlockSpec(memory_space=pltpu.SMEM)


LITTLE = pl.CostEstimate(flops=1000, bytes_accessed=1000, transcendentals=0)


def call(body, operands, shapes, scratch=(), index=0, after=(), room=8):
    many = isinstance(shapes, (list, tuple))
    count = len(operands)
    operands = [*operands, *after]

    def reads(*refs):
        body(*refs[:count], *refs[count + len(after) :])

    return pl.pallas_call(
        reads,
        in_specs=[SCALARS] * index
        + [WHOLE] * (count - index)
        + [pl.BlockSpec(memory_space=pl.ANY)] * len(after),
        out_specs=[WHOLE] * len(shapes) if many else WHOLE,
        out_shape=shapes,
        scratch_shapes=scratch,
        compiler_params=pltpu.CompilerParams(vmem_limit_bytes=room * 1024 * 1024),
        cost_estimate=LITTLE,
    )(*operands)


def bf16(*shape):
    return jax.ShapeDtypeStruct(shape, BF16)


def pairs(move):
    def index(x, y, z, core):
        pipe = (z % 2) * 4 + x
        tensor = (z // 2) * 2 + core
        return (pipe * 4 + tensor) * 4 + y

    found = []
    for x in range(4):
        for y in range(4):
            for z in range(4):
                for core in range(2):
                    to_x, to_y, to_z, to_core = move(x, y, z, core)
                    found.append((index(x, y, z, core), index(to_x, to_y, to_z % 4, to_core)))
    return found


def partner(place, core, which):
    return place ^ 1 if core == which else 3 - place


X_FIRST = pairs(lambda x, y, z, core: (partner(x, core, 0), y, z, core))
X_SECOND = pairs(lambda x, y, z, core: (partner(x, core, 1), y, z, core))
Y_FIRST = pairs(lambda x, y, z, core: (x, partner(y, core, 0), z, core))
Y_SECOND = pairs(lambda x, y, z, core: (x, partner(y, core, 1), z, core))
ALONG_Z = pairs(lambda x, y, z, core: (x, y, z + 1 - 2 * core, core))
BACK_Z = pairs(lambda x, y, z, core: (x, y, z - 1 + 2 * core, core))
ACROSS_Z = pairs(lambda x, y, z, core: (x, y, z + 2, core))
SWAP = pairs(lambda x, y, z, core: (x, y, z, 1 - core))


def send(array, route):
    return lax.ppermute(array, ALL, route)


def project_body(a, b, c, d, w, keys, values):
    x = jnp.concatenate([a[...], b[...], c[...], d[...]], 0)
    keys[...] = jnp.dot(x, w[0, 0], preferred_element_type=F32).astype(BF16)
    values[...] = jnp.dot(x, w[0, 1], preferred_element_type=F32).astype(BF16)


def project(pieces, kv_weight):
    shape = bf16(4 * pieces[0].shape[0], kv_weight.shape[3])
    return call(project_body, [*pieces, kv_weight], [shape, shape])


def arrange(groups):
    quarter = groups[0].shape[0] // 4

    def at(group, place):
        return groups[group][place * quarter : (place + 1) * quarter, :]

    order = [(0, 0), (1, 0), (1, 2), (3, 0), (0, 2), (2, 0), (2, 2), (3, 2)]
    return jnp.concatenate(
        [at(g, p) for g, p in order] + [at(g, p + 1) for g, p in order], 0
    )


def attend_body(q, g, k0, k1, k2, k3, v0, v1, v2, v3, att, dq, kg, vg, kgt, vgt, low, dlow):
    scale = HEAD_DIM ** (-0.5)
    total = q.shape[2]
    chunk = total // 2
    for head in range(q.shape[3] // HEAD_DIM):
        cols = slice(head * HEAD_DIM, (head + 1) * HEAD_DIM)
        k = arrange([ref[:, cols] for ref in (k0, k1, k2, k3)])
        v = arrange([ref[:, cols] for ref in (v0, v1, v2, v3)])
        for part in range(2):
            rows = slice(part * chunk, (part + 1) * chunk)
            g_rows = g[0, 0, rows, cols]
            scores = scale * lax.dot_general(
                q[0, 0, rows, cols], k, NT, preferred_element_type=F32
            )
            expd = jnp.exp(scores - jnp.max(scores, axis=-1, keepdims=True))
            probs = expd * (1.0 / jnp.sum(expd, axis=-1, keepdims=True))
            probs_low = probs.astype(BF16)
            low[head, rows, :] = probs_low
            out = jnp.dot(probs_low, v, preferred_element_type=F32).astype(BF16)
            att[0, 0, rows, cols] = out
            dprobs = lax.dot_general(g_rows, v, NT, preferred_element_type=F32)
            delta = jnp.sum(g_rows.astype(F32) * out.astype(F32), axis=-1, keepdims=True)
            ds_low = (probs * (dprobs - delta)).astype(BF16)
            dlow[head, rows, :] = ds_low
            dq[0, 0, rows, cols] = (
                scale * jnp.dot(ds_low, k, preferred_element_type=F32)
            ).astype(BF16)
        value_t = lax.dot_general(g[0, 0, :, cols], low[head], TN, preferred_element_type=F32)
        vgt[cols, :] = value_t.astype(BF16)
        vg[:, cols] = value_t.T.astype(BF16)
        key_t = scale * lax.dot_general(
            q[0, 0, :, cols], dlow[head], TN, preferred_element_type=F32
        )
        kgt[cols, :] = key_t.astype(BF16)
        kg[:, cols] = key_t.T.astype(BF16)


def attend(queries, cotangent, keys, values):
    _, _, total, width = queries.shape
    span = 4 * keys[0].shape[0]
    same = bf16(*queries.shape)
    return call(
        attend_body,
        [queries, cotangent, *keys, *values],
        [same, same, bf16(span, width), bf16(span, width), bf16(width, span), bf16(width, span)],
        [pltpu.VMEM((width // HEAD_DIM, total, span), BF16)] * 2,
        room=16,
    )


def weight_body(count, index, grad_t, *refs):
    pieces, out = refs[:count], refs[count]
    for i in range(index.shape[0]):
        start = pl.multiple_of(index[i], TILE)
        rows = jnp.concatenate([piece[:, pl.ds(start, TILE)] for piece in pieces], 0)
        out[:, i * TILE : (i + 1) * TILE] = jnp.dot(
            grad_t[...], rows, preferred_element_type=F32
        ).astype(BF16)


def weight_part(index, grad_t, pieces, after=()):
    return call(
        functools.partial(weight_body, len(pieces)),
        [index, grad_t, *pieces],
        bf16(grad_t.shape[0], index.shape[0] * TILE),
        index=1,
        after=after,
    )


def share_body(part, keep, first, second, *refs):
    out, terms, turned, sems = refs[-4:]
    span = second.shape[1]
    step = TILE // 2
    sources = (keep.at[:, span:], first.at[:, :span], second)
    coming = [
        pltpu.make_async_copy(source, terms.at[i], sems.at[i])
        for i, source in enumerate(sources)
    ]
    for copy in coming:
        copy.start()
    for copy in coming:
        copy.wait()
    going = []
    for i in range(span // step):
        cols = slice(i * step, (i + 1) * step)
        total = terms[0, :, cols].astype(F32) + terms[1, :, cols].astype(F32)
        total = total + terms[2, :, cols].astype(F32)
        turned[cols, :] = total.T.astype(BF16)
        going.append(
            pltpu.make_async_copy(turned.at[cols, :], out.at[0, part, cols, :], sems.at[3 + i])
        )
        going[-1].start()
    for copy in going:
        copy.wait()


def share(part, keep, first, second, into=None):
    width, span = second.shape
    given = [] if into is None else [into]
    return pl.pallas_call(
        functools.partial(share_body, part),
        in_specs=[pl.BlockSpec(memory_space=pl.ANY)] * (3 + len(given)),
        out_specs=pl.BlockSpec(memory_space=pl.ANY),
        out_shape=bf16(1, 2, span, width),
        scratch_shapes=[
            pltpu.VMEM((3, width, span), BF16),
            pltpu.VMEM((span, width), BF16),
            pltpu.SemaphoreType.DMA((3 + 2 * span // TILE,)),
        ],
        input_output_aliases={3: 0} if given else {},
        compiler_params=pltpu.CompilerParams(vmem_limit_bytes=40 * 1024 * 1024),
        cost_estimate=LITTLE,
    )(keep, first, second, *given)


def place_body(core, mine, theirs, out, sems):
    half = mine.shape[0]
    low = pl.multiple_of(core[0] * half, half)
    high = pl.multiple_of((1 - core[0]) * half, half)
    copies = [
        pltpu.make_async_copy(mine, out.at[0, pl.ds(low, half), :], sems.at[0]),
        pltpu.make_async_copy(theirs, out.at[0, pl.ds(high, half), :], sems.at[1]),
    ]
    for copy in copies:
        copy.start()
    for copy in copies:
        copy.wait()


def place(core, mine, theirs):
    half, depth = mine.shape
    return pl.pallas_call(
        place_body,
        in_specs=[SCALARS, WHOLE, WHOLE],
        out_specs=pl.BlockSpec(memory_space=pl.ANY),
        out_shape=bf16(1, 2 * half, depth),
        scratch_shapes=[pltpu.SemaphoreType.DMA((2,))],
        compiler_params=pltpu.CompilerParams(vmem_limit_bytes=4 * 1024 * 1024),
        cost_estimate=LITTLE,
    )(core[None], mine, theirs)


def load_body(*refs):
    count = len(refs) // 2
    sems = refs[-1]
    copies = [
        pltpu.make_async_copy(refs[i], refs[count + i], sems.at[i]) for i in range(count)
    ]
    for copy in copies:
        copy.start()
    for copy in copies:
        copy.wait()


def load(*arrays):
    return pl.pallas_call(
        load_body,
        in_specs=[pl.BlockSpec(memory_space=pl.ANY)] * len(arrays),
        out_specs=[WHOLE] * len(arrays),
        out_shape=[bf16(*array.shape) for array in arrays],
        scratch_shapes=[pltpu.SemaphoreType.DMA((len(arrays),))],
        compiler_params=pltpu.CompilerParams(vmem_limit_bytes=4 * 1024 * 1024),
        cost_estimate=LITTLE,
    )(*arrays)


def encoder_body(low, left, kg, vg, w, *refs):
    outs = refs[-1:] if len(refs) == 1 else refs[-2:]
    rows = slice(low, low + kg.shape[0] // 2)
    half = outs[0].shape[0]
    for i in range(outs[0].shape[1] // TILE):
        cols = slice(i * TILE, (i + 1) * TILE)
        from_w = slice(left + i * TILE, left + (i + 1) * TILE)
        total = lax.dot_general(kg[rows, :], w[0, 0, from_w, :], NT, preferred_element_type=F32)
        total = total + lax.dot_general(
            vg[rows, :], w[0, 1, from_w, :], NT, preferred_element_type=F32
        )
        if len(refs) > 1:
            total = total + refs[0][:, cols].astype(F32)
        for j, out in enumerate(outs):
            out[:, cols] = total[j * half : (j + 1) * half].astype(BF16)


def encoder_part(key_grad, value_grad, kv_weight, side, columns, moved=None, after=()):
    rows, depth = key_grad.shape[0] // 2, kv_weight.shape[2] // 2
    return call(
        functools.partial(encoder_body, side * rows, columns * depth),
        [key_grad, value_grad, kv_weight] + ([] if moved is None else [moved]),
        bf16(rows, depth) if moved is None else [bf16(rows // 2, depth)] * 2,
        after=after,
        room=12,
    )


def tie(array, *others):
    return lax.optimization_barrier((array, *others))[0]


def on_device(encoded, kv_weight, queries, cotangent):
    core = lax.axis_index("tensor") % 2
    y = lax.axis_index("dp")
    block = encoded[0]
    half = block.shape[0] // 2

    one, other = y ^ 1, 3 - y
    first = jnp.where(core == 0, one, other)
    second = jnp.where(core == 0, other, one)

    def starts(*places):
        index = jnp.stack([2 * TILE * place + low for place in places for low in (0, TILE)])
        return index.astype(jnp.int32)

    own = lax.dynamic_slice_in_dim(block, core * half, half, 0)
    too = lax.dynamic_slice_in_dim(block, (1 - core) * half, half, 0)
    own, too, go, stay = lax.optimization_barrier(
        (own, too, starts(first, (y + 2) % 4), starts(second, y))
    )
    h, h_too = {"o": own}, {"o": too}
    g, g_too = {}, {}
    h["a"] = send(h["o"], X_FIRST)
    h["b"] = send(h["o"], X_SECOND)
    g["o"] = send(h["o"], ALONG_Z)
    kv_weight, queries, cotangent = load(kv_weight, queries, cotangent)
    g["a"] = send(tie(h["a"], kv_weight, queries), ALONG_Z)
    h["d"] = send(h["a"], X_SECOND)
    g["b"] = send(h["b"], ALONG_Z)
    h_too["a"] = send(h["a"], SWAP)
    h_too["b"] = send(h["b"], SWAP)
    g_too["o"] = send(g["o"], SWAP)
    done = [
        project((h["o"], h_too["o"], h["a"], h_too["a"]), kv_weight),
        project((g["o"], g_too["o"], h["b"], h_too["b"]), kv_weight),
    ]
    g["d"] = send(tie(g["a"], done[0][0], done[1][0]), X_SECOND)
    h_too["d"] = send(h["d"], SWAP)
    g_too["a"] = send(g["a"], SWAP)
    g_too["b"] = send(g["b"], SWAP)
    done.append(project((g["a"], g_too["a"], h["d"], h_too["d"]), kv_weight))
    g_too["d"] = send(tie(g["d"], done[2][0]), SWAP)
    done.append(project((g["b"], g_too["b"], g["d"], g_too["d"]), kv_weight))
    keys, values = zip(*done)
    order = ["ho", "go", "hb", "gb", "ha", "ga", "hd", "gd"]
    pieces = [{"h": h, "g": g}[name[0]][name[1]] for name in order]
    pieces += [{"h": h_too, "g": g_too}[name[0]][name[1]] for name in order]

    attended, query_grad, key_grad, value_grad, key_grad_t, value_grad_t = attend(
        queries, cotangent, keys, values
    )

    grads = (key_grad, value_grad, kv_weight)
    moved = [encoder_part(*grads, 1, i) for i in range(2)]
    value_out = weight_part(go, value_grad_t, pieces, moved)
    moved = [send(part, SWAP) for part in moved]
    early = (value_out,)
    kept, x_out = zip(*[encoder_part(*grads, 0, i, moved[i], early) for i in range(2)])
    key_out = weight_part(go, key_grad_t, pieces, x_out)
    value_keep = weight_part(stay, value_grad_t, pieces, (key_out,))
    key_keep = weight_part(stay, key_grad_t, pieces, (value_keep,))

    def onward(keep, moved):
        span = keep.shape[1] // 2
        return (keep[:, :span].astype(F32) + moved[:, span:].astype(F32)).astype(BF16)

    value_in = send(value_out, Y_FIRST)
    key_in = send(tie(key_out, value_in), Y_FIRST)
    value_two = send(tie(onward(value_keep, value_in), key_in), Y_SECOND)
    key_two = send(tie(onward(key_keep, key_in), value_two), Y_SECOND)

    last = []
    for keep, out in zip(kept, x_out):
        came = send(out, X_FIRST)
        total = tie(keep, key_keep).astype(F32) + came.astype(F32)
        came = send(total[2 * half :].astype(BF16), X_SECOND)
        total = total[: 2 * half] + came.astype(F32)
        here = total[:half] + send(total[half:].astype(BF16), BACK_Z).astype(F32)
        here = here.astype(BF16)
        came = send(here, ACROSS_Z)
        last.append((tie(here, key_in).astype(F32) + came.astype(F32)).astype(BF16))
    last = jnp.concatenate(last, 1)
    enc_grad = place(core, last, send(last, SWAP))

    weight_grad = share(1, value_keep, value_in, value_two)
    weight_grad = share(0, key_keep, key_in, key_two, weight_grad)
    return (attended, query_grad, enc_grad, weight_grad)


def solution(mesh):
    return jax.shard_map(
        on_device,
        mesh=mesh,
        in_specs=(
            P("dp", "pipe", None),
            P("pipe", None, None, "tensor"),
            P("dp", "pipe", None, "tensor"),
            P("dp", "pipe", None, "tensor"),
        ),
        out_specs=(
            P("dp", "pipe", None, "tensor"),
            P("dp", "pipe", None, "tensor"),
            P("dp", "pipe", None),
            P("pipe", None, "dp", "tensor"),
        ),
        check_vma=False,
    )
```

```python
import functools

import jax
import jax.numpy as jnp
from jax import lax
from jax.experimental import pallas as pl
from jax.experimental.pallas import tpu as pltpu
from jax.sharding import PartitionSpec as P

HEAD_DIM = 256
ALL = ("pipe", "tensor", "dp")
F32, BF16 = jnp.float32, jnp.bfloat16
NT = (((1,), (1,)), ((), ()))
TN = (((0,), (0,)), ((), ()))
TILE = 512
WHOLE = pl.BlockSpec(memory_space=pltpu.VMEM)
SCALARS = pl.BlockSpec(memory_space=pltpu.SMEM)


LITTLE = pl.CostEstimate(flops=1000, bytes_accessed=1000, transcendentals=0)


def call(body, operands, shapes, scratch=(), index=0, after=(), room=8):
    many = isinstance(shapes, (list, tuple))
    count = len(operands)
    operands = [*operands, *after]

    def reads(*refs):
        body(*refs[:count], *refs[count + len(after) :])

    return pl.pallas_call(
        reads,
        in_specs=[SCALARS] * index
        + [WHOLE] * (count - index)
        + [pl.BlockSpec(memory_space=pl.ANY)] * len(after),
        out_specs=[WHOLE] * len(shapes) if many else WHOLE,
        out_shape=shapes,
        scratch_shapes=scratch,
        compiler_params=pltpu.CompilerParams(vmem_limit_bytes=room * 1024 * 1024),
        cost_estimate=LITTLE,
    )(*operands)


def bf16(*shape):
    return jax.ShapeDtypeStruct(shape, BF16)


def pairs(move):
    def index(x, y, z, core):
        pipe = (z % 2) * 4 + x
        tensor = (z // 2) * 2 + core
        return (pipe * 4 + tensor) * 4 + y

    found = []
    for x in range(4):
        for y in range(4):
            for z in range(4):
                for core in range(2):
                    to_x, to_y, to_z, to_core = move(x, y, z, core)
                    found.append((index(x, y, z, core), index(to_x, to_y, to_z % 4, to_core)))
    return found


def partner(place, core, which):
    return place ^ 1 if core == which else 3 - place


X_FIRST = pairs(lambda x, y, z, core: (partner(x, core, 0), y, z, core))
X_SECOND = pairs(lambda x, y, z, core: (partner(x, core, 1), y, z, core))
Y_FIRST = pairs(lambda x, y, z, core: (x, partner(y, core, 0), z, core))
Y_SECOND = pairs(lambda x, y, z, core: (x, partner(y, core, 1), z, core))
ALONG_Z = pairs(lambda x, y, z, core: (x, y, z + 1 - 2 * core, core))
BACK_Z = pairs(lambda x, y, z, core: (x, y, z - 1 + 2 * core, core))
ACROSS_Z = pairs(lambda x, y, z, core: (x, y, z + 2, core))
SWAP = pairs(lambda x, y, z, core: (x, y, z, 1 - core))


def send(array, route):
    return lax.ppermute(array, ALL, route)


def project_body(a, b, c, d, w, keys, values):
    x = jnp.concatenate([a[...], b[...], c[...], d[...]], 0)
    keys[...] = jnp.dot(x, w[0, 0], preferred_element_type=F32).astype(BF16)
    values[...] = jnp.dot(x, w[0, 1], preferred_element_type=F32).astype(BF16)


def project(pieces, kv_weight):
    shape = bf16(4 * pieces[0].shape[0], kv_weight.shape[3])
    return call(project_body, [*pieces, kv_weight], [shape, shape])


def arrange(groups):
    quarter = groups[0].shape[0] // 4

    def at(group, place):
        return groups[group][place * quarter : (place + 1) * quarter, :]

    order = [(0, 0), (1, 0), (1, 2), (3, 0), (0, 2), (2, 0), (2, 2), (3, 2)]
    return jnp.concatenate(
        [at(g, p) for g, p in order] + [at(g, p + 1) for g, p in order], 0
    )


def forward_body(q, g, k0, k1, k2, k3, v0, v1, v2, v3, att, probs_out, vg, vgt, low):
    scale = HEAD_DIM ** (-0.5)
    total = q.shape[2]
    chunk = total // 2
    for head in range(q.shape[3] // HEAD_DIM):
        cols = slice(head * HEAD_DIM, (head + 1) * HEAD_DIM)
        k = arrange([ref[:, cols] for ref in (k0, k1, k2, k3)])
        v = arrange([ref[:, cols] for ref in (v0, v1, v2, v3)])
        for part in range(2):
            rows = slice(part * chunk, (part + 1) * chunk)
            scores = scale * lax.dot_general(
                q[0, 0, rows, cols], k, NT, preferred_element_type=F32
            )
            expd = jnp.exp(scores - jnp.max(scores, axis=-1, keepdims=True))
            probs = expd * (1.0 / jnp.sum(expd, axis=-1, keepdims=True))
            probs_out[head, rows, :] = probs
            probs_low = probs.astype(BF16)
            low[head, rows, :] = probs_low
            att[0, 0, rows, cols] = jnp.dot(
                probs_low, v, preferred_element_type=F32
            ).astype(BF16)
        value_t = lax.dot_general(g[0, 0, :, cols], low[head], TN, preferred_element_type=F32)
        vgt[cols, :] = value_t.astype(BF16)
        vg[:, cols] = value_t.T.astype(BF16)


def backward_body(q, g, k0, k1, k2, k3, v0, v1, v2, v3, att, probs, dq, kg, kgt, dlow):
    scale = HEAD_DIM ** (-0.5)
    total = q.shape[2]
    chunk = total // 2
    for head in range(q.shape[3] // HEAD_DIM):
        cols = slice(head * HEAD_DIM, (head + 1) * HEAD_DIM)
        k = arrange([ref[:, cols] for ref in (k0, k1, k2, k3)])
        v = arrange([ref[:, cols] for ref in (v0, v1, v2, v3)])
        for part in range(2):
            rows = slice(part * chunk, (part + 1) * chunk)
            g_rows = g[0, 0, rows, cols]
            dprobs = lax.dot_general(g_rows, v, NT, preferred_element_type=F32)
            delta = jnp.sum(
                g_rows.astype(F32) * att[0, 0, rows, cols].astype(F32), axis=-1, keepdims=True
            )
            ds_low = (probs[head, rows, :] * (dprobs - delta)).astype(BF16)
            dlow[head, rows, :] = ds_low
            dq[0, 0, rows, cols] = (
                scale * jnp.dot(ds_low, k, preferred_element_type=F32)
            ).astype(BF16)
        key_t = scale * lax.dot_general(
            q[0, 0, :, cols], dlow[head], TN, preferred_element_type=F32
        )
        kgt[cols, :] = key_t.astype(BF16)
        kg[:, cols] = key_t.T.astype(BF16)


def forward(queries, cotangent, keys, values):
    _, _, total, width = queries.shape
    span, heads = 4 * keys[0].shape[0], width // HEAD_DIM
    return call(
        forward_body,
        [queries, cotangent, *keys, *values],
        [
            bf16(*queries.shape),
            jax.ShapeDtypeStruct((heads, total, span), F32),
            bf16(span, width),
            bf16(width, span),
        ],
        [pltpu.VMEM((heads, total, span), BF16)],
        room=12,
    )


def backward(queries, cotangent, keys, values, attended, probs, after):
    _, _, total, width = queries.shape
    span, heads = 4 * keys[0].shape[0], width // HEAD_DIM
    return call(
        backward_body,
        [queries, cotangent, *keys, *values, attended, probs],
        [bf16(*queries.shape), bf16(span, width), bf16(width, span)],
        [pltpu.VMEM((heads, total, span), BF16)],
        after=after,
        room=12,
    )


def weight_body(count, index, grad_t, *refs):
    pieces, out = refs[:count], refs[count]
    for i in range(index.shape[0]):
        start = pl.multiple_of(index[i], TILE)
        rows = jnp.concatenate([piece[:, pl.ds(start, TILE)] for piece in pieces], 0)
        out[:, i * TILE : (i + 1) * TILE] = jnp.dot(
            grad_t[...], rows, preferred_element_type=F32
        ).astype(BF16)


def weight_part(index, grad_t, pieces, after=()):
    return call(
        functools.partial(weight_body, len(pieces)),
        [index, grad_t, *pieces],
        bf16(grad_t.shape[0], index.shape[0] * TILE),
        index=1,
        after=after,
    )


def share_body(part, keep, first, second, *refs):
    out, terms, turned, sems = refs[-4:]
    span = second.shape[1]
    step = TILE // 2
    sources = (keep.at[:, span:], first.at[:, :span], second)
    coming = [
        pltpu.make_async_copy(source, terms.at[i], sems.at[i])
        for i, source in enumerate(sources)
    ]
    for copy in coming:
        copy.start()
    for copy in coming:
        copy.wait()
    going = []
    for i in range(span // step):
        cols = slice(i * step, (i + 1) * step)
        total = terms[0, :, cols].astype(F32) + terms[1, :, cols].astype(F32)
        total = total + terms[2, :, cols].astype(F32)
        turned[cols, :] = total.T.astype(BF16)
        going.append(
            pltpu.make_async_copy(turned.at[cols, :], out.at[0, part, cols, :], sems.at[3 + i])
        )
        going[-1].start()
    for copy in going:
        copy.wait()


def share(part, keep, first, second, into=None):
    width, span = second.shape
    given = [] if into is None else [into]
    return pl.pallas_call(
        functools.partial(share_body, part),
        in_specs=[pl.BlockSpec(memory_space=pl.ANY)] * (3 + len(given)),
        out_specs=pl.BlockSpec(memory_space=pl.ANY),
        out_shape=bf16(1, 2, span, width),
        scratch_shapes=[
            pltpu.VMEM((3, width, span), BF16),
            pltpu.VMEM((span, width), BF16),
            pltpu.SemaphoreType.DMA((3 + 2 * span // TILE,)),
        ],
        input_output_aliases={3: 0} if given else {},
        compiler_params=pltpu.CompilerParams(vmem_limit_bytes=40 * 1024 * 1024),
        cost_estimate=LITTLE,
    )(keep, first, second, *given)


def place_body(core, *refs):
    parts, out, sems = refs[:4], refs[4], refs[5]
    half, span = parts[0].shape
    low = pl.multiple_of(core[0] * half, half)
    high = pl.multiple_of((1 - core[0]) * half, half)
    copies = []
    for i, part in enumerate(parts):
        rows = pl.ds(low if i < 2 else high, half)
        cols = slice(i % 2 * span, (i % 2 + 1) * span)
        copies.append(pltpu.make_async_copy(part, out.at[0, rows, cols], sems.at[i]))
        copies[-1].start()
    for copy in copies:
        copy.wait()


def place(core, mine, theirs):
    half, span = mine[0].shape
    return pl.pallas_call(
        place_body,
        in_specs=[SCALARS] + [WHOLE] * 4,
        out_specs=pl.BlockSpec(memory_space=pl.ANY),
        out_shape=bf16(1, 2 * half, 2 * span),
        scratch_shapes=[pltpu.SemaphoreType.DMA((4,))],
        compiler_params=pltpu.CompilerParams(vmem_limit_bytes=4 * 1024 * 1024),
        cost_estimate=LITTLE,
    )(core[None], *mine, *theirs)


def load_body(*refs):
    count = len(refs) // 2
    sems = refs[-1]
    copies = [
        pltpu.make_async_copy(refs[i], refs[count + i], sems.at[i]) for i in range(count)
    ]
    for copy in copies:
        copy.start()
    for copy in copies:
        copy.wait()


def load(*arrays):
    return pl.pallas_call(
        load_body,
        in_specs=[pl.BlockSpec(memory_space=pl.ANY)] * len(arrays),
        out_specs=[WHOLE] * len(arrays),
        out_shape=[bf16(*array.shape) for array in arrays],
        scratch_shapes=[pltpu.SemaphoreType.DMA((len(arrays),))],
        compiler_params=pltpu.CompilerParams(vmem_limit_bytes=4 * 1024 * 1024),
        cost_estimate=LITTLE,
    )(*arrays)


def encoder_body(low, left, kg, vg, w, *refs):
    moved, outs = refs[:-2], refs[-2:]
    half = outs[0].shape[0]
    rows = slice(low, low + 2 * half)
    for i in range(outs[0].shape[1] // TILE):
        cols = slice(i * TILE, (i + 1) * TILE)
        from_w = slice(left + i * TILE, left + (i + 1) * TILE)
        total = lax.dot_general(kg[rows, :], w[0, 0, from_w, :], NT, preferred_element_type=F32)
        total = total + lax.dot_general(
            vg[rows, :], w[0, 1, from_w, :], NT, preferred_element_type=F32
        )
        for j, out in enumerate(outs):
            part = total[j * half : (j + 1) * half]
            if moved:
                part = part + moved[j][:, cols].astype(F32)
            out[:, cols] = part.astype(BF16)


def encoder_part(key_grad, value_grad, kv_weight, side, columns, moved=(), after=()):
    rows, depth = key_grad.shape[0] // 4, kv_weight.shape[2] // 2
    return call(
        functools.partial(encoder_body, 2 * side * rows, columns * depth),
        [key_grad, value_grad, kv_weight, *moved],
        [bf16(rows, depth)] * 2,
        after=after,
        room=12,
    )


def tie(array, *others):
    return lax.optimization_barrier((array, *others))[0]


def on_device(encoded, kv_weight, queries, cotangent):
    core = lax.axis_index("tensor") % 2
    y = lax.axis_index("dp")
    block = encoded[0]
    half = block.shape[0] // 2

    one, other = y ^ 1, 3 - y
    first = jnp.where(core == 0, one, other)
    second = jnp.where(core == 0, other, one)

    def starts(*places):
        index = jnp.stack([2 * TILE * place + low for place in places for low in (0, TILE)])
        return index.astype(jnp.int32)

    own = lax.dynamic_slice_in_dim(block, core * half, half, 0)
    too = lax.dynamic_slice_in_dim(block, (1 - core) * half, half, 0)
    own, too, go, stay = lax.optimization_barrier(
        (own, too, starts(first, (y + 2) % 4), starts(second, y))
    )
    h, h_too = {"o": own}, {"o": too}
    g, g_too = {}, {}
    h["a"] = send(h["o"], X_FIRST)
    h["b"] = send(h["o"], X_SECOND)
    g["o"] = send(h["o"], ALONG_Z)
    kv_weight, queries, cotangent = load(kv_weight, queries, cotangent)
    g["a"] = send(tie(h["a"], kv_weight, queries), ALONG_Z)
    h["d"] = send(h["a"], X_SECOND)
    g["b"] = send(h["b"], ALONG_Z)
    h_too["a"] = send(h["a"], SWAP)
    h_too["b"] = send(h["b"], SWAP)
    g_too["o"] = send(g["o"], SWAP)
    done = [
        project((h["o"], h_too["o"], h["a"], h_too["a"]), kv_weight),
        project((g["o"], g_too["o"], h["b"], h_too["b"]), kv_weight),
    ]
    g["d"] = send(tie(g["a"], done[0][0], done[1][0]), X_SECOND)
    h_too["d"] = send(h["d"], SWAP)
    g_too["a"] = send(g["a"], SWAP)
    g_too["b"] = send(g["b"], SWAP)
    done.append(project((g["a"], g_too["a"], h["d"], h_too["d"]), kv_weight))
    g_too["d"] = send(tie(g["d"], done[2][0]), SWAP)
    done.append(project((g["b"], g_too["b"], g["d"], g_too["d"]), kv_weight))
    keys, values = zip(*done)
    order = ["ho", "go", "hb", "gb", "ha", "ga", "hd", "gd"]
    pieces = [{"h": h, "g": g}[name[0]][name[1]] for name in order]
    pieces += [{"h": h_too, "g": g_too}[name[0]][name[1]] for name in order]

    inputs = (queries, cotangent, keys, values)
    attended, probs, value_grad, value_grad_t = forward(*inputs)
    value_out = weight_part(go, value_grad_t, pieces)
    query_grad, key_grad, key_grad_t = backward(*inputs, attended, probs, (value_out,))

    grads = (key_grad, value_grad, kv_weight)
    moved = [[send(part, SWAP) for part in encoder_part(*grads, 1, i)] for i in range(2)]
    kept, x_out = zip(*[encoder_part(*grads, 0, i, moved[i]) for i in range(2)])
    key_out = weight_part(go, key_grad_t, pieces, x_out)
    value_keep = weight_part(stay, value_grad_t, pieces, (key_out,))
    key_keep = weight_part(stay, key_grad_t, pieces, (value_keep,))

    def onward(keep, moved):
        span = keep.shape[1] // 2
        return (keep[:, :span].astype(F32) + moved[:, span:].astype(F32)).astype(BF16)

    value_in = send(value_out, Y_FIRST)
    key_in = send(tie(key_out, value_in), Y_FIRST)
    value_two = send(tie(onward(value_keep, value_in), key_in), Y_SECOND)
    key_two = send(tie(onward(key_keep, key_in), value_two), Y_SECOND)

    last = []
    for keep, out in zip(kept, x_out):
        came = send(out, X_FIRST)
        total = tie(keep, key_keep).astype(F32) + came.astype(F32)
        came = send(total[2 * half :].astype(BF16), X_SECOND)
        total = total[: 2 * half] + came.astype(F32)
        here = total[:half] + send(total[half:].astype(BF16), BACK_Z).astype(F32)
        here = here.astype(BF16)
        came = send(here, ACROSS_Z)
        last.append((tie(here, key_in).astype(F32) + came.astype(F32)).astype(BF16))
    enc_grad = place(core, last, [send(part, SWAP) for part in last])

    weight_grad = share(1, value_keep, value_in, value_two)
    weight_grad = share(0, key_keep, key_in, key_two, weight_grad)
    return (attended, query_grad, enc_grad, weight_grad)


def solution(mesh):
    return jax.shard_map(
        on_device,
        mesh=mesh,
        in_specs=(
            P("dp", "pipe", None),
            P("pipe", None, None, "tensor"),
            P("dp", "pipe", None, "tensor"),
            P("dp", "pipe", None, "tensor"),
        ),
        out_specs=(
            P("dp", "pipe", None, "tensor"),
            P("dp", "pipe", None, "tensor"),
            P("dp", "pipe", None),
            P("pipe", None, "dp", "tensor"),
        ),
        check_vma=False,
    )
```

```python
import functools

import jax
import jax.numpy as jnp
from jax import lax
from jax.experimental import pallas as pl
from jax.experimental.pallas import tpu as pltpu
from jax.sharding import PartitionSpec as P

HEAD_DIM = 256
ALL = ("pipe", "tensor", "dp")
F32, BF16 = jnp.float32, jnp.bfloat16
NT = (((1,), (1,)), ((), ()))
TN = (((0,), (0,)), ((), ()))
TILE = 512
WHOLE = pl.BlockSpec(memory_space=pltpu.VMEM)
ANY = pl.BlockSpec(memory_space=pl.ANY)
SCALARS = pl.BlockSpec(memory_space=pltpu.SMEM)


LITTLE = pl.CostEstimate(flops=1000, bytes_accessed=1000, transcendentals=0)


def call(body, operands, shapes, scratch=(), index=0, after=(), room=8):
    many = isinstance(shapes, (list, tuple))
    count = len(operands)
    operands = [*operands, *after]

    def reads(*refs):
        body(*refs[:count], *refs[count + len(after) :])

    return pl.pallas_call(
        reads,
        in_specs=[SCALARS] * index
        + [WHOLE] * (count - index)
        + [pl.BlockSpec(memory_space=pl.ANY)] * len(after),
        out_specs=[WHOLE] * len(shapes) if many else WHOLE,
        out_shape=shapes,
        scratch_shapes=scratch,
        compiler_params=pltpu.CompilerParams(vmem_limit_bytes=room * 1024 * 1024),
        cost_estimate=LITTLE,
    )(*operands)


def bf16(*shape):
    return jax.ShapeDtypeStruct(shape, BF16)


def pairs(move):
    def index(x, y, z, core):
        pipe = (z % 2) * 4 + x
        tensor = (z // 2) * 2 + core
        return (pipe * 4 + tensor) * 4 + y

    found = []
    for x in range(4):
        for y in range(4):
            for z in range(4):
                for core in range(2):
                    to_x, to_y, to_z, to_core = move(x, y, z, core)
                    found.append((index(x, y, z, core), index(to_x, to_y, to_z % 4, to_core)))
    return found


def partner(place, core, which):
    return place ^ 1 if core == which else 3 - place


X_FIRST = pairs(lambda x, y, z, core: (partner(x, core, 0), y, z, core))
X_SECOND = pairs(lambda x, y, z, core: (partner(x, core, 1), y, z, core))
Y_FIRST = pairs(lambda x, y, z, core: (x, partner(y, core, 0), z, core))
Y_SECOND = pairs(lambda x, y, z, core: (x, partner(y, core, 1), z, core))
ALONG_Z = pairs(lambda x, y, z, core: (x, y, z + 1 - 2 * core, core))
BACK_Z = pairs(lambda x, y, z, core: (x, y, z - 1 + 2 * core, core))
ACROSS_Z = pairs(lambda x, y, z, core: (x, y, z + 2, core))
SWAP = pairs(lambda x, y, z, core: (x, y, z, 1 - core))


def send(array, route):
    return lax.ppermute(array, ALL, route)


def project_body(a, b, c, d, w, keys, values):
    x = jnp.concatenate([a[...], b[...], c[...], d[...]], 0)
    keys[...] = jnp.dot(x, w[0, 0], preferred_element_type=F32).astype(BF16)
    values[...] = jnp.dot(x, w[0, 1], preferred_element_type=F32).astype(BF16)


def project(pieces, kv_weight):
    shape = bf16(4 * pieces[0].shape[0], kv_weight.shape[3])
    return call(project_body, [*pieces, kv_weight], [shape, shape])


def arrange(groups):
    quarter = groups[0].shape[0] // 4

    def at(group, place):
        return groups[group][place * quarter : (place + 1) * quarter, :]

    order = [(0, 0), (1, 0), (1, 2), (3, 0), (0, 2), (2, 0), (2, 2), (3, 2)]
    return jnp.concatenate(
        [at(g, p) for g, p in order] + [at(g, p + 1) for g, p in order], 0
    )


def forward_body(q, g, k0, k1, k2, k3, v0, v1, v2, v3, att, probs_out, vg, vgt, low):
    scale = HEAD_DIM ** (-0.5)
    total = q.shape[2]
    chunk = total // 2
    for head in range(q.shape[3] // HEAD_DIM):
        cols = slice(head * HEAD_DIM, (head + 1) * HEAD_DIM)
        k = arrange([ref[:, cols] for ref in (k0, k1, k2, k3)])
        v = arrange([ref[:, cols] for ref in (v0, v1, v2, v3)])
        for part in range(2):
            rows = slice(part * chunk, (part + 1) * chunk)
            scores = scale * lax.dot_general(
                q[0, 0, rows, cols], k, NT, preferred_element_type=F32
            )
            expd = jnp.exp(scores - jnp.max(scores, axis=-1, keepdims=True))
            probs = expd * (1.0 / jnp.sum(expd, axis=-1, keepdims=True))
            probs_out[head, rows, :] = probs
            probs_low = probs.astype(BF16)
            low[head, rows, :] = probs_low
            att[0, 0, rows, cols] = jnp.dot(
                probs_low, v, preferred_element_type=F32
            ).astype(BF16)
        value_t = lax.dot_general(g[0, 0, :, cols], low[head], TN, preferred_element_type=F32)
        vgt[cols, :] = value_t.astype(BF16)
        vg[:, cols] = value_t.T.astype(BF16)


def backward_body(q, g, k0, k1, k2, k3, v0, v1, v2, v3, att, probs, dq, kg, kgt, dlow):
    scale = HEAD_DIM ** (-0.5)
    total = q.shape[2]
    chunk = total // 2
    for head in range(q.shape[3] // HEAD_DIM):
        cols = slice(head * HEAD_DIM, (head + 1) * HEAD_DIM)
        k = arrange([ref[:, cols] for ref in (k0, k1, k2, k3)])
        v = arrange([ref[:, cols] for ref in (v0, v1, v2, v3)])
        for part in range(2):
            rows = slice(part * chunk, (part + 1) * chunk)
            g_rows = g[0, 0, rows, cols]
            dprobs = lax.dot_general(g_rows, v, NT, preferred_element_type=F32)
            delta = jnp.sum(
                g_rows.astype(F32) * att[0, 0, rows, cols].astype(F32), axis=-1, keepdims=True
            )
            ds_low = (probs[head, rows, :] * (dprobs - delta)).astype(BF16)
            dlow[head, rows, :] = ds_low
            dq[0, 0, rows, cols] = (
                scale * jnp.dot(ds_low, k, preferred_element_type=F32)
            ).astype(BF16)
        key_t = scale * lax.dot_general(
            q[0, 0, :, cols], dlow[head], TN, preferred_element_type=F32
        )
        kgt[cols, :] = key_t.astype(BF16)
        kg[:, cols] = key_t.T.astype(BF16)


def forward(queries, cotangent, keys, values):
    _, _, total, width = queries.shape
    span, heads = 4 * keys[0].shape[0], width // HEAD_DIM
    return call(
        forward_body,
        [queries, cotangent, *keys, *values],
        [
            bf16(*queries.shape),
            jax.ShapeDtypeStruct((heads, total, span), F32),
            bf16(span, width),
            bf16(width, span),
        ],
        [pltpu.VMEM((heads, total, span), BF16)],
        room=12,
    )


def backward(queries, cotangent, keys, values, attended, probs, after):
    _, _, total, width = queries.shape
    span, heads = 4 * keys[0].shape[0], width // HEAD_DIM
    return call(
        backward_body,
        [queries, cotangent, *keys, *values, attended, probs],
        [bf16(*queries.shape), bf16(span, width), bf16(width, span)],
        [pltpu.VMEM((heads, total, span), BF16)],
        after=after,
        room=12,
    )


def weight_body(count, index, grad_t, *refs):
    pieces, out = refs[:count], refs[count]
    for i in range(index.shape[0]):
        start = pl.multiple_of(index[i], TILE)
        rows = jnp.concatenate([piece[:, pl.ds(start, TILE)] for piece in pieces], 0)
        out[:, i * TILE : (i + 1) * TILE] = jnp.dot(
            grad_t[...], rows, preferred_element_type=F32
        ).astype(BF16)


def weight_part(index, grad_t, pieces, after=()):
    return call(
        functools.partial(weight_body, len(pieces)),
        [index, grad_t, *pieces],
        bf16(grad_t.shape[0], index.shape[0] * TILE),
        index=1,
        after=after,
    )


def share_body(part, count, keep, first, *refs):
    seconds, (out, terms, turned, sems) = refs[:count], refs[-4:]
    span = turned.shape[0]
    step = TILE // 2
    sources = [(keep.at[:, span:], terms.at[0]), (first.at[:, :span], terms.at[1])]
    for i, second in enumerate(seconds):
        cols = slice(i * second.shape[1], (i + 1) * second.shape[1])
        sources.append((second, terms.at[2, :, cols]))
    coming = [
        pltpu.make_async_copy(source, target, sems.at[i])
        for i, (source, target) in enumerate(sources)
    ]
    for copy in coming:
        copy.start()
    for copy in coming:
        copy.wait()
    going = []
    for i in range(span // step):
        cols = slice(i * step, (i + 1) * step)
        total = terms[0, :, cols].astype(F32) + terms[1, :, cols].astype(F32)
        total = total + terms[2, :, cols].astype(F32)
        turned[cols, :] = total.T.astype(BF16)
        going.append(
            pltpu.make_async_copy(turned.at[cols, :], out.at[0, part, cols, :], sems.at[4 + i])
        )
        going[-1].start()
    for copy in going:
        copy.wait()


def share(part, keep, first, seconds, into=None):
    width, span = keep.shape[0], keep.shape[1] // 2
    given = [] if into is None else [into]
    return pl.pallas_call(
        functools.partial(share_body, part, len(seconds)),
        in_specs=[ANY] * (2 + len(seconds) + len(given)),
        out_specs=ANY,
        out_shape=bf16(1, 2, span, width),
        scratch_shapes=[
            pltpu.VMEM((3, width, span), BF16),
            pltpu.VMEM((span, width), BF16),
            pltpu.SemaphoreType.DMA((4 + 2 * span // TILE,)),
        ],
        input_output_aliases={2 + len(seconds): 0} if given else {},
        compiler_params=pltpu.CompilerParams(vmem_limit_bytes=40 * 1024 * 1024),
        cost_estimate=LITTLE,
    )(keep, first, *seconds, *given)


def place_body(core, *refs):
    parts, out, sems = refs[:4], refs[4], refs[5]
    half, span = parts[0].shape
    low = pl.multiple_of(core[0] * half, half)
    high = pl.multiple_of((1 - core[0]) * half, half)
    copies = []
    for i, part in enumerate(parts):
        rows = pl.ds(low if i < 2 else high, half)
        cols = slice(i % 2 * span, (i % 2 + 1) * span)
        copies.append(pltpu.make_async_copy(part, out.at[0, rows, cols], sems.at[i]))
        copies[-1].start()
    for copy in copies:
        copy.wait()


def place(core, mine, theirs):
    half, span = mine[0].shape
    return pl.pallas_call(
        place_body,
        in_specs=[SCALARS] + [WHOLE] * 4,
        out_specs=pl.BlockSpec(memory_space=pl.ANY),
        out_shape=bf16(1, 2 * half, 2 * span),
        scratch_shapes=[pltpu.SemaphoreType.DMA((4,))],
        compiler_params=pltpu.CompilerParams(vmem_limit_bytes=4 * 1024 * 1024),
        cost_estimate=LITTLE,
    )(core[None], *mine, *theirs)


def load_body(*refs):
    count = len(refs) // 2
    sems = refs[-1]
    copies = [
        pltpu.make_async_copy(refs[i], refs[count + i], sems.at[i]) for i in range(count)
    ]
    for copy in copies:
        copy.start()
    for copy in copies:
        copy.wait()


def load(*arrays):
    return pl.pallas_call(
        load_body,
        in_specs=[pl.BlockSpec(memory_space=pl.ANY)] * len(arrays),
        out_specs=[WHOLE] * len(arrays),
        out_shape=[bf16(*array.shape) for array in arrays],
        scratch_shapes=[pltpu.SemaphoreType.DMA((len(arrays),))],
        compiler_params=pltpu.CompilerParams(vmem_limit_bytes=4 * 1024 * 1024),
        cost_estimate=LITTLE,
    )(*arrays)


def encoder_body(low, left, kg, vg, w, *refs):
    moved, outs = refs[:-2], refs[-2:]
    half = outs[0].shape[0]
    rows = slice(low, low + 2 * half)
    for i in range(outs[0].shape[1] // TILE):
        cols = slice(i * TILE, (i + 1) * TILE)
        from_w = slice(left + i * TILE, left + (i + 1) * TILE)
        total = lax.dot_general(kg[rows, :], w[0, 0, from_w, :], NT, preferred_element_type=F32)
        total = total + lax.dot_general(
            vg[rows, :], w[0, 1, from_w, :], NT, preferred_element_type=F32
        )
        for j, out in enumerate(outs):
            part = total[j * half : (j + 1) * half]
            if moved:
                part = part + moved[j][:, cols].astype(F32)
            out[:, cols] = part.astype(BF16)


def encoder_part(key_grad, value_grad, kv_weight, side, columns, moved=(), after=()):
    rows, depth = key_grad.shape[0] // 4, kv_weight.shape[2] // 2
    return call(
        functools.partial(encoder_body, 2 * side * rows, columns * depth),
        [key_grad, value_grad, kv_weight, *moved],
        [bf16(rows, depth)] * 2,
        after=after,
        room=12,
    )


def add_body(held, came, stay, out):
    half = stay.shape[0]
    for i in range(held.shape[1] // TILE):
        cols = slice(i * TILE, (i + 1) * TILE)
        total = held[:, cols].astype(F32) + came[:, cols].astype(F32)
        stay[:, cols] = total[:half]
        out[:, cols] = total[half:].astype(BF16)


def add(held, came, after=()):
    rows, span = held.shape
    shapes = [jax.ShapeDtypeStruct((rows // 2, span), F32), bf16(rows // 2, span)]
    return call(add_body, [held, came], shapes, after=after, room=6)


def tie(array, *others):
    return lax.optimization_barrier((array, *others))[0]


def on_device(encoded, kv_weight, queries, cotangent):
    core = lax.axis_index("tensor") % 2
    y = lax.axis_index("dp")
    block = encoded[0]
    half = block.shape[0] // 2

    one, other = y ^ 1, 3 - y
    first = jnp.where(core == 0, one, other)
    second = jnp.where(core == 0, other, one)

    def starts(*places):
        index = jnp.stack([2 * TILE * place + low for place in places for low in (0, TILE)])
        return index.astype(jnp.int32)

    own = lax.dynamic_slice_in_dim(block, core * half, half, 0)
    too = lax.dynamic_slice_in_dim(block, (1 - core) * half, half, 0)
    own, too, go, stay = lax.optimization_barrier(
        (own, too, starts(first, (y + 2) % 4), starts(second, y))
    )
    h, h_too = {"o": own}, {"o": too}
    g, g_too = {}, {}
    h["a"] = send(h["o"], X_FIRST)
    h["b"] = send(h["o"], X_SECOND)
    g["o"] = send(h["o"], ALONG_Z)
    kv_weight, queries, cotangent = load(kv_weight, queries, cotangent)
    g["a"] = send(tie(h["a"], kv_weight, queries), ALONG_Z)
    h["d"] = send(h["a"], X_SECOND)
    g["d"] = send(g["a"], X_SECOND)
    h_too["a"] = send(h["a"], SWAP)
    h_too["b"] = send(h["b"], SWAP)
    g_too["o"] = send(g["o"], SWAP)
    h_too["d"] = send(h["d"], SWAP)
    g_too["a"] = send(g["a"], SWAP)
    done = [project((h["o"], h_too["o"], h["a"], h_too["a"]), kv_weight)]
    g["b"] = send(tie(h["b"], g["a"], done[0][0]), ALONG_Z)
    done.append(project((g["o"], g_too["o"], h["b"], h_too["b"]), kv_weight))
    done.append(project((g["a"], g_too["a"], h["d"], h_too["d"]), kv_weight))
    g_too["b"] = send(tie(g["b"], done[1][0]), SWAP)
    g_too["d"] = send(tie(g["d"], done[2][0]), SWAP)
    done.append(project((g["b"], g_too["b"], g["d"], g_too["d"]), kv_weight))
    keys, values = zip(*done)
    order = ["ho", "go", "hb", "gb", "ha", "ga", "hd", "gd"]
    pieces = [{"h": h, "g": g}[name[0]][name[1]] for name in order]
    pieces += [{"h": h_too, "g": g_too}[name[0]][name[1]] for name in order]

    inputs = (queries, cotangent, keys, values)
    attended, probs, value_grad, value_grad_t = forward(*inputs)
    value_out = weight_part(go, value_grad_t, pieces)
    query_grad, key_grad, key_grad_t = backward(*inputs, attended, probs, (value_out,))

    grads = (key_grad, value_grad, kv_weight)
    moved = [[send(part, SWAP) for part in encoder_part(*grads, 1, i)] for i in range(2)]
    kept, x_out = zip(*[encoder_part(*grads, 0, i, moved[i]) for i in range(2)])
    key_out = weight_part(go, key_grad_t, pieces, x_out)
    value_keep = weight_part(stay, value_grad_t, pieces, (key_out,))
    key_keep = weight_part(stay, key_grad_t, pieces, (value_keep,))

    def onward(keep, moved):
        span = keep.shape[1] // 2
        return (keep[:, :span].astype(F32) + moved[:, span:].astype(F32)).astype(BF16)

    value_in = send(value_out, Y_FIRST)
    key_in = send(tie(key_out, value_in), Y_FIRST)
    value_two = send(tie(onward(value_keep, value_in), key_in), Y_SECOND)
    key_two = jnp.split(onward(key_keep, key_in), 2, 1)
    key_two[0] = send(key_two[0], Y_SECOND)
    key_two[1] = send(tie(key_two[1], key_two[0]), Y_SECOND)

    mine, theirs = [], []
    for keep, out in zip(kept, x_out):
        held, going = add(keep, send(out, X_FIRST), (key_keep,))
        total = held + send(going, X_SECOND).astype(F32)
        here = total[:half] + send(total[half:].astype(BF16), BACK_Z).astype(F32)
        here = here.astype(BF16)
        came = send(here, ACROSS_Z)
        mine.append((here.astype(F32) + came.astype(F32)).astype(BF16))
        theirs.append(send(mine[-1], SWAP))
    enc_grad = place(core, mine, theirs)

    weight_grad = share(1, value_keep, value_in, [value_two])
    weight_grad = share(0, key_keep, key_in, key_two, weight_grad)
    return (attended, query_grad, enc_grad, weight_grad)


def solution(mesh):
    return jax.shard_map(
        on_device,
        mesh=mesh,
        in_specs=(
            P("dp", "pipe", None),
            P("pipe", None, None, "tensor"),
            P("dp", "pipe", None, "tensor"),
            P("dp", "pipe", None, "tensor"),
        ),
        out_specs=(
            P("dp", "pipe", None, "tensor"),
            P("dp", "pipe", None, "tensor"),
            P("dp", "pipe", None),
            P("pipe", None, "dp", "tensor"),
        ),
        check_vma=False,
    )
```

```python
import functools

import jax
import jax.numpy as jnp
from jax import lax
from jax.experimental import pallas as pl
from jax.experimental.pallas import tpu as pltpu
from jax.sharding import PartitionSpec as P

HEAD_DIM = 256
ALL = ("pipe", "tensor", "dp")
F32, BF16 = jnp.float32, jnp.bfloat16
NT = (((1,), (1,)), ((), ()))
TN = (((0,), (0,)), ((), ()))
TILE = 512
WHOLE = pl.BlockSpec(memory_space=pltpu.VMEM)
ANY = pl.BlockSpec(memory_space=pl.ANY)
SCALARS = pl.BlockSpec(memory_space=pltpu.SMEM)


LITTLE = pl.CostEstimate(flops=1000, bytes_accessed=1000, transcendentals=0)


def call(body, operands, shapes, scratch=(), index=0, after=(), room=8):
    many = isinstance(shapes, (list, tuple))
    count = len(operands)
    operands = [*operands, *after]

    def reads(*refs):
        body(*refs[:count], *refs[count + len(after) :])

    return pl.pallas_call(
        reads,
        in_specs=[SCALARS] * index
        + [WHOLE] * (count - index)
        + [pl.BlockSpec(memory_space=pl.ANY)] * len(after),
        out_specs=[WHOLE] * len(shapes) if many else WHOLE,
        out_shape=shapes,
        scratch_shapes=scratch,
        compiler_params=pltpu.CompilerParams(vmem_limit_bytes=room * 1024 * 1024),
        cost_estimate=LITTLE,
    )(*operands)


def bf16(*shape):
    return jax.ShapeDtypeStruct(shape, BF16)


def pairs(move):
    def index(x, y, z, core):
        pipe = (z % 2) * 4 + x
        tensor = (z // 2) * 2 + core
        return (pipe * 4 + tensor) * 4 + y

    found = []
    for x in range(4):
        for y in range(4):
            for z in range(4):
                for core in range(2):
                    to_x, to_y, to_z, to_core = move(x, y, z, core)
                    found.append((index(x, y, z, core), index(to_x, to_y, to_z % 4, to_core)))
    return found


def partner(place, core, which):
    return place ^ 1 if core == which else 3 - place


X_FIRST = pairs(lambda x, y, z, core: (partner(x, core, 0), y, z, core))
X_SECOND = pairs(lambda x, y, z, core: (partner(x, core, 1), y, z, core))
Y_FIRST = pairs(lambda x, y, z, core: (x, partner(y, core, 0), z, core))
Y_SECOND = pairs(lambda x, y, z, core: (x, partner(y, core, 1), z, core))
ALONG_Z = pairs(lambda x, y, z, core: (x, y, z + 1 - 2 * core, core))
BACK_Z = pairs(lambda x, y, z, core: (x, y, z - 1 + 2 * core, core))
DIAGONAL = pairs(lambda x, y, z, core: (partner(x, core, 1), y, z + 1 - 2 * core, core))
ACROSS_Z = pairs(lambda x, y, z, core: (x, y, z + 2, core))
SWAP = pairs(lambda x, y, z, core: (x, y, z, 1 - core))


def send(array, route):
    return lax.ppermute(array, ALL, route)


def project_body(a, b, c, d, w, keys, values):
    x = jnp.concatenate([a[...], b[...], c[...], d[...]], 0)
    keys[...] = jnp.dot(x, w[0, 0], preferred_element_type=F32).astype(BF16)
    values[...] = jnp.dot(x, w[0, 1], preferred_element_type=F32).astype(BF16)


def project(pieces, kv_weight):
    shape = bf16(4 * pieces[0].shape[0], kv_weight.shape[3])
    return call(project_body, [*pieces, kv_weight], [shape, shape])


def arrange(groups):
    quarter = groups[0].shape[0] // 4

    def at(group, place):
        return groups[group][place * quarter : (place + 1) * quarter, :]

    order = [(0, 0), (1, 0), (1, 2), (3, 0), (0, 2), (2, 0), (2, 2), (3, 2)]
    return jnp.concatenate(
        [at(g, p) for g, p in order] + [at(g, p + 1) for g, p in order], 0
    )


def forward_body(q, g, k0, k1, k2, k3, v0, v1, v2, v3, att, probs_out, vg, vgt, low):
    scale = HEAD_DIM ** (-0.5)
    total = q.shape[2]
    chunk = total // 2
    for head in range(q.shape[3] // HEAD_DIM):
        cols = slice(head * HEAD_DIM, (head + 1) * HEAD_DIM)
        k = arrange([ref[:, cols] for ref in (k0, k1, k2, k3)])
        v = arrange([ref[:, cols] for ref in (v0, v1, v2, v3)])
        for part in range(2):
            rows = slice(part * chunk, (part + 1) * chunk)
            scores = scale * lax.dot_general(
                q[0, 0, rows, cols], k, NT, preferred_element_type=F32
            )
            expd = jnp.exp(scores - jnp.max(scores, axis=-1, keepdims=True))
            probs = expd * (1.0 / jnp.sum(expd, axis=-1, keepdims=True))
            probs_out[head, rows, :] = probs
            probs_low = probs.astype(BF16)
            low[head, rows, :] = probs_low
            att[0, 0, rows, cols] = jnp.dot(
                probs_low, v, preferred_element_type=F32
            ).astype(BF16)
        value_t = lax.dot_general(g[0, 0, :, cols], low[head], TN, preferred_element_type=F32)
        vgt[cols, :] = value_t.astype(BF16)
        vg[:, cols] = value_t.T.astype(BF16)


def backward_body(q, g, k0, k1, k2, k3, v0, v1, v2, v3, att, probs, dq, kg, kgt, dlow):
    scale = HEAD_DIM ** (-0.5)
    total = q.shape[2]
    chunk = total // 2
    for head in range(q.shape[3] // HEAD_DIM):
        cols = slice(head * HEAD_DIM, (head + 1) * HEAD_DIM)
        k = arrange([ref[:, cols] for ref in (k0, k1, k2, k3)])
        v = arrange([ref[:, cols] for ref in (v0, v1, v2, v3)])
        for part in range(2):
            rows = slice(part * chunk, (part + 1) * chunk)
            g_rows = g[0, 0, rows, cols]
            dprobs = lax.dot_general(g_rows, v, NT, preferred_element_type=F32)
            delta = jnp.sum(
                g_rows.astype(F32) * att[0, 0, rows, cols].astype(F32), axis=-1, keepdims=True
            )
            ds_low = (probs[head, rows, :] * (dprobs - delta)).astype(BF16)
            dlow[head, rows, :] = ds_low
            dq[0, 0, rows, cols] = (
                scale * jnp.dot(ds_low, k, preferred_element_type=F32)
            ).astype(BF16)
        key_t = scale * lax.dot_general(
            q[0, 0, :, cols], dlow[head], TN, preferred_element_type=F32
        )
        kgt[cols, :] = key_t.astype(BF16)
        kg[:, cols] = key_t.T.astype(BF16)


def forward(queries, cotangent, keys, values):
    _, _, total, width = queries.shape
    span, heads = 4 * keys[0].shape[0], width // HEAD_DIM
    return call(
        forward_body,
        [queries, cotangent, *keys, *values],
        [
            bf16(*queries.shape),
            jax.ShapeDtypeStruct((heads, total, span), F32),
            bf16(span, width),
            bf16(width, span),
        ],
        [pltpu.VMEM((heads, total, span), BF16)],
        room=12,
    )


def backward(queries, cotangent, keys, values, attended, probs, after):
    _, _, total, width = queries.shape
    span, heads = 4 * keys[0].shape[0], width // HEAD_DIM
    return call(
        backward_body,
        [queries, cotangent, *keys, *values, attended, probs],
        [bf16(*queries.shape), bf16(span, width), bf16(width, span)],
        [pltpu.VMEM((heads, total, span), BF16)],
        after=after,
        room=12,
    )


def weight_body(count, index, grad_t, *refs):
    pieces, out = refs[:count], refs[count]
    for i in range(index.shape[0]):
        start = pl.multiple_of(index[i], TILE)
        rows = jnp.concatenate([piece[:, pl.ds(start, TILE)] for piece in pieces], 0)
        out[:, i * TILE : (i + 1) * TILE] = jnp.dot(
            grad_t[...], rows, preferred_element_type=F32
        ).astype(BF16)


def weight_part(index, grad_t, pieces, after=()):
    return call(
        functools.partial(weight_body, len(pieces)),
        [index, grad_t, *pieces],
        bf16(grad_t.shape[0], index.shape[0] * TILE),
        index=1,
        after=after,
    )


def share_body(part, count, keep, first, *refs):
    seconds, (out, terms, turned, sems) = refs[:count], refs[-4:]
    span = turned.shape[0]
    step = TILE // 2
    sources = [(keep.at[:, span:], terms.at[0]), (first.at[:, :span], terms.at[1])]
    for i, second in enumerate(seconds):
        cols = slice(i * second.shape[1], (i + 1) * second.shape[1])
        sources.append((second, terms.at[2, :, cols]))
    coming = [
        pltpu.make_async_copy(source, target, sems.at[i])
        for i, (source, target) in enumerate(sources)
    ]
    for copy in coming:
        copy.start()
    for copy in coming:
        copy.wait()
    going = []
    for i in range(span // step):
        cols = slice(i * step, (i + 1) * step)
        total = terms[0, :, cols].astype(F32) + terms[1, :, cols].astype(F32)
        total = total + terms[2, :, cols].astype(F32)
        turned[cols, :] = total.T.astype(BF16)
        going.append(
            pltpu.make_async_copy(turned.at[cols, :], out.at[0, part, cols, :], sems.at[4 + i])
        )
        going[-1].start()
    for copy in going:
        copy.wait()


def share(part, keep, first, seconds, into=None):
    width, span = keep.shape[0], keep.shape[1] // 2
    given = [] if into is None else [into]
    return pl.pallas_call(
        functools.partial(share_body, part, len(seconds)),
        in_specs=[ANY] * (2 + len(seconds) + len(given)),
        out_specs=ANY,
        out_shape=bf16(1, 2, span, width),
        scratch_shapes=[
            pltpu.VMEM((3, width, span), BF16),
            pltpu.VMEM((span, width), BF16),
            pltpu.SemaphoreType.DMA((4 + 2 * span // TILE,)),
        ],
        input_output_aliases={2 + len(seconds): 0} if given else {},
        compiler_params=pltpu.CompilerParams(vmem_limit_bytes=40 * 1024 * 1024),
        cost_estimate=LITTLE,
    )(keep, first, *seconds, *given)


def place_body(core, *refs):
    parts, out, sems = refs[:4], refs[4], refs[5]
    half, span = parts[0].shape
    low = pl.multiple_of(core[0] * half, half)
    high = pl.multiple_of((1 - core[0]) * half, half)
    copies = []
    for i, part in enumerate(parts):
        rows = pl.ds(low if i < 2 else high, half)
        cols = slice(i % 2 * span, (i % 2 + 1) * span)
        copies.append(pltpu.make_async_copy(part, out.at[0, rows, cols], sems.at[i]))
        copies[-1].start()
    for copy in copies:
        copy.wait()


def place(core, mine, theirs):
    half, span = mine[0].shape
    return pl.pallas_call(
        place_body,
        in_specs=[SCALARS] + [WHOLE] * 4,
        out_specs=pl.BlockSpec(memory_space=pl.ANY),
        out_shape=bf16(1, 2 * half, 2 * span),
        scratch_shapes=[pltpu.SemaphoreType.DMA((4,))],
        compiler_params=pltpu.CompilerParams(vmem_limit_bytes=4 * 1024 * 1024),
        cost_estimate=LITTLE,
    )(core[None], *mine, *theirs)


def load_body(*refs):
    count = len(refs) // 2
    sems = refs[-1]
    copies = [
        pltpu.make_async_copy(refs[i], refs[count + i], sems.at[i]) for i in range(count)
    ]
    for copy in copies:
        copy.start()
    for copy in copies:
        copy.wait()


def load(*arrays):
    return pl.pallas_call(
        load_body,
        in_specs=[pl.BlockSpec(memory_space=pl.ANY)] * len(arrays),
        out_specs=[WHOLE] * len(arrays),
        out_shape=[bf16(*array.shape) for array in arrays],
        scratch_shapes=[pltpu.SemaphoreType.DMA((len(arrays),))],
        compiler_params=pltpu.CompilerParams(vmem_limit_bytes=4 * 1024 * 1024),
        cost_estimate=LITTLE,
    )(*arrays)


def encoder_body(low, left, kg, vg, w, *refs):
    moved, outs = refs[:-2], refs[-2:]
    half = outs[0].shape[0]
    rows = slice(low, low + 2 * half)
    for i in range(outs[0].shape[1] // TILE):
        cols = slice(i * TILE, (i + 1) * TILE)
        from_w = slice(left + i * TILE, left + (i + 1) * TILE)
        total = lax.dot_general(kg[rows, :], w[0, 0, from_w, :], NT, preferred_element_type=F32)
        total = total + lax.dot_general(
            vg[rows, :], w[0, 1, from_w, :], NT, preferred_element_type=F32
        )
        for j, out in enumerate(outs):
            part = total[j * half : (j + 1) * half]
            if moved:
                part = part + moved[j][:, cols].astype(F32)
            out[:, cols] = part.astype(BF16)


def encoder_part(key_grad, value_grad, kv_weight, side, columns, moved=(), after=()):
    rows, depth = key_grad.shape[0] // 4, kv_weight.shape[2] // 2
    return call(
        functools.partial(encoder_body, 2 * side * rows, columns * depth),
        [key_grad, value_grad, kv_weight, *moved],
        [bf16(rows, depth)] * 2,
        after=after,
        room=12,
    )


def add_body(held, came, stay, out):
    half = stay.shape[0]
    for i in range(held.shape[1] // TILE):
        cols = slice(i * TILE, (i + 1) * TILE)
        total = held[:, cols].astype(F32) + came[:, cols].astype(F32)
        stay[:, cols] = total[:half]
        out[:, cols] = total[half:].astype(BF16)


def add(held, came, after=()):
    rows, span = held.shape
    shapes = [jax.ShapeDtypeStruct((rows // 2, span), F32), bf16(rows // 2, span)]
    return call(add_body, [held, came], shapes, after=after, room=6)


def tie(array, *others):
    return lax.optimization_barrier((array, *others))[0]


def on_device(encoded, kv_weight, queries, cotangent):
    core = lax.axis_index("tensor") % 2
    y = lax.axis_index("dp")
    block = encoded[0]
    half = block.shape[0] // 2

    one, other = y ^ 1, 3 - y
    first = jnp.where(core == 0, one, other)
    second = jnp.where(core == 0, other, one)

    def starts(*places):
        index = jnp.stack([2 * TILE * place + low for place in places for low in (0, TILE)])
        return index.astype(jnp.int32)

    own = lax.dynamic_slice_in_dim(block, core * half, half, 0)
    too = lax.dynamic_slice_in_dim(block, (1 - core) * half, half, 0)
    own, too, go, stay = lax.optimization_barrier(
        (own, too, starts(first, (y + 2) % 4), starts(second, y))
    )
    h, h_too = {"o": own}, {"o": too}
    g, g_too = {}, {}
    h["a"] = send(h["o"], X_FIRST)
    h["b"] = send(h["o"], X_SECOND)
    g["o"] = send(h["o"], ALONG_Z)
    kv_weight, queries, cotangent = load(kv_weight, queries, cotangent)
    g["a"] = send(tie(h["a"], kv_weight, queries), ALONG_Z)
    h["d"] = send(h["a"], X_SECOND)
    g["b"] = send(h["b"], ALONG_Z)
    g["d"] = send(h["a"], DIAGONAL)
    h_too["a"] = send(h["a"], SWAP)
    h_too["b"] = send(h["b"], SWAP)
    g_too["o"] = send(g["o"], SWAP)
    done = [project((h["o"], h_too["o"], h["a"], h_too["a"]), kv_weight)]
    done.append(project((g["o"], g_too["o"], h["b"], h_too["b"]), kv_weight))
    h_too["d"] = send(tie(h["d"], done[0][0]), SWAP)
    g_too["a"] = send(tie(g["a"], done[1][0]), SWAP)
    done.append(project((g["a"], g_too["a"], h["d"], h_too["d"]), kv_weight))
    g_too["b"] = send(g["b"], SWAP)
    g_too["d"] = send(tie(g["d"], done[2][0]), SWAP)
    done.append(project((g["b"], g_too["b"], g["d"], g_too["d"]), kv_weight))
    keys, values = zip(*done)
    order = ["ho", "go", "hb", "gb", "ha", "ga", "hd", "gd"]
    pieces = [{"h": h, "g": g}[name[0]][name[1]] for name in order]
    pieces += [{"h": h_too, "g": g_too}[name[0]][name[1]] for name in order]

    inputs = (queries, cotangent, keys, values)
    attended, probs, value_grad, value_grad_t = forward(*inputs)
    value_out = weight_part(go, value_grad_t, pieces)
    query_grad, key_grad, key_grad_t = backward(*inputs, attended, probs, (value_out,))

    grads = (key_grad, value_grad, kv_weight)
    moved = [[send(part, SWAP) for part in encoder_part(*grads, 1, i)] for i in range(2)]
    kept, x_out = zip(*[encoder_part(*grads, 0, i, moved[i]) for i in range(2)])
    key_out = weight_part(go, key_grad_t, pieces, x_out)
    value_keep = weight_part(stay, value_grad_t, pieces, (key_out,))
    key_keep = weight_part(stay, key_grad_t, pieces, (value_keep,))

    def onward(keep, moved):
        span = keep.shape[1] // 2
        return (keep[:, :span].astype(F32) + moved[:, span:].astype(F32)).astype(BF16)

    value_in = send(value_out, Y_FIRST)
    key_in = send(tie(key_out, value_in), Y_FIRST)

    def last_two(part):
        one, two = jnp.split(part, 2, 1)
        one = send(one, Y_SECOND)
        return [one, send(tie(two, one), Y_SECOND)]

    value_two = last_two(tie(onward(value_keep, value_in), key_in))
    key_two = last_two(onward(key_keep, key_in))

    mine, theirs = [], []
    for keep, out in zip(kept, x_out):
        held, going = add(keep, send(out, X_FIRST), (key_keep,))
        total = held + send(going, X_SECOND).astype(F32)
        here = total[:half] + send(total[half:].astype(BF16), BACK_Z).astype(F32)
        here = here.astype(BF16)
        came = send(here, ACROSS_Z)
        mine.append((here.astype(F32) + came.astype(F32)).astype(BF16))
        theirs.append(send(mine[-1], SWAP))
    enc_grad = place(core, mine, theirs)

    weight_grad = share(1, value_keep, value_in, value_two)
    weight_grad = share(0, key_keep, key_in, key_two, weight_grad)
    return (attended, query_grad, enc_grad, weight_grad)


def solution(mesh):
    return jax.shard_map(
        on_device,
        mesh=mesh,
        in_specs=(
            P("dp", "pipe", None),
            P("pipe", None, None, "tensor"),
            P("dp", "pipe", None, "tensor"),
            P("dp", "pipe", None, "tensor"),
        ),
        out_specs=(
            P("dp", "pipe", None, "tensor"),
            P("dp", "pipe", None, "tensor"),
            P("dp", "pipe", None),
            P("pipe", None, "dp", "tensor"),
        ),
        check_vma=False,
    )
```

```python
import functools

import jax
import jax.numpy as jnp
from jax import lax
from jax.experimental import pallas as pl
from jax.experimental.pallas import tpu as pltpu
from jax.sharding import PartitionSpec as P

HEAD_DIM = 256
ALL = ("pipe", "tensor", "dp")
F32, BF16 = jnp.float32, jnp.bfloat16
NT = (((1,), (1,)), ((), ()))
TN = (((0,), (0,)), ((), ()))
TILE = 512
WHOLE = pl.BlockSpec(memory_space=pltpu.VMEM)
ANY = pl.BlockSpec(memory_space=pl.ANY)
SCALARS = pl.BlockSpec(memory_space=pltpu.SMEM)


LITTLE = pl.CostEstimate(flops=1000, bytes_accessed=1000, transcendentals=0)


def call(body, operands, shapes, scratch=(), index=0, after=(), room=8):
    many = isinstance(shapes, (list, tuple))
    count = len(operands)
    operands = [*operands, *after]

    def reads(*refs):
        body(*refs[:count], *refs[count + len(after) :])

    return pl.pallas_call(
        reads,
        in_specs=[SCALARS] * index
        + [WHOLE] * (count - index)
        + [pl.BlockSpec(memory_space=pl.ANY)] * len(after),
        out_specs=[WHOLE] * len(shapes) if many else WHOLE,
        out_shape=shapes,
        scratch_shapes=scratch,
        compiler_params=pltpu.CompilerParams(vmem_limit_bytes=room * 1024 * 1024),
        cost_estimate=LITTLE,
    )(*operands)


def bf16(*shape):
    return jax.ShapeDtypeStruct(shape, BF16)


def pairs(move):
    def index(x, y, z, core):
        pipe = (z % 2) * 4 + x
        tensor = (z // 2) * 2 + core
        return (pipe * 4 + tensor) * 4 + y

    found = []
    for x in range(4):
        for y in range(4):
            for z in range(4):
                for core in range(2):
                    to_x, to_y, to_z, to_core = move(x, y, z, core)
                    found.append((index(x, y, z, core), index(to_x, to_y, to_z % 4, to_core)))
    return found


def partner(place, core, which):
    return place ^ 1 if core == which else 3 - place


X_FIRST = pairs(lambda x, y, z, core: (partner(x, core, 0), y, z, core))
X_SECOND = pairs(lambda x, y, z, core: (partner(x, core, 1), y, z, core))
Y_FIRST = pairs(lambda x, y, z, core: (x, partner(y, core, 0), z, core))
Y_SECOND = pairs(lambda x, y, z, core: (x, partner(y, core, 1), z, core))
ALONG_Z = pairs(lambda x, y, z, core: (x, y, z + 1 - 2 * core, core))
BACK_Z = pairs(lambda x, y, z, core: (x, y, z - 1 + 2 * core, core))
ACROSS_Z = pairs(lambda x, y, z, core: (x, y, z + 2, core))
SWAP = pairs(lambda x, y, z, core: (x, y, z, 1 - core))


def send(array, route):
    return lax.ppermute(array, ALL, route)


def project_body(a, b, c, d, w, keys, values):
    x = jnp.concatenate([a[...], b[...], c[...], d[...]], 0)
    keys[...] = jnp.dot(x, w[0, 0], preferred_element_type=F32).astype(BF16)
    values[...] = jnp.dot(x, w[0, 1], preferred_element_type=F32).astype(BF16)


def project(pieces, kv_weight):
    shape = bf16(4 * pieces[0].shape[0], kv_weight.shape[3])
    return call(project_body, [*pieces, kv_weight], [shape, shape])


def arrange(groups):
    quarter = groups[0].shape[0] // 4

    def at(group, place):
        return groups[group][place * quarter : (place + 1) * quarter, :]

    order = [(0, 0), (1, 0), (1, 2), (3, 0), (0, 2), (2, 0), (2, 2), (3, 2)]
    return jnp.concatenate(
        [at(g, p) for g, p in order] + [at(g, p + 1) for g, p in order], 0
    )


def forward_body(q, g, k0, k1, k2, k3, v0, v1, v2, v3, att, probs_out, vg, vgt, low):
    scale = HEAD_DIM ** (-0.5)
    total = q.shape[2]
    chunk = total // 2
    for head in range(q.shape[3] // HEAD_DIM):
        cols = slice(head * HEAD_DIM, (head + 1) * HEAD_DIM)
        k = arrange([ref[:, cols] for ref in (k0, k1, k2, k3)])
        v = arrange([ref[:, cols] for ref in (v0, v1, v2, v3)])
        for part in range(2):
            rows = slice(part * chunk, (part + 1) * chunk)
            scores = scale * lax.dot_general(
                q[0, 0, rows, cols], k, NT, preferred_element_type=F32
            )
            expd = jnp.exp(scores - jnp.max(scores, axis=-1, keepdims=True))
            probs = expd * (1.0 / jnp.sum(expd, axis=-1, keepdims=True))
            probs_out[head, rows, :] = probs
            probs_low = probs.astype(BF16)
            low[head, rows, :] = probs_low
            att[0, 0, rows, cols] = jnp.dot(
                probs_low, v, preferred_element_type=F32
            ).astype(BF16)
        value_t = lax.dot_general(g[0, 0, :, cols], low[head], TN, preferred_element_type=F32)
        vgt[cols, :] = value_t.astype(BF16)
        vg[:, cols] = value_t.T.astype(BF16)


def backward_body(q, g, k0, k1, k2, k3, v0, v1, v2, v3, att, probs, dq, kg, kgt, dlow):
    scale = HEAD_DIM ** (-0.5)
    total = q.shape[2]
    chunk = total // 2
    for head in range(q.shape[3] // HEAD_DIM):
        cols = slice(head * HEAD_DIM, (head + 1) * HEAD_DIM)
        k = arrange([ref[:, cols] for ref in (k0, k1, k2, k3)])
        v = arrange([ref[:, cols] for ref in (v0, v1, v2, v3)])
        for part in range(2):
            rows = slice(part * chunk, (part + 1) * chunk)
            g_rows = g[0, 0, rows, cols]
            dprobs = lax.dot_general(g_rows, v, NT, preferred_element_type=F32)
            delta = jnp.sum(
                g_rows.astype(F32) * att[0, 0, rows, cols].astype(F32), axis=-1, keepdims=True
            )
            ds_low = (probs[head, rows, :] * (dprobs - delta)).astype(BF16)
            dlow[head, rows, :] = ds_low
            dq[0, 0, rows, cols] = (
                scale * jnp.dot(ds_low, k, preferred_element_type=F32)
            ).astype(BF16)
        key_t = scale * lax.dot_general(
            q[0, 0, :, cols], dlow[head], TN, preferred_element_type=F32
        )
        kgt[cols, :] = key_t.astype(BF16)
        kg[:, cols] = key_t.T.astype(BF16)


def forward(queries, cotangent, keys, values):
    _, _, total, width = queries.shape
    span, heads = 4 * keys[0].shape[0], width // HEAD_DIM
    return call(
        forward_body,
        [queries, cotangent, *keys, *values],
        [
            bf16(*queries.shape),
            jax.ShapeDtypeStruct((heads, total, span), F32),
            bf16(span, width),
            bf16(width, span),
        ],
        [pltpu.VMEM((heads, total, span), BF16)],
        room=12,
    )


def backward(queries, cotangent, keys, values, attended, probs, after):
    _, _, total, width = queries.shape
    span, heads = 4 * keys[0].shape[0], width // HEAD_DIM
    return call(
        backward_body,
        [queries, cotangent, *keys, *values, attended, probs],
        [bf16(*queries.shape), bf16(span, width), bf16(width, span)],
        [pltpu.VMEM((heads, total, span), BF16)],
        after=after,
        room=12,
    )


def weight_body(count, index, grad_t, *refs):
    pieces, out = refs[:count], refs[count]
    for i in range(index.shape[0]):
        start = pl.multiple_of(index[i], TILE)
        rows = jnp.concatenate([piece[:, pl.ds(start, TILE)] for piece in pieces], 0)
        out[:, i * TILE : (i + 1) * TILE] = jnp.dot(
            grad_t[...], rows, preferred_element_type=F32
        ).astype(BF16)


def weight_part(index, grad_t, pieces, after=()):
    return call(
        functools.partial(weight_body, len(pieces)),
        [index, grad_t, *pieces],
        bf16(grad_t.shape[0], index.shape[0] * TILE),
        index=1,
        after=after,
    )


def share_body(part, count, keep, first, *refs):
    seconds, (out, terms, turned, sems) = refs[:count], refs[-4:]
    span = turned.shape[0]
    step = TILE // 2
    sources = [(keep.at[:, span:], terms.at[0]), (first.at[:, :span], terms.at[1])]
    for i, second in enumerate(seconds):
        cols = slice(i * second.shape[1], (i + 1) * second.shape[1])
        sources.append((second, terms.at[2, :, cols]))
    coming = [
        pltpu.make_async_copy(source, target, sems.at[i])
        for i, (source, target) in enumerate(sources)
    ]
    for copy in coming:
        copy.start()
    for copy in coming:
        copy.wait()
    going = []
    for i in range(span // step):
        cols = slice(i * step, (i + 1) * step)
        total = terms[0, :, cols].astype(F32) + terms[1, :, cols].astype(F32)
        total = total + terms[2, :, cols].astype(F32)
        turned[cols, :] = total.T.astype(BF16)
        going.append(
            pltpu.make_async_copy(turned.at[cols, :], out.at[0, part, cols, :], sems.at[4 + i])
        )
        going[-1].start()
    for copy in going:
        copy.wait()


def share(part, keep, first, seconds, into=None):
    width, span = keep.shape[0], keep.shape[1] // 2
    given = [] if into is None else [into]
    return pl.pallas_call(
        functools.partial(share_body, part, len(seconds)),
        in_specs=[ANY] * (2 + len(seconds) + len(given)),
        out_specs=ANY,
        out_shape=bf16(1, 2, span, width),
        scratch_shapes=[
            pltpu.VMEM((3, width, span), BF16),
            pltpu.VMEM((span, width), BF16),
            pltpu.SemaphoreType.DMA((4 + 2 * span // TILE,)),
        ],
        input_output_aliases={2 + len(seconds): 0} if given else {},
        compiler_params=pltpu.CompilerParams(vmem_limit_bytes=40 * 1024 * 1024),
        cost_estimate=LITTLE,
    )(keep, first, *seconds, *given)


def place_body(core, *refs):
    parts, out, sems = refs[:4], refs[4], refs[5]
    half, span = parts[0].shape
    low = pl.multiple_of(core[0] * half, half)
    high = pl.multiple_of((1 - core[0]) * half, half)
    copies = []
    for i, part in enumerate(parts):
        rows = pl.ds(low if i < 2 else high, half)
        cols = slice(i % 2 * span, (i % 2 + 1) * span)
        copies.append(pltpu.make_async_copy(part, out.at[0, rows, cols], sems.at[i]))
        copies[-1].start()
    for copy in copies:
        copy.wait()


def place(core, mine, theirs):
    half, span = mine[0].shape
    return pl.pallas_call(
        place_body,
        in_specs=[SCALARS] + [WHOLE] * 4,
        out_specs=pl.BlockSpec(memory_space=pl.ANY),
        out_shape=bf16(1, 2 * half, 2 * span),
        scratch_shapes=[pltpu.SemaphoreType.DMA((4,))],
        compiler_params=pltpu.CompilerParams(vmem_limit_bytes=4 * 1024 * 1024),
        cost_estimate=LITTLE,
    )(core[None], *mine, *theirs)


def load_body(*refs):
    count = len(refs) // 2
    sems = refs[-1]
    copies = [
        pltpu.make_async_copy(refs[i], refs[count + i], sems.at[i]) for i in range(count)
    ]
    for copy in copies:
        copy.start()
    for copy in copies:
        copy.wait()


def load(*arrays):
    return pl.pallas_call(
        load_body,
        in_specs=[pl.BlockSpec(memory_space=pl.ANY)] * len(arrays),
        out_specs=[WHOLE] * len(arrays),
        out_shape=[bf16(*array.shape) for array in arrays],
        scratch_shapes=[pltpu.SemaphoreType.DMA((len(arrays),))],
        compiler_params=pltpu.CompilerParams(vmem_limit_bytes=4 * 1024 * 1024),
        cost_estimate=LITTLE,
    )(*arrays)


def encoder_body(low, left, kg, vg, w, *refs):
    moved, outs = refs[:-2], refs[-2:]
    half = outs[0].shape[0]
    rows = slice(low, low + 2 * half)
    for i in range(outs[0].shape[1] // TILE):
        cols = slice(i * TILE, (i + 1) * TILE)
        from_w = slice(left + i * TILE, left + (i + 1) * TILE)
        total = lax.dot_general(kg[rows, :], w[0, 0, from_w, :], NT, preferred_element_type=F32)
        total = total + lax.dot_general(
            vg[rows, :], w[0, 1, from_w, :], NT, preferred_element_type=F32
        )
        for j, out in enumerate(outs):
            part = total[j * half : (j + 1) * half]
            if moved:
                part = part + moved[j][:, cols].astype(F32)
            out[:, cols] = part.astype(BF16)


def encoder_part(key_grad, value_grad, kv_weight, side, columns, moved=(), after=()):
    rows, depth = key_grad.shape[0] // 4, kv_weight.shape[2] // 2
    return call(
        functools.partial(encoder_body, 2 * side * rows, columns * depth),
        [key_grad, value_grad, kv_weight, *moved],
        [bf16(rows, depth)] * 2,
        after=after,
        room=12,
    )


def add_body(held, came, stay, out):
    half = stay.shape[0]
    for i in range(held.shape[1] // TILE):
        cols = slice(i * TILE, (i + 1) * TILE)
        total = held[:, cols].astype(F32) + came[:, cols].astype(F32)
        stay[:, cols] = total[:half]
        out[:, cols] = total[half:].astype(BF16)


def add(held, came, after=()):
    rows, span = held.shape
    shapes = [jax.ShapeDtypeStruct((rows // 2, span), F32), bf16(rows // 2, span)]
    return call(add_body, [held, came], shapes, after=after, room=6)


def tie(array, *others):
    return lax.optimization_barrier((array, *others))[0]


def on_device(encoded, kv_weight, queries, cotangent):
    core = lax.axis_index("tensor") % 2
    y = lax.axis_index("dp")
    block = encoded[0]
    half = block.shape[0] // 2

    one, other = y ^ 1, 3 - y
    first = jnp.where(core == 0, one, other)
    second = jnp.where(core == 0, other, one)

    def starts(*places):
        index = jnp.stack([2 * TILE * place + low for place in places for low in (0, TILE)])
        return index.astype(jnp.int32)

    own = lax.dynamic_slice_in_dim(block, core * half, half, 0)
    too = lax.dynamic_slice_in_dim(block, (1 - core) * half, half, 0)
    own, too, go, stay = lax.optimization_barrier(
        (own, too, starts(first, (y + 2) % 4), starts(second, y))
    )
    h, h_too = {"o": own}, {"o": too}
    g, g_too = {}, {}
    h["a"] = send(h["o"], X_FIRST)
    h["b"] = send(h["o"], X_SECOND)
    g["o"] = send(h["o"], ALONG_Z)
    kv_weight, queries, cotangent = load(kv_weight, queries, cotangent)
    g["a"] = send(tie(h["a"], kv_weight, queries), ALONG_Z)
    h["d"] = send(h["a"], X_SECOND)
    g["d"] = send(g["a"], X_SECOND)
    h_too["a"] = send(h["a"], SWAP)
    h_too["b"] = send(h["b"], SWAP)
    g_too["o"] = send(g["o"], SWAP)
    h_too["d"] = send(h["d"], SWAP)
    g_too["a"] = send(g["a"], SWAP)
    done = [project((h["o"], h_too["o"], h["a"], h_too["a"]), kv_weight)]
    g["b"] = send(tie(h["b"], g["a"], done[0][0]), ALONG_Z)
    done.append(project((g["o"], g_too["o"], h["b"], h_too["b"]), kv_weight))
    done.append(project((g["a"], g_too["a"], h["d"], h_too["d"]), kv_weight))
    g_too["b"] = send(tie(g["b"], done[1][0]), SWAP)
    g_too["d"] = send(tie(g["d"], done[2][0]), SWAP)
    done.append(project((g["b"], g_too["b"], g["d"], g_too["d"]), kv_weight))
    keys, values = zip(*done)
    order = ["ho", "go", "hb", "gb", "ha", "ga", "hd", "gd"]
    pieces = [{"h": h, "g": g}[name[0]][name[1]] for name in order]
    pieces += [{"h": h_too, "g": g_too}[name[0]][name[1]] for name in order]

    inputs = (queries, cotangent, keys, values)
    attended, probs, value_grad, value_grad_t = forward(*inputs)
    value_out = weight_part(go, value_grad_t, pieces)
    query_grad, key_grad, key_grad_t = backward(*inputs, attended, probs, (value_out,))

    grads = (key_grad, value_grad, kv_weight)
    moved = [[send(part, SWAP) for part in encoder_part(*grads, 1, i)] for i in range(2)]
    kept, x_out = zip(*[encoder_part(*grads, 0, i, moved[i]) for i in range(2)])
    key_out = weight_part(go, key_grad_t, pieces, x_out)
    value_keep = weight_part(stay, value_grad_t, pieces, (key_out,))
    key_keep = weight_part(stay, key_grad_t, pieces, (value_keep,))

    def onward(keep, moved):
        span = keep.shape[1] // 2
        return (keep[:, :span].astype(F32) + moved[:, span:].astype(F32)).astype(BF16)

    value_in = send(value_out, Y_FIRST)
    key_in = send(tie(key_out, value_in), Y_FIRST)

    def last_two(part):
        one, two = jnp.split(part, 2, 1)
        one = send(one, Y_SECOND)
        return [one, send(tie(two, one), Y_SECOND)]

    value_two = last_two(tie(onward(value_keep, value_in), key_in))
    key_two = last_two(onward(key_keep, key_in))

    mine, theirs = [], []
    for keep, out in zip(kept, x_out):
        held, going = add(keep, send(out, X_FIRST), (key_keep,))
        if mine:
            held = tie(held, key_in)
        total = held + send(going, X_SECOND).astype(F32)
        here = total[:half] + send(total[half:].astype(BF16), BACK_Z).astype(F32)
        here = here.astype(BF16)
        came = send(here, ACROSS_Z)
        mine.append((here.astype(F32) + came.astype(F32)).astype(BF16))
        theirs.append(send(mine[-1], SWAP))
    enc_grad = place(core, mine, theirs)

    weight_grad = share(1, value_keep, value_in, value_two)
    weight_grad = share(0, key_keep, key_in, key_two, weight_grad)
    return (attended, query_grad, enc_grad, weight_grad)


def solution(mesh):
    return jax.shard_map(
        on_device,
        mesh=mesh,
        in_specs=(
            P("dp", "pipe", None),
            P("pipe", None, None, "tensor"),
            P("dp", "pipe", None, "tensor"),
            P("dp", "pipe", None, "tensor"),
        ),
        out_specs=(
            P("dp", "pipe", None, "tensor"),
            P("dp", "pipe", None, "tensor"),
            P("dp", "pipe", None),
            P("pipe", None, "dp", "tensor"),
        ),
        check_vma=False,
    )
```

```python
import functools

import jax
import jax.numpy as jnp
from jax import lax
from jax.experimental import pallas as pl
from jax.experimental.pallas import tpu as pltpu
from jax.sharding import PartitionSpec as P

HEAD_DIM = 256
ALL = ("pipe", "tensor", "dp")
F32, BF16 = jnp.float32, jnp.bfloat16
NT = (((1,), (1,)), ((), ()))
TN = (((0,), (0,)), ((), ()))
TILE = 512
WHOLE = pl.BlockSpec(memory_space=pltpu.VMEM)
ANY = pl.BlockSpec(memory_space=pl.ANY)
SCALARS = pl.BlockSpec(memory_space=pltpu.SMEM)


LITTLE = pl.CostEstimate(flops=1000, bytes_accessed=1000, transcendentals=0)


def call(body, operands, shapes, scratch=(), index=0, after=(), room=8):
    many = isinstance(shapes, (list, tuple))
    count = len(operands)
    operands = [*operands, *after]

    def reads(*refs):
        body(*refs[:count], *refs[count + len(after) :])

    return pl.pallas_call(
        reads,
        in_specs=[SCALARS] * index
        + [WHOLE] * (count - index)
        + [pl.BlockSpec(memory_space=pl.ANY)] * len(after),
        out_specs=[WHOLE] * len(shapes) if many else WHOLE,
        out_shape=shapes,
        scratch_shapes=scratch,
        compiler_params=pltpu.CompilerParams(vmem_limit_bytes=room * 1024 * 1024),
        cost_estimate=LITTLE,
    )(*operands)


def bf16(*shape):
    return jax.ShapeDtypeStruct(shape, BF16)


def pairs(move):
    def index(x, y, z, core):
        pipe = (z % 2) * 4 + x
        tensor = (z // 2) * 2 + core
        return (pipe * 4 + tensor) * 4 + y

    found = []
    for x in range(4):
        for y in range(4):
            for z in range(4):
                for core in range(2):
                    to_x, to_y, to_z, to_core = move(x, y, z, core)
                    found.append((index(x, y, z, core), index(to_x, to_y, to_z % 4, to_core)))
    return found


def partner(place, core, which):
    return place ^ 1 if core == which else 3 - place


X_FIRST = pairs(lambda x, y, z, core: (partner(x, core, 0), y, z, core))
X_SECOND = pairs(lambda x, y, z, core: (partner(x, core, 1), y, z, core))
Y_FIRST = pairs(lambda x, y, z, core: (x, partner(y, core, 0), z, core))
Y_SECOND = pairs(lambda x, y, z, core: (x, partner(y, core, 1), z, core))
ALONG_Z = pairs(lambda x, y, z, core: (x, y, z + 1 - 2 * core, core))
BACK_Z = pairs(lambda x, y, z, core: (x, y, z - 1 + 2 * core, core))
ACROSS_Z = pairs(lambda x, y, z, core: (x, y, z + 2, core))
SWAP = pairs(lambda x, y, z, core: (x, y, z, 1 - core))


def send(array, route):
    return lax.ppermute(array, ALL, route)


def project_body(a, b, c, d, w, keys, values):
    x = jnp.concatenate([a[...], b[...], c[...], d[...]], 0)
    keys[...] = jnp.dot(x, w[0, 0], preferred_element_type=F32).astype(BF16)
    values[...] = jnp.dot(x, w[0, 1], preferred_element_type=F32).astype(BF16)


def project(pieces, kv_weight):
    shape = bf16(4 * pieces[0].shape[0], kv_weight.shape[3])
    return call(project_body, [*pieces, kv_weight], [shape, shape])


def arrange(groups):
    quarter = groups[0].shape[0] // 4

    def at(group, place):
        return groups[group][place * quarter : (place + 1) * quarter, :]

    order = [(0, 0), (1, 0), (1, 2), (3, 0), (0, 2), (2, 0), (2, 2), (3, 2)]
    return jnp.concatenate(
        [at(g, p) for g, p in order] + [at(g, p + 1) for g, p in order], 0
    )


def forward_body(q, g, k0, k1, k2, k3, v0, v1, v2, v3, att, probs_out, vg, vgt, low):
    scale = HEAD_DIM ** (-0.5)
    total = q.shape[2]
    chunk = total // 2
    for head in range(q.shape[3] // HEAD_DIM):
        cols = slice(head * HEAD_DIM, (head + 1) * HEAD_DIM)
        k = arrange([ref[:, cols] for ref in (k0, k1, k2, k3)])
        v = arrange([ref[:, cols] for ref in (v0, v1, v2, v3)])
        for part in range(2):
            rows = slice(part * chunk, (part + 1) * chunk)
            scores = scale * lax.dot_general(
                q[0, 0, rows, cols], k, NT, preferred_element_type=F32
            )
            expd = jnp.exp(scores - jnp.max(scores, axis=-1, keepdims=True))
            probs = expd * (1.0 / jnp.sum(expd, axis=-1, keepdims=True))
            probs_out[head, rows, :] = probs
            probs_low = probs.astype(BF16)
            low[head, rows, :] = probs_low
            att[0, 0, rows, cols] = jnp.dot(
                probs_low, v, preferred_element_type=F32
            ).astype(BF16)
        value_t = lax.dot_general(g[0, 0, :, cols], low[head], TN, preferred_element_type=F32)
        vgt[cols, :] = value_t.astype(BF16)
        vg[:, cols] = value_t.T.astype(BF16)


def backward_body(q, g, k0, k1, k2, k3, v0, v1, v2, v3, att, probs, dq, kg, kgt, dlow):
    scale = HEAD_DIM ** (-0.5)
    total = q.shape[2]
    chunk = total // 2
    for head in range(q.shape[3] // HEAD_DIM):
        cols = slice(head * HEAD_DIM, (head + 1) * HEAD_DIM)
        k = arrange([ref[:, cols] for ref in (k0, k1, k2, k3)])
        v = arrange([ref[:, cols] for ref in (v0, v1, v2, v3)])
        for part in range(2):
            rows = slice(part * chunk, (part + 1) * chunk)
            g_rows = g[0, 0, rows, cols]
            dprobs = lax.dot_general(g_rows, v, NT, preferred_element_type=F32)
            delta = jnp.sum(
                g_rows.astype(F32) * att[0, 0, rows, cols].astype(F32), axis=-1, keepdims=True
            )
            ds_low = (probs[head, rows, :] * (dprobs - delta)).astype(BF16)
            dlow[head, rows, :] = ds_low
            dq[0, 0, rows, cols] = (
                scale * jnp.dot(ds_low, k, preferred_element_type=F32)
            ).astype(BF16)
        key_t = scale * lax.dot_general(
            q[0, 0, :, cols], dlow[head], TN, preferred_element_type=F32
        )
        kgt[cols, :] = key_t.astype(BF16)
        kg[:, cols] = key_t.T.astype(BF16)


def forward(queries, cotangent, keys, values):
    _, _, total, width = queries.shape
    span, heads = 4 * keys[0].shape[0], width // HEAD_DIM
    return call(
        forward_body,
        [queries, cotangent, *keys, *values],
        [
            bf16(*queries.shape),
            jax.ShapeDtypeStruct((heads, total, span), F32),
            bf16(span, width),
            bf16(width, span),
        ],
        [pltpu.VMEM((heads, total, span), BF16)],
        room=12,
    )


def backward(queries, cotangent, keys, values, attended, probs, after):
    _, _, total, width = queries.shape
    span, heads = 4 * keys[0].shape[0], width // HEAD_DIM
    return call(
        backward_body,
        [queries, cotangent, *keys, *values, attended, probs],
        [bf16(*queries.shape), bf16(span, width), bf16(width, span)],
        [pltpu.VMEM((heads, total, span), BF16)],
        after=after,
        room=12,
    )


def weight_body(count, index, grad_t, *refs):
    pieces, out = refs[:count], refs[count]
    for i in range(index.shape[0]):
        start = pl.multiple_of(index[i], TILE)
        rows = jnp.concatenate([piece[:, pl.ds(start, TILE)] for piece in pieces], 0)
        out[:, i * TILE : (i + 1) * TILE] = jnp.dot(
            grad_t[...], rows, preferred_element_type=F32
        ).astype(BF16)


def weight_part(index, grad_t, pieces, after=()):
    return call(
        functools.partial(weight_body, len(pieces)),
        [index, grad_t, *pieces],
        bf16(grad_t.shape[0], index.shape[0] * TILE),
        index=1,
        after=after,
    )


def share_body(part, tile, keep, first, second, *refs):
    out, terms, turned, sems = refs[-4:]
    span = first.shape[1] // 2
    low = tile * TILE
    sources = (keep.at[:, span + low : span + low + TILE], first.at[:, low : low + TILE], second)
    coming = [
        pltpu.make_async_copy(source, terms.at[i], sems.at[i])
        for i, source in enumerate(sources)
    ]
    for copy in coming:
        copy.start()
    for copy in coming:
        copy.wait()
    going = []
    step = TILE // 2
    for i in range(2):
        cols = slice(i * step, (i + 1) * step)
        total = terms[0, :, cols].astype(F32) + terms[1, :, cols].astype(F32)
        total = total + terms[2, :, cols].astype(F32)
        turned[cols, :] = total.T.astype(BF16)
        target = out.at[0, part, low + i * step : low + (i + 1) * step, :]
        going.append(pltpu.make_async_copy(turned.at[cols, :], target, sems.at[3 + i]))
        going[-1].start()
    for copy in going:
        copy.wait()


def share(part, tile, keep, first, second, into=None):
    width, span = keep.shape[0], keep.shape[1] // 2
    given = [] if into is None else [into]
    return pl.pallas_call(
        functools.partial(share_body, part, tile),
        in_specs=[ANY] * (3 + len(given)),
        out_specs=ANY,
        out_shape=bf16(1, 2, span, width),
        scratch_shapes=[
            pltpu.VMEM((3, width, TILE), BF16),
            pltpu.VMEM((TILE, width), BF16),
            pltpu.SemaphoreType.DMA((5,)),
        ],
        input_output_aliases={3: 0} if given else {},
        compiler_params=pltpu.CompilerParams(vmem_limit_bytes=40 * 1024 * 1024),
        cost_estimate=LITTLE,
    )(keep, first, second, *given)


def place_body(core, *refs):
    parts, out, sems = refs[:4], refs[4], refs[5]
    half, span = parts[0].shape
    low = pl.multiple_of(core[0] * half, half)
    high = pl.multiple_of((1 - core[0]) * half, half)
    copies = []
    for i, part in enumerate(parts):
        rows = pl.ds(low if i < 2 else high, half)
        cols = slice(i % 2 * span, (i % 2 + 1) * span)
        copies.append(pltpu.make_async_copy(part, out.at[0, rows, cols], sems.at[i]))
        copies[-1].start()
    for copy in copies:
        copy.wait()


def place(core, mine, theirs):
    half, span = mine[0].shape
    return pl.pallas_call(
        place_body,
        in_specs=[SCALARS] + [WHOLE] * 4,
        out_specs=pl.BlockSpec(memory_space=pl.ANY),
        out_shape=bf16(1, 2 * half, 2 * span),
        scratch_shapes=[pltpu.SemaphoreType.DMA((4,))],
        compiler_params=pltpu.CompilerParams(vmem_limit_bytes=4 * 1024 * 1024),
        cost_estimate=LITTLE,
    )(core[None], *mine, *theirs)


def load_body(*refs):
    count = len(refs) // 2
    sems = refs[-1]
    copies = [
        pltpu.make_async_copy(refs[i], refs[count + i], sems.at[i]) for i in range(count)
    ]
    for copy in copies:
        copy.start()
    for copy in copies:
        copy.wait()


def load(*arrays):
    return pl.pallas_call(
        load_body,
        in_specs=[pl.BlockSpec(memory_space=pl.ANY)] * len(arrays),
        out_specs=[WHOLE] * len(arrays),
        out_shape=[bf16(*array.shape) for array in arrays],
        scratch_shapes=[pltpu.SemaphoreType.DMA((len(arrays),))],
        compiler_params=pltpu.CompilerParams(vmem_limit_bytes=4 * 1024 * 1024),
        cost_estimate=LITTLE,
    )(*arrays)


def encoder_body(low, left, kg, vg, w, *refs):
    moved, outs = refs[:-2], refs[-2:]
    half = outs[0].shape[0]
    rows = slice(low, low + 2 * half)
    for i in range(outs[0].shape[1] // TILE):
        cols = slice(i * TILE, (i + 1) * TILE)
        from_w = slice(left + i * TILE, left + (i + 1) * TILE)
        total = lax.dot_general(kg[rows, :], w[0, 0, from_w, :], NT, preferred_element_type=F32)
        total = total + lax.dot_general(
            vg[rows, :], w[0, 1, from_w, :], NT, preferred_element_type=F32
        )
        for j, out in enumerate(outs):
            part = total[j * half : (j + 1) * half]
            if moved:
                part = part + moved[j][:, cols].astype(F32)
            out[:, cols] = part.astype(BF16)


def encoder_part(key_grad, value_grad, kv_weight, side, columns, moved=(), after=()):
    rows, depth = key_grad.shape[0] // 4, kv_weight.shape[2] // 2
    return call(
        functools.partial(encoder_body, 2 * side * rows, columns * depth),
        [key_grad, value_grad, kv_weight, *moved],
        [bf16(rows, depth)] * 2,
        after=after,
        room=12,
    )


def add_body(held, came, stay, out):
    half = stay.shape[0]
    for i in range(held.shape[1] // TILE):
        cols = slice(i * TILE, (i + 1) * TILE)
        total = held[:, cols].astype(F32) + came[:, cols].astype(F32)
        stay[:, cols] = total[:half]
        out[:, cols] = total[half:].astype(BF16)


def add(held, came, after=()):
    rows, span = held.shape
    shapes = [jax.ShapeDtypeStruct((rows // 2, span), F32), bf16(rows // 2, span)]
    return call(add_body, [held, came], shapes, after=after, room=6)


def add_first_body(held, came, out):
    out[...] = (held[: out.shape[0], :] + came[...].astype(F32)).astype(BF16)


def add_first(held, came, after):
    return call(add_first_body, [held, came], bf16(*came.shape), after=after, room=6)


def tie(array, *others):
    return lax.optimization_barrier((array, *others))[0]


def on_device(encoded, kv_weight, queries, cotangent):
    core = lax.axis_index("tensor") % 2
    y = lax.axis_index("dp")
    block = encoded[0]
    half = block.shape[0] // 2

    one, other = y ^ 1, 3 - y
    first = jnp.where(core == 0, one, other)
    second = jnp.where(core == 0, other, one)

    def starts(*places):
        index = jnp.stack([2 * TILE * place + low for place in places for low in (0, TILE)])
        return index.astype(jnp.int32)

    own = lax.dynamic_slice_in_dim(block, core * half, half, 0)
    too = lax.dynamic_slice_in_dim(block, (1 - core) * half, half, 0)
    own, too, go, stay = lax.optimization_barrier(
        (own, too, starts(first, (y + 2) % 4), starts(second, y))
    )
    h, h_too = {"o": own}, {"o": too}
    g, g_too = {}, {}
    h["a"] = send(h["o"], X_FIRST)
    h["b"] = send(h["o"], X_SECOND)
    g["o"] = send(h["o"], ALONG_Z)
    kv_weight, queries, cotangent = load(kv_weight, queries, cotangent)
    g["a"] = send(tie(h["a"], kv_weight, queries), ALONG_Z)
    h["d"] = send(h["a"], X_SECOND)
    g["d"] = send(g["a"], X_SECOND)
    h_too["a"] = send(h["a"], SWAP)
    h_too["b"] = send(h["b"], SWAP)
    g_too["o"] = send(g["o"], SWAP)
    h_too["d"] = send(h["d"], SWAP)
    g_too["a"] = send(g["a"], SWAP)
    done = [project((h["o"], h_too["o"], h["a"], h_too["a"]), kv_weight)]
    g["b"] = send(tie(h["b"], g["a"], done[0][0]), ALONG_Z)
    done.append(project((g["o"], g_too["o"], h["b"], h_too["b"]), kv_weight))
    done.append(project((g["a"], g_too["a"], h["d"], h_too["d"]), kv_weight))
    g_too["b"] = send(tie(g["b"], done[1][0]), SWAP)
    g_too["d"] = send(tie(g["d"], done[2][0]), SWAP)
    done.append(project((g["b"], g_too["b"], g["d"], g_too["d"]), kv_weight))
    keys, values = zip(*done)
    order = ["ho", "go", "hb", "gb", "ha", "ga", "hd", "gd"]
    pieces = [{"h": h, "g": g}[name[0]][name[1]] for name in order]
    pieces += [{"h": h_too, "g": g_too}[name[0]][name[1]] for name in order]

    inputs = (queries, cotangent, keys, values)
    attended, probs, value_grad, value_grad_t = forward(*inputs)
    value_out = weight_part(go, value_grad_t, pieces)
    query_grad, key_grad, key_grad_t = backward(*inputs, attended, probs, (value_out,))

    grads = (key_grad, value_grad, kv_weight)
    moved = [[send(part, SWAP) for part in encoder_part(*grads, 1, i)] for i in range(2)]
    kept, x_out = zip(*[encoder_part(*grads, 0, i, moved[i]) for i in range(2)])
    key_out = weight_part(go, key_grad_t, pieces, x_out)
    value_keep = weight_part(stay, value_grad_t, pieces, (key_out,))
    key_keep = weight_part(stay, key_grad_t, pieces, (value_keep,))

    def onward(keep, moved):
        span = keep.shape[1] // 2
        return (keep[:, :span].astype(F32) + moved[:, span:].astype(F32)).astype(BF16)

    value_in = send(value_out, Y_FIRST)
    key_in = send(tie(key_out, value_in), Y_FIRST)

    def last_two(part):
        one, two = jnp.split(part, 2, 1)
        one = send(one, Y_SECOND)
        return [one, send(tie(two, one), Y_SECOND)]

    value_two = last_two(tie(onward(value_keep, value_in), key_in))
    key_two = last_two(onward(key_keep, key_in))

    mine, theirs = [], []
    for keep, out in zip(kept, x_out):
        if mine:
            held, going = add(keep, send(out, X_FIRST), (key_keep,))
        else:
            held = tie(keep, key_keep).astype(F32) + send(out, X_FIRST).astype(F32)
            held, going = held[: 2 * half], held[2 * half :].astype(BF16)
        if mine:
            held = tie(held, key_in)
        total = held + send(going, X_SECOND).astype(F32)
        came = send(total[half:].astype(BF16), BACK_Z)
        if mine:
            here = (total[:half] + came.astype(F32)).astype(BF16)
        else:
            here = add_first(total, came, (key_in,))
        came = send(here, ACROSS_Z)
        mine.append((here.astype(F32) + came.astype(F32)).astype(BF16))
        theirs.append(send(mine[-1], SWAP))
    enc_grad = place(core, mine, theirs)

    weight_grad = None
    terms = ((1, value_keep, value_in, value_two), (0, key_keep, key_in, key_two))
    for part, keep, one, two in terms:
        for tile in range(2):
            weight_grad = share(part, tile, keep, one, two[tile], weight_grad)
    return (attended, query_grad, enc_grad, weight_grad)


def solution(mesh):
    return jax.shard_map(
        on_device,
        mesh=mesh,
        in_specs=(
            P("dp", "pipe", None),
            P("pipe", None, None, "tensor"),
            P("dp", "pipe", None, "tensor"),
            P("dp", "pipe", None, "tensor"),
        ),
        out_specs=(
            P("dp", "pipe", None, "tensor"),
            P("dp", "pipe", None, "tensor"),
            P("dp", "pipe", None),
            P("pipe", None, "dp", "tensor"),
        ),
        check_vma=False,
    )
```

```python
import functools

import jax
import jax.numpy as jnp
from jax import lax
from jax.experimental import pallas as pl
from jax.experimental.pallas import tpu as pltpu
from jax.sharding import PartitionSpec as P

HEAD_DIM = 256
ALL = ("pipe", "tensor", "dp")
F32, BF16 = jnp.float32, jnp.bfloat16
NT = (((1,), (1,)), ((), ()))
TN = (((0,), (0,)), ((), ()))
TILE = 512
WHOLE = pl.BlockSpec(memory_space=pltpu.VMEM)
ANY = pl.BlockSpec(memory_space=pl.ANY)
SCALARS = pl.BlockSpec(memory_space=pltpu.SMEM)


LITTLE = pl.CostEstimate(flops=1000, bytes_accessed=1000, transcendentals=0)


def call(body, operands, shapes, scratch=(), index=0, after=(), room=8):
    many = isinstance(shapes, (list, tuple))
    count = len(operands)
    operands = [*operands, *after]

    def reads(*refs):
        body(*refs[:count], *refs[count + len(after) :])

    return pl.pallas_call(
        reads,
        in_specs=[SCALARS] * index
        + [WHOLE] * (count - index)
        + [pl.BlockSpec(memory_space=pl.ANY)] * len(after),
        out_specs=[WHOLE] * len(shapes) if many else WHOLE,
        out_shape=shapes,
        scratch_shapes=scratch,
        compiler_params=pltpu.CompilerParams(vmem_limit_bytes=room * 1024 * 1024),
        cost_estimate=LITTLE,
    )(*operands)


def bf16(*shape):
    return jax.ShapeDtypeStruct(shape, BF16)


def pairs(move):
    def index(x, y, z, core):
        pipe = (z % 2) * 4 + x
        tensor = (z // 2) * 2 + core
        return (pipe * 4 + tensor) * 4 + y

    found = []
    for x in range(4):
        for y in range(4):
            for z in range(4):
                for core in range(2):
                    to_x, to_y, to_z, to_core = move(x, y, z, core)
                    found.append((index(x, y, z, core), index(to_x, to_y, to_z % 4, to_core)))
    return found


def partner(place, core, which):
    return place ^ 1 if core == which else 3 - place


X_FIRST = pairs(lambda x, y, z, core: (partner(x, core, 0), y, z, core))
X_SECOND = pairs(lambda x, y, z, core: (partner(x, core, 1), y, z, core))
Y_FIRST = pairs(lambda x, y, z, core: (x, partner(y, core, 0), z, core))
Y_SECOND = pairs(lambda x, y, z, core: (x, partner(y, core, 1), z, core))
ALONG_Z = pairs(lambda x, y, z, core: (x, y, z + 1 - 2 * core, core))
BACK_Z = pairs(lambda x, y, z, core: (x, y, z - 1 + 2 * core, core))
ACROSS_Z = pairs(lambda x, y, z, core: (x, y, z + 2, core))
SWAP = pairs(lambda x, y, z, core: (x, y, z, 1 - core))


def send(array, route):
    return lax.ppermute(array, ALL, route)


def project_body(a, b, c, d, w, keys, values):
    x = jnp.concatenate([a[...], b[...], c[...], d[...]], 0)
    keys[...] = jnp.dot(x, w[0, 0], preferred_element_type=F32).astype(BF16)
    values[...] = jnp.dot(x, w[0, 1], preferred_element_type=F32).astype(BF16)


def project(pieces, kv_weight):
    shape = bf16(4 * pieces[0].shape[0], kv_weight.shape[3])
    return call(project_body, [*pieces, kv_weight], [shape, shape])


def arrange(groups):
    quarter = groups[0].shape[0] // 4

    def at(group, place):
        return groups[group][place * quarter : (place + 1) * quarter, :]

    order = [(0, 0), (1, 0), (1, 2), (3, 0), (0, 2), (2, 0), (2, 2), (3, 2)]
    return jnp.concatenate(
        [at(g, p) for g, p in order] + [at(g, p + 1) for g, p in order], 0
    )


def forward_body(q, g, k0, k1, k2, k3, v0, v1, v2, v3, att, probs_out, vg, vgt, low):
    scale = HEAD_DIM ** (-0.5)
    total = q.shape[2]
    chunk = total // 2
    for head in range(q.shape[3] // HEAD_DIM):
        cols = slice(head * HEAD_DIM, (head + 1) * HEAD_DIM)
        k = arrange([ref[:, cols] for ref in (k0, k1, k2, k3)])
        v = arrange([ref[:, cols] for ref in (v0, v1, v2, v3)])
        for part in range(2):
            rows = slice(part * chunk, (part + 1) * chunk)
            scores = scale * lax.dot_general(
                q[0, 0, rows, cols], k, NT, preferred_element_type=F32
            )
            expd = jnp.exp(scores - jnp.max(scores, axis=-1, keepdims=True))
            probs = expd * (1.0 / jnp.sum(expd, axis=-1, keepdims=True))
            probs_out[head, rows, :] = probs
            probs_low = probs.astype(BF16)
            low[head, rows, :] = probs_low
            att[0, 0, rows, cols] = jnp.dot(
                probs_low, v, preferred_element_type=F32
            ).astype(BF16)
        value_t = lax.dot_general(g[0, 0, :, cols], low[head], TN, preferred_element_type=F32)
        vgt[cols, :] = value_t.astype(BF16)
        vg[:, cols] = value_t.T.astype(BF16)


def backward_body(q, g, k0, k1, k2, k3, v0, v1, v2, v3, att, probs, dq, kg, kgt, dlow):
    scale = HEAD_DIM ** (-0.5)
    total = q.shape[2]
    chunk = total // 2
    for head in range(q.shape[3] // HEAD_DIM):
        cols = slice(head * HEAD_DIM, (head + 1) * HEAD_DIM)
        k = arrange([ref[:, cols] for ref in (k0, k1, k2, k3)])
        v = arrange([ref[:, cols] for ref in (v0, v1, v2, v3)])
        for part in range(2):
            rows = slice(part * chunk, (part + 1) * chunk)
            g_rows = g[0, 0, rows, cols]
            dprobs = lax.dot_general(g_rows, v, NT, preferred_element_type=F32)
            delta = jnp.sum(
                g_rows.astype(F32) * att[0, 0, rows, cols].astype(F32), axis=-1, keepdims=True
            )
            ds_low = (probs[head, rows, :] * (dprobs - delta)).astype(BF16)
            dlow[head, rows, :] = ds_low
            dq[0, 0, rows, cols] = (
                scale * jnp.dot(ds_low, k, preferred_element_type=F32)
            ).astype(BF16)
        key_t = scale * lax.dot_general(
            q[0, 0, :, cols], dlow[head], TN, preferred_element_type=F32
        )
        kgt[cols, :] = key_t.astype(BF16)
        kg[:, cols] = key_t.T.astype(BF16)


def forward(queries, cotangent, keys, values):
    _, _, total, width = queries.shape
    span, heads = 4 * keys[0].shape[0], width // HEAD_DIM
    return call(
        forward_body,
        [queries, cotangent, *keys, *values],
        [
            bf16(*queries.shape),
            jax.ShapeDtypeStruct((heads, total, span), F32),
            bf16(span, width),
            bf16(width, span),
        ],
        [pltpu.VMEM((heads, total, span), BF16)],
        room=12,
    )


def backward(queries, cotangent, keys, values, attended, probs, after):
    _, _, total, width = queries.shape
    span, heads = 4 * keys[0].shape[0], width // HEAD_DIM
    return call(
        backward_body,
        [queries, cotangent, *keys, *values, attended, probs],
        [bf16(*queries.shape), bf16(span, width), bf16(width, span)],
        [pltpu.VMEM((heads, total, span), BF16)],
        after=after,
        room=12,
    )


def weight_body(count, index, grad_t, *refs):
    pieces, out = refs[:count], refs[count]
    for i in range(index.shape[0]):
        start = pl.multiple_of(index[i], TILE)
        rows = jnp.concatenate([piece[:, pl.ds(start, TILE)] for piece in pieces], 0)
        out[:, i * TILE : (i + 1) * TILE] = jnp.dot(
            grad_t[...], rows, preferred_element_type=F32
        ).astype(BF16)


def weight_part(index, grad_t, pieces, after=()):
    return call(
        functools.partial(weight_body, len(pieces)),
        [index, grad_t, *pieces],
        bf16(grad_t.shape[0], index.shape[0] * TILE),
        index=1,
        after=after,
    )


def share_body(part, tile, keep, first, second, *refs):
    out, terms, turned, sems = refs[-4:]
    span = first.shape[1] // 2
    low = tile * TILE
    sources = (keep.at[:, span + low : span + low + TILE], first.at[:, low : low + TILE], second)
    coming = [
        pltpu.make_async_copy(source, terms.at[i], sems.at[i])
        for i, source in enumerate(sources)
    ]
    for copy in coming:
        copy.start()
    for copy in coming:
        copy.wait()
    going = []
    step = TILE // 2
    for i in range(2):
        cols = slice(i * step, (i + 1) * step)
        total = terms[0, :, cols].astype(F32) + terms[1, :, cols].astype(F32)
        total = total + terms[2, :, cols].astype(F32)
        turned[cols, :] = total.T.astype(BF16)
        target = out.at[0, part, low + i * step : low + (i + 1) * step, :]
        going.append(pltpu.make_async_copy(turned.at[cols, :], target, sems.at[3 + i]))
        going[-1].start()
    for copy in going:
        copy.wait()


def share(part, tile, keep, first, second, into=None):
    width, span = keep.shape[0], keep.shape[1] // 2
    given = [] if into is None else [into]
    return pl.pallas_call(
        functools.partial(share_body, part, tile),
        in_specs=[ANY] * (3 + len(given)),
        out_specs=ANY,
        out_shape=bf16(1, 2, span, width),
        scratch_shapes=[
            pltpu.VMEM((3, width, TILE), BF16),
            pltpu.VMEM((TILE, width), BF16),
            pltpu.SemaphoreType.DMA((5,)),
        ],
        input_output_aliases={3: 0} if given else {},
        compiler_params=pltpu.CompilerParams(vmem_limit_bytes=40 * 1024 * 1024),
        cost_estimate=LITTLE,
    )(keep, first, second, *given)


def place_body(core, *refs):
    parts, out, sems = refs[:4], refs[4], refs[5]
    half, span = parts[0].shape
    low = pl.multiple_of(core[0] * half, half)
    high = pl.multiple_of((1 - core[0]) * half, half)
    copies = []
    for i, part in enumerate(parts):
        rows = pl.ds(low if i < 2 else high, half)
        cols = slice(i % 2 * span, (i % 2 + 1) * span)
        copies.append(pltpu.make_async_copy(part, out.at[0, rows, cols], sems.at[i]))
        copies[-1].start()
    for copy in copies:
        copy.wait()


def place(core, mine, theirs):
    half, span = mine[0].shape
    return pl.pallas_call(
        place_body,
        in_specs=[SCALARS] + [WHOLE] * 4,
        out_specs=pl.BlockSpec(memory_space=pl.ANY),
        out_shape=bf16(1, 2 * half, 2 * span),
        scratch_shapes=[pltpu.SemaphoreType.DMA((4,))],
        compiler_params=pltpu.CompilerParams(vmem_limit_bytes=4 * 1024 * 1024),
        cost_estimate=LITTLE,
    )(core[None], *mine, *theirs)


def load_body(*refs):
    count = len(refs) // 2
    sems = refs[-1]
    copies = [
        pltpu.make_async_copy(refs[i], refs[count + i], sems.at[i]) for i in range(count)
    ]
    for copy in copies:
        copy.start()
    for copy in copies:
        copy.wait()


def load(*arrays):
    return pl.pallas_call(
        load_body,
        in_specs=[pl.BlockSpec(memory_space=pl.ANY)] * len(arrays),
        out_specs=[WHOLE] * len(arrays),
        out_shape=[bf16(*array.shape) for array in arrays],
        scratch_shapes=[pltpu.SemaphoreType.DMA((len(arrays),))],
        compiler_params=pltpu.CompilerParams(vmem_limit_bytes=4 * 1024 * 1024),
        cost_estimate=LITTLE,
    )(*arrays)


def encoder_body(low, left, kg, vg, w, *refs):
    moved, outs = refs[:-2], refs[-2:]
    half = outs[0].shape[0]
    rows = slice(low, low + 2 * half)
    for i in range(outs[0].shape[1] // TILE):
        cols = slice(i * TILE, (i + 1) * TILE)
        from_w = slice(left + i * TILE, left + (i + 1) * TILE)
        total = lax.dot_general(kg[rows, :], w[0, 0, from_w, :], NT, preferred_element_type=F32)
        total = total + lax.dot_general(
            vg[rows, :], w[0, 1, from_w, :], NT, preferred_element_type=F32
        )
        for j, out in enumerate(outs):
            part = total[j * half : (j + 1) * half]
            if moved:
                part = part + moved[j][:, cols].astype(F32)
            out[:, cols] = part.astype(BF16)


def encoder_part(key_grad, value_grad, kv_weight, side, columns, moved=(), after=()):
    rows, depth = key_grad.shape[0] // 4, kv_weight.shape[2] // 2
    return call(
        functools.partial(encoder_body, 2 * side * rows, columns * depth),
        [key_grad, value_grad, kv_weight, *moved],
        [bf16(rows, depth)] * 2,
        after=after,
        room=12,
    )


def add_body(held, came, stay, out):
    half = stay.shape[0]
    for i in range(held.shape[1] // TILE):
        cols = slice(i * TILE, (i + 1) * TILE)
        total = held[:, cols].astype(F32) + came[:, cols].astype(F32)
        stay[:, cols] = total[:half]
        out[:, cols] = total[half:].astype(BF16)


def add(held, came, after=()):
    rows, span = held.shape
    shapes = [jax.ShapeDtypeStruct((rows // 2, span), F32), bf16(rows // 2, span)]
    return call(add_body, [held, came], shapes, after=after, room=6)


def tie(array, *others):
    return lax.optimization_barrier((array, *others))[0]


def on_device(encoded, kv_weight, queries, cotangent):
    core = lax.axis_index("tensor") % 2
    y = lax.axis_index("dp")
    block = encoded[0]
    half = block.shape[0] // 2

    one, other = y ^ 1, 3 - y
    first = jnp.where(core == 0, one, other)
    second = jnp.where(core == 0, other, one)

    def starts(*places):
        index = jnp.stack([2 * TILE * place + low for place in places for low in (0, TILE)])
        return index.astype(jnp.int32)

    own = lax.dynamic_slice_in_dim(block, core * half, half, 0)
    too = lax.dynamic_slice_in_dim(block, (1 - core) * half, half, 0)
    own, too, go, stay = lax.optimization_barrier(
        (own, too, starts(first, (y + 2) % 4), starts(second, y))
    )
    h, h_too = {"o": own}, {"o": too}
    g, g_too = {}, {}
    h["a"] = send(h["o"], X_FIRST)
    h["b"] = send(h["o"], X_SECOND)
    g["o"] = send(h["o"], ALONG_Z)
    kv_weight, queries, cotangent = load(kv_weight, queries, cotangent)
    g["a"] = send(tie(h["a"], kv_weight, queries), ALONG_Z)
    h["d"] = send(h["a"], X_SECOND)
    g["d"] = send(g["a"], X_SECOND)
    h_too["a"] = send(h["a"], SWAP)
    h_too["b"] = send(h["b"], SWAP)
    g_too["o"] = send(g["o"], SWAP)
    h_too["d"] = send(h["d"], SWAP)
    g_too["a"] = send(g["a"], SWAP)
    done = [project((h["o"], h_too["o"], h["a"], h_too["a"]), kv_weight)]
    g["b"] = send(tie(h["b"], g["a"], done[0][0]), ALONG_Z)
    done.append(project((g["o"], g_too["o"], h["b"], h_too["b"]), kv_weight))
    done.append(project((g["a"], g_too["a"], h["d"], h_too["d"]), kv_weight))
    g_too["b"] = send(tie(g["b"], done[1][0]), SWAP)
    g_too["d"] = send(tie(g["d"], done[2][0]), SWAP)
    done.append(project((g["b"], g_too["b"], g["d"], g_too["d"]), kv_weight))
    keys, values = zip(*done)
    order = ["ho", "go", "hb", "gb", "ha", "ga", "hd", "gd"]
    pieces = [{"h": h, "g": g}[name[0]][name[1]] for name in order]
    pieces += [{"h": h_too, "g": g_too}[name[0]][name[1]] for name in order]

    inputs = (queries, cotangent, keys, values)
    attended, probs, value_grad, value_grad_t = forward(*inputs)
    value_out = weight_part(go, value_grad_t, pieces)
    query_grad, key_grad, key_grad_t = backward(*inputs, attended, probs, (value_out,))

    grads = (key_grad, value_grad, kv_weight)
    moved = [[send(part, SWAP) for part in encoder_part(*grads, 1, i)] for i in range(2)]
    kept, x_out = zip(*[encoder_part(*grads, 0, i, moved[i]) for i in range(2)])
    key_out = weight_part(go, key_grad_t, pieces, x_out)
    value_keep = weight_part(stay, value_grad_t, pieces, (key_out,))
    key_keep = weight_part(stay, key_grad_t, pieces, (value_keep,))

    def onward(keep, moved):
        span = keep.shape[1] // 2
        return (keep[:, :span].astype(F32) + moved[:, span:].astype(F32)).astype(BF16)

    value_in = send(value_out, Y_FIRST)
    key_in = send(tie(key_out, value_in), Y_FIRST)

    def last_two(part):
        one, two = jnp.split(part, 2, 1)
        one = send(one, Y_SECOND)
        return [one, send(tie(two, one), Y_SECOND)]

    value_two = last_two(tie(onward(value_keep, value_in), key_in))
    key_two = last_two(onward(key_keep, key_in))

    mine, theirs = [], []
    for keep, out in zip(kept, x_out):
        held, going = add(keep, send(out, X_FIRST), (key_keep,))
        if mine:
            held = tie(held, key_in)
        total = held + send(going, X_SECOND).astype(F32)
        here = total[:half] + send(total[half:].astype(BF16), BACK_Z).astype(F32)
        here = here.astype(BF16)
        came = send(here, ACROSS_Z)
        mine.append((here.astype(F32) + came.astype(F32)).astype(BF16))
        theirs.append(send(mine[-1], SWAP))
    enc_grad = place(core, mine, theirs)

    weight_grad = None
    terms = ((1, value_keep, value_in, value_two), (0, key_keep, key_in, key_two))
    for part, keep, one, two in terms:
        for tile in range(2):
            weight_grad = share(part, tile, keep, one, two[tile], weight_grad)
    return (attended, query_grad, enc_grad, weight_grad)


def solution(mesh):
    return jax.shard_map(
        on_device,
        mesh=mesh,
        in_specs=(
            P("dp", "pipe", None),
            P("pipe", None, None, "tensor"),
            P("dp", "pipe", None, "tensor"),
            P("dp", "pipe", None, "tensor"),
        ),
        out_specs=(
            P("dp", "pipe", None, "tensor"),
            P("dp", "pipe", None, "tensor"),
            P("dp", "pipe", None),
            P("pipe", None, "dp", "tensor"),
        ),
        check_vma=False,
    )
```
